128 devices in a mesh: branch: 2 (over y_lo), dp: 64 (over x, z, y_hi, core).
Axes of the slice: x: 4, y: 4 (y_hi: 2, y_lo: 2; y = y_hi * 2 + y_lo), z: 4, core: 2. Of those that a mesh axis runs over, the one named last changes fastest.
Arguments:
- frames: float32 [3, 128, 256, 512], P(None, 'dp'), may hold values from -16 to 16
- attend_norm: float32 [2, 512], replicated, may hold values from -0.5 to 1.25
- attend_in: bfloat16 [512, 3, 512], P('dp', None, 'branch'), may hold values from -0.25 to 0.25
- attend_out: bfloat16 [512, 512], P('dp', 'branch'), may hold values from -1.5 to 1.5
- position_slope: float32 [8], P('branch'), may hold values from 0.004 to 0.1
- mixer_norm: float32 [2, 512], replicated, may hold values from -0.5 to 1.25
- mixer_in: bfloat16 [512, 2, 1536], P('dp', None, 'branch'), may hold values from -0.25 to 0.25
- gating_norm: float32 [2, 1536], P(None, 'branch'), may hold values from -0.5 to 1.25
- kernel_taps: float32 [31, 1536], P(None, 'branch'), may hold values from -1 to 1
- kernel_bias: float32 [1536], P('branch'), may hold values from -4 to 4
- mixer_out: bfloat16 [512, 1536], P('dp', 'branch'), may hold values from -0.3125 to 0.3125
- merge_logits: float32 [2], replicated, may hold values from -1 to 1
- final_norm: float32 [2, 512], replicated, may hold values from -0.5 to 1.25
- lengths: int32 [3, 128], P(None, 'dp'), may hold values from 64 to 256, as said below
- cotangent: float32 [3, 128, 256, 512], P(None, 'dp'), may hold values from -16 to 16
Outputs:
- layer_out: float32 [3, 128, 256, 512], P(None, 'dp')
- frames_grad: float32 [3, 128, 256, 512], P(None, 'dp')
- attend_norm_grad: float32 [2, 512], replicated
- attend_in_grad: float32 [512, 3, 512], P('dp', None, 'branch')
- attend_out_grad: float32 [512, 512], P('dp', 'branch')
- position_slope_grad: float32 [8], P('branch')
- mixer_norm_grad: float32 [2, 512], replicated
- mixer_in_grad: float32 [512, 2, 1536], P('dp', None, 'branch')
- gating_norm_grad: float32 [2, 1536], P(None, 'branch')
- kernel_taps_grad: float32 [31, 1536], P(None, 'branch')
- kernel_bias_grad: float32 [1536], P('branch')
- mixer_out_grad: float32 [512, 1536], P('dp', 'branch')
- merge_logits_grad: float32 [2], replicated
- final_norm_grad: float32 [2, 512], replicated
The draws below stay inside these ranges and needn't reach their ends.
Inputs may be any that keep to these rules, and one draw needn't show every extreme that they name: `lengths`: in every micro-batch one utterance fills the slot and one has a quarter of 256 frames.
All inputs are finite; a program needn't handle non-finite values.
Results may differ from the reference program's by a relative error of at most 0.0095.
Values may be sent and summed in bfloat16 or wider, within the bound.
No kernel may reach another device: no remote copies, remote signals or barrier semaphores. Data moves between devices by JAX's collectives and lax.ppermute only.
A program may use at most 448 MiB of HBM per device.

```python
import math
import jax
import jax.numpy as jnp
from jax import lax

D = 512
H = 8
FF = 3072
KERNEL = 31
DH = 64
LEN = 256
MICRO = 3
HALF = 1536
SEQS = 128


def norm_pair(key, width_in):
    gain_key, bias_key = jax.random.split(key)
    gains = 1.0 + 0.25 * jax.random.uniform(gain_key, (width_in,), jnp.float32, -1.0, 1.0)
    biases = 0.5 * jax.random.uniform(bias_key, (width_in,), jnp.float32, -1.0, 1.0)
    return jnp.stack([gains, biases])


def draw_attend_norm(key, part):
    key = jax.random.fold_in(key, 11)
    return norm_pair(key, D)


def draw_mixer_norm(key, part):
    key = jax.random.fold_in(key, 12)
    return norm_pair(key, D)


def draw_gating_norm(key, part):
    key = jax.random.fold_in(key, 13)
    return norm_pair(key, FF // 2)


def draw_final_norm(key, part):
    key = jax.random.fold_in(key, 14)
    return norm_pair(key, D)


def draw_lengths(key, part):
    key = jax.random.fold_in(key, 31)
    base_key, order_key = jax.random.split(key)
    drawn = jax.random.randint(base_key, (MICRO, SEQS), LEN // 4, LEN + 1)
    ranking = jax.random.randint(order_key, (MICRO, SEQS), 0, 1 << 20) * SEQS + jnp.arange(SEQS)[None, :]
    ranks = jnp.argsort(jnp.argsort(ranking, axis=1), axis=1)
    drawn = jnp.where(ranks == 0, LEN, drawn)
    drawn = jnp.where(ranks == 1, LEN // 4, drawn)
    return drawn.astype(jnp.int32)


def strengthened(array, key, source, target, parts, factor):
    def block_of(position):
        return (jnp.arange(array.shape[position]) // (array.shape[position] // parts)).reshape((-1,) + (1,) * (array.ndim - 1 - position))

    first = jax.random.permutation(key, parts)[block_of(target)]
    second = (block_of(target) + parts // 2) % parts
    return jnp.where((block_of(source) == first) | (block_of(source) == second), factor * array, array)


def block_scale(own_key, extent, cuts, smallest, largest):
    def one(dim, parts):
        draws = jax.random.uniform(jax.random.fold_in(jax.random.fold_in(own_key, 6), dim), (parts,), jnp.float32, smallest / len(cuts), largest / len(cuts))
        return jnp.repeat(jnp.exp(draws), extent[dim] // parts).reshape((-1,) + (1,) * (len(extent) - dim - 1))

    level = one(*cuts[0])
    for cut in cuts[1:]:
        level = level * one(*cut)
    return level


def noise(rng, extent, scale, most, shards=(), kind=jnp.bfloat16):
    values = scale * jax.random.normal(rng, extent, jnp.float32)
    if shards:
        values = values * block_scale(rng, extent, shards, -0.22, 0.18)
    return jnp.clip(values, -most, most).astype(kind)


def bell_draw_with(stream_key, dims, deviation, limit, shards, heavy, kind=jnp.bfloat16):
    values = deviation * jax.random.normal(stream_key, dims, jnp.float32)
    if shards:
        values = values * block_scale(stream_key, dims, shards, -0.22, 0.18)
    return jnp.clip(strengthened(values, jax.random.fold_in(stream_key, 3), *heavy), -limit, limit).astype(kind)


def setup_inputs(seed: int = 0) -> dict:
    seeds = jax.random.split(jax.random.key(seed), 16)
    frames = bell_draw_with(seeds[0], (MICRO, SEQS, LEN, D), 1.0, 16.0, ((1, 64),), (1, 3, 64, 4.0), jnp.float32)
    attend_norm = draw_attend_norm(jax.random.fold_in(seeds[15], 71), 0)
    attend_in = noise(seeds[2], (D, 3, H * DH), D ** -0.5, 0.25, ((0, 64), (2, 2)))
    attend_out = noise(seeds[3], (D, H * DH), (H * DH // 32) ** -0.5, 1.5, ((0, 64), (1, 2)))
    position_slope = jnp.clip(jnp.exp(math.log(0.1) - 3.218876 * jax.random.uniform(seeds[4], (H,), jnp.float32) ** block_scale(seeds[4], (H,), ((0, 2),), -0.2, 0.2)), 0.004, 0.1)
    mixer_norm = draw_mixer_norm(jax.random.fold_in(seeds[15], 71), 0)
    mixer_in = noise(seeds[6], (D, 2, HALF), D ** -0.5, 0.25, ((0, 64), (2, 2)))
    gating_norm = draw_gating_norm(jax.random.fold_in(seeds[15], 71), 0)
    kernel_taps = noise(seeds[8], (KERNEL, HALF), KERNEL ** -0.5, 1.0, ((1, 2),), jnp.float32)
    kernel_bias = noise(seeds[9], (HALF,), 0.3, 4.0, ((0, 2),), jnp.float32)
    mixer_out = noise(seeds[10], (D, HALF), (HALF // 4) ** -0.5, 0.3125, ((0, 64), (1, 2)))
    merge_logits = jnp.clip(jax.random.uniform(seeds[11], (2,), jnp.float32, -1.0, 1.0), -1.0, 1.0)
    final_norm = draw_final_norm(jax.random.fold_in(seeds[15], 71), 0)
    lengths = draw_lengths(jax.random.fold_in(seeds[15], 71), 0)
    cotangent = bell_draw_with(seeds[14], (MICRO, SEQS, LEN, D), 1.0, 16.0, ((1, 64),), (1, 3, 64, 4.0), jnp.float32)
    return {"frames": frames, "attend_norm": attend_norm, "attend_in": attend_in, "attend_out": attend_out, "position_slope": position_slope, "mixer_norm": mixer_norm, "mixer_in": mixer_in, "gating_norm": gating_norm, "kernel_taps": kernel_taps, "kernel_bias": kernel_bias, "mixer_out": mixer_out, "merge_logits": merge_logits, "final_norm": final_norm, "lengths": lengths, "cotangent": cotangent}


@jax.custom_vjp
def low(v):
    return lax.optimization_barrier(v.astype(jnp.bfloat16)).astype(jnp.float32)

@jax.custom_vjp
def low_back(v):
    return v

def low_keep(v):
    return (low(v), None)

def low_pass(kept, grad):
    return (grad,)

def back_keep(v):
    return (v, None)

def back_low(kept, grad):
    return (low(grad),)
low.defvjp(low_keep, low_pass)
low_back.defvjp(back_keep, back_low)
EPSILON = 1e-05
NEGATIVE = -1e+30
HIGHEST = lax.Precision.HIGHEST

def norm_rows(rows_in, params):
    average = lax.optimization_barrier(jnp.mean(rows_in, axis=-1, keepdims=True))
    centered = rows_in - average
    variance = lax.optimization_barrier(jnp.mean(centered * centered, axis=-1, keepdims=True))
    return centered * lax.rsqrt(variance + EPSILON) * params[0] + params[1]

def depthwise(field_in, kernel_taps):
    tap_count = kernel_taps.shape[0]
    reach_len = (tap_count - 1) // 2
    slot_len = field_in.shape[1]
    padded = jnp.pad(field_in, ((0, 0), (reach_len, reach_len), (0, 0)))
    result = kernel_taps[0] * padded[:, 0:slot_len]
    for tap in range(1, tap_count):
        result = result + kernel_taps[tap] * padded[:, tap:tap + slot_len]
    return result

def group_forward(params, frames_group, lengths_group):
    attend_norm, attend_in, attend_out, position_slope, mixer_norm, mixer_in, gating_norm, kernel_taps, kernel_bias, mixer_out, merge_logits, final_norm = params
    groups = frames_group.shape[0]
    positions = jnp.arange(LEN, dtype=jnp.int32)
    valid_mask = (positions[None, :] < lengths_group[:, None]).astype(jnp.float32)[:, :, None]
    offsets = (positions[None, :] - positions[:, None]).astype(jnp.float32)
    distance = jnp.sqrt(offsets * offsets + 1.0)
    attend_low = low(norm_rows(frames_group, attend_norm))
    triple = low(low_back(jnp.einsum('gtd,dkc->gtkc', attend_low, attend_in, precision=HIGHEST)))
    queries = triple[:, :, 0].reshape(groups, LEN, H, DH)
    key_heads = triple[:, :, 1].reshape(groups, LEN, H, DH)
    value_heads = triple[:, :, 2].reshape(groups, LEN, H, DH)
    scores = low_back(jnp.einsum('gihe,gjhe->ghij', queries, key_heads, precision=HIGHEST) * DH ** (-0.5))
    logits = scores - position_slope[None, :, None, None] * distance[None, None]
    key_mask = valid_mask[:, None, None, :, 0] > 0.5
    logits = jnp.where(key_mask, logits, NEGATIVE)
    highest = lax.optimization_barrier(jnp.max(logits, axis=-1, keepdims=True))
    exponent = jnp.exp(logits - highest)
    prob_full = exponent / lax.optimization_barrier(jnp.sum(exponent, axis=-1, keepdims=True))
    context = low(low_back(jnp.einsum('ghij,gjhe->gihe', low(prob_full), value_heads, precision=HIGHEST)))
    context = context.reshape(groups, LEN, H * DH)
    attend_branch = low_back(jnp.einsum('gtc,dc->gtd', context, attend_out, precision=HIGHEST))
    mixer_low = low(norm_rows(frames_group, mixer_norm))
    hidden = low_back(jnp.einsum('gtd,dkc->gtkc', mixer_low, mixer_in, precision=HIGHEST))
    active = jax.nn.gelu(hidden)
    gate_in = norm_rows(active[:, :, 1], gating_norm) * valid_mask
    conved = depthwise(gate_in, kernel_taps) + kernel_bias
    gated_out = low(active[:, :, 0] * conved)
    mixer_branch = low_back(jnp.einsum('gtc,dc->gtd', gated_out, mixer_out, precision=HIGHEST))
    merge_top = jnp.max(merge_logits)
    merge_exp = jnp.exp(merge_logits - merge_top)
    mixing = merge_exp / jnp.sum(merge_exp)
    merged = frames_group + mixing[0] * attend_branch + mixing[1] * mixer_branch
    return norm_rows(merged, final_norm) * valid_mask

def reference(frames, attend_norm, attend_in, attend_out, position_slope, mixer_norm, mixer_in, gating_norm, kernel_taps, kernel_bias, mixer_out, merge_logits, final_norm, lengths, cotangent):
    group_size = math.gcd(SEQS, max(1, 2048 // LEN))
    blocks = MICRO * SEQS // group_size
    lengths_blocks = lengths.reshape(blocks, group_size).astype(jnp.int32)
    block_step = jax.checkpoint(group_forward)

    def forward(frames_in, params):
        frames_blocks = frames_in.reshape(blocks, group_size, LEN, D)

        def apply_block(operands):
            return block_step(params, operands[0], operands[1])
        results = lax.map(apply_block, (frames_blocks, lengths_blocks))
        return results.reshape(MICRO, SEQS, LEN, D)
    params32 = tuple((tensor.astype(jnp.float32) for tensor in (attend_norm, attend_in, attend_out, position_slope, mixer_norm, mixer_in, gating_norm, kernel_taps, kernel_bias, mixer_out, merge_logits, final_norm)))
    layer_out, pullback = jax.vjp(forward, frames.astype(jnp.float32), params32)
    frames_grad, grad_params = pullback(cotangent.astype(jnp.float32))
    grad_anorm, grad_attend_in, grad_attend_out, grad_slope, grad_mnorm, grad_mixer_in, grad_gnorm, grad_taps, grad_kbias, grad_mixer_out, grad_merge, grad_fnorm = grad_params
    return (layer_out, frames_grad, grad_anorm, grad_attend_in, grad_attend_out, grad_slope, grad_mnorm, grad_mixer_in, grad_gnorm, grad_taps, grad_kbias, grad_mixer_out, grad_merge, grad_fnorm)
```

```python
from functools import partial

import jax
import jax.numpy as jnp
import numpy as np
from jax import lax
from jax.experimental import pallas as pl
from jax.experimental.pallas import tpu as pltpu
from jax.sharding import PartitionSpec as P

EPSILON = 1e-05
NEGATIVE = -1e30
F32 = jnp.float32
BF16 = jnp.bfloat16
SLOT = 256
WIDTH = 512
HEADS = 8
HEAD = 64
HALF = 1536
TAPS = 31
REACH = 15
UTTS = 3
ROWS = UTTS * SLOT
PERIOD = SLOT + REACH
BINS = (PERIOD + 1) // 2
SPEC = 2 * BINS
BLOCK = 256
BLOCKS = HALF // BLOCK
PER_BRANCH = 768 // BLOCK
GELU_A = 0.7978845608028654
GELU_B = GELU_A * 0.044715
VMEM_LIMIT = 60 * 1024 * 1024


def transform_tables():
    bins = np.arange(BINS)[:, None]
    angle = 2 * np.pi * bins * np.arange(SLOT)[None, :] / PERIOD
    lag_angle = 2 * np.pi * bins * (np.arange(TAPS) - REACH)[None, :] / PERIOD
    weight = np.where(bins == 0, 1.0, 2.0) / PERIOD
    forward = np.concatenate([np.cos(angle), -np.sin(angle)], 0)
    inverse = np.concatenate([np.cos(angle) * weight, -np.sin(angle) * weight], 0).T
    tap_forward = np.concatenate([np.cos(lag_angle), -np.sin(lag_angle)], 0)
    tap_inverse = np.concatenate([np.cos(lag_angle) * weight, -np.sin(lag_angle) * weight], 0).T
    tap_forward = np.pad(tap_forward, ((0, 0), (0, 1)))
    tap_inverse = np.pad(tap_inverse, ((0, 1), (0, 0)))
    return forward, inverse, tap_forward, tap_inverse


def dot_nn(a, b):
    return lax.dot_general(a, b, (((1,), (0,)), ((), ())), preferred_element_type=F32)


def dot_nt(a, b):
    return lax.dot_general(a, b, (((1,), (1,)), ((), ())), preferred_element_type=F32)


def dot_tn(a, b):
    return lax.dot_general(a, b, (((0,), (0,)), ((), ())), preferred_element_type=F32)


def standardize(rows_in):
    average = jnp.mean(rows_in, axis=-1, keepdims=True)
    centered = rows_in - average
    variance = jnp.mean(centered * centered, axis=-1, keepdims=True)
    rstd = lax.rsqrt(variance + EPSILON)
    return centered * rstd, rstd


def gelu_pair(v):
    square = v * v
    half = 0.5 + 0.5 * jnp.tanh(v * (GELU_A + GELU_B * square))
    active = v * half
    slope = half + active * (1.0 - half) * (2 * GELU_A + 6 * GELU_B * square)
    return active, slope


def fill_distance(distance):
    key_at = lax.broadcasted_iota(jnp.int32, (SLOT, SLOT), 0)
    query_at = lax.broadcasted_iota(jnp.int32, (SLOT, SLOT), 1)
    offset = (key_at - query_at).astype(F32)
    distance[...] = jnp.sqrt(offset * offset + 1.0)


def attend_forward(info, slopes, frames, norm, weights, triple, context, log_total, distance):
    step = pl.program_id(0)

    @pl.when(step == 0)
    def _():
        fill_distance(distance)

    normed, _ = standardize(frames[0, 0])
    low = (normed * norm[0:1] + norm[1:2]).astype(BF16)
    for b in range(2):
        part = dot_nn(low, weights[b, :, 0:768])
        part = jnp.concatenate([part[:, 0:256] * (HEAD**-0.5), part[:, 256:768]], axis=1)
        triple[0, b * 768 : (b + 1) * 768, :] = part.astype(BF16).T
    length = info[1 + step]
    is_key = lax.broadcasted_iota(jnp.int32, (SLOT, SLOT), 0) < length

    def head(h, carry):
        base = pl.multiple_of((h // 4) * 768 + (h % 4) * HEAD, HEAD)
        q = triple[0, pl.ds(base, HEAD), :]
        k = triple[0, pl.ds(base + 256, HEAD), :]
        v = triple[0, pl.ds(base + 512, HEAD), :]
        logits = dot_tn(k, q) - slopes[h] * distance[...]
        logits = jnp.where(is_key, logits, NEGATIVE)
        highest = jnp.max(logits, axis=0, keepdims=True)
        exponent = jnp.exp(logits - highest)
        total = jnp.sum(exponent, axis=0, keepdims=True)
        prob = (exponent * (1.0 / total)).astype(BF16)
        context[0, pl.ds(pl.multiple_of(h * HEAD, HEAD), HEAD), :] = dot_nn(v, prob).astype(BF16)
        log_total[0, pl.ds(h, 1), :] = highest + jnp.log(total)
        return carry

    lax.fori_loop(0, HEADS, head, 0)


def mixer_both(
    info,
    mixing,
    frames,
    cotangent,
    context,
    mixer_norm,
    final_norm,
    gating_norm,
    taps,
    kernel_bias,
    weights,
    out_weights,
    forward,
    inverse,
    tap_forward,
    tap_inverse,
    layer,
    grad_merged_out,
    grad_mixer_out,
    weight_grads,
    small_wide,
    small_narrow,
    tap_spec,
    second_s,
    second_slope,
    first_s,
    first_slope,
    conv_s,
    spec_s,
    cross_s,
    back_s,
    sums,
    part_s,
    gated_s,
    hidden_s,
    low_t,
    grad_t,
):
    step = pl.program_id(0)
    here = pl.ds(pl.multiple_of(step * SLOT, SLOT), SLOT)

    @pl.when(step == 0)
    def _():
        for k in range(BLOCKS):
            tap_spec[k] = jnp.dot(
                tap_forward[...],
                taps[:, k * BLOCK : (k + 1) * BLOCK],
                precision=lax.Precision.HIGHEST,
                preferred_element_type=F32,
            )
        cross_s[...] = jnp.zeros_like(cross_s)
        small_wide[...] = jnp.zeros_like(small_wide)
        small_narrow[...] = jnp.zeros_like(small_narrow)

    rows_in = frames[0, 0]
    normed, rstd = standardize(rows_in)
    low = (normed * mixer_norm[0:1] + mixer_norm[1:2]).astype(BF16)
    low_t[:, here] = low.T
    length = info[1 + step]
    valid = (lax.broadcasted_iota(jnp.int32, (SLOT, 1), 0) < length).astype(F32)

    def place(k):
        b = k // PER_BRANCH
        return b, (k - b * PER_BRANCH) * BLOCK

    def lanes(offset):
        return pl.ds(pl.multiple_of(offset, BLOCK), BLOCK)

    def fold(v):
        return v[:, 0:128] + v[:, 128:256]

    sums[...] = jnp.zeros_like(sums)

    def second_step(k, carry):
        b, off = place(k)
        active, slope = gelu_pair(dot_nn(low, weights[b, :, lanes(768 + off)]))
        second_s[k] = active
        second_slope[k] = slope
        sums[0] += fold(active)
        return carry

    lax.fori_loop(0, BLOCKS, second_step, 0)
    average = jnp.sum(sums[0], axis=-1, keepdims=True) / HALF

    def variance_step(k, carry):
        centered = second_s[k] - average
        second_s[k] = centered
        sums[1] += fold(centered * centered)
        return carry

    lax.fori_loop(0, BLOCKS, variance_step, 0)
    gate_rstd = lax.rsqrt(jnp.sum(sums[1], axis=-1, keepdims=True) / HALF + EPSILON)

    part_s[...] = jnp.zeros_like(part_s)

    def conv_step(k, carry):
        b, off = place(k)
        wide = lanes(k * BLOCK)
        standard = second_s[k] * gate_rstd
        second_s[k] = standard
        gate_in = (standard * gating_norm[0:1, wide] + gating_norm[1:2, wide]) * valid
        spec = dot_nn(forward[...], gate_in.astype(BF16))
        spec_s[k] = spec
        real, imag = spec[0:BINS], spec[BINS:SPEC]
        tap_real, tap_imag = tap_spec[k, 0:BINS], tap_spec[k, BINS:SPEC]
        product = jnp.concatenate(
            [real * tap_real + imag * tap_imag, imag * tap_real - real * tap_imag], axis=0
        )
        conved = dot_nn(inverse[...], product.astype(BF16)) + kernel_bias[0:1, wide]
        conv_s[k] = conved
        active, slope = gelu_pair(dot_nn(low, weights[b, :, lanes(off)]))
        first_s[k] = active
        first_slope[k] = slope
        gated = (active * conved).astype(BF16)
        gated_s[k, here, :] = gated
        part_s[...] += dot_nt(gated, weights[b, :, lanes(1536 + off)])
        return carry

    lax.fori_loop(0, BLOCKS, conv_step, 0)

    mixer_part = part_s[...]
    attend_part = dot_tn(context[0, 0:256, :], out_weights[0].T) + dot_tn(
        context[0, 256:512, :], out_weights[1].T
    )
    merged = rows_in + mixing[0] * attend_part + mixing[1] * mixer_part
    merged_normed, merged_rstd = standardize(merged)
    layer[0] = ((merged_normed * final_norm[0:1] + final_norm[1:2]) * valid).astype(BF16)
    grad_out = cotangent[0, 0] * valid
    scaled = grad_out * final_norm[0:1]
    grad_merged = merged_rstd * (
        scaled
        - jnp.mean(scaled, axis=-1, keepdims=True)
        - merged_normed * jnp.mean(scaled * merged_normed, axis=-1, keepdims=True)
    )
    grad_merged_out[0] = grad_merged
    small_narrow[0:1] += jnp.sum(grad_out * merged_normed, axis=0, keepdims=True)
    small_narrow[1:2] += jnp.sum(grad_out, axis=0, keepdims=True)
    small_narrow[2:3] += jnp.sum(grad_merged * attend_part, axis=0, keepdims=True)
    small_narrow[3:4] += jnp.sum(grad_merged * mixer_part, axis=0, keepdims=True)
    grad_mixer = (mixing[1] * grad_merged).astype(BF16)
    grad_t[:, here] = grad_mixer.T
    sums[...] = jnp.zeros_like(sums)

    def back_step(k, carry):
        b, off = place(k)
        wide = lanes(k * BLOCK)
        grad_gated = dot_nn(grad_mixer, weights[b, :, lanes(1536 + off)])
        grad_conved = grad_gated * first_s[k]
        hidden_s[k, here, :] = (first_slope[k] * (grad_gated * conv_s[k])).astype(BF16)
        small_wide[31:32, wide] += jnp.sum(grad_conved, axis=0, keepdims=True)
        grad_spec = dot_nn(forward[...], grad_conved.astype(BF16))
        grad_real, grad_imag = grad_spec[0:BINS], grad_spec[BINS:SPEC]
        real, imag = spec_s[k, 0:BINS], spec_s[k, BINS:SPEC]
        cross_s[k, 0:BINS] += grad_real * real + grad_imag * imag
        cross_s[k, BINS:SPEC] += grad_real * imag - grad_imag * real
        tap_real, tap_imag = tap_spec[k, 0:BINS], tap_spec[k, BINS:SPEC]
        product = jnp.concatenate(
            [
                grad_real * tap_real - grad_imag * tap_imag,
                grad_real * tap_imag + grad_imag * tap_real,
            ],
            axis=0,
        )
        grad_gate = dot_nn(inverse[...], product.astype(BF16)) * valid
        standard = second_s[k]
        small_wide[32:33, wide] += jnp.sum(grad_gate * standard, axis=0, keepdims=True)
        small_wide[33:34, wide] += jnp.sum(grad_gate, axis=0, keepdims=True)
        grad_standard = grad_gate * gating_norm[0:1, wide]
        back_s[k] = grad_standard
        sums[0] += fold(grad_standard)
        sums[1] += fold(grad_standard * standard)
        return carry

    lax.fori_loop(0, BLOCKS, back_step, 0)
    back_average = jnp.sum(sums[0], axis=-1, keepdims=True) / HALF
    back_scale = jnp.sum(sums[1], axis=-1, keepdims=True) / HALF
    part_s[...] = jnp.zeros_like(part_s)

    def hidden_step(k, carry):
        b, off = place(k)
        grad_second = gate_rstd * (back_s[k] - back_average - second_s[k] * back_scale)
        grad_hidden = (second_slope[k] * grad_second).astype(BF16)
        hidden_s[BLOCKS + k, here, :] = grad_hidden
        part_s[...] += dot_nt(hidden_s[k, here, :], weights[b, :, lanes(off)]) + dot_nt(
            grad_hidden, weights[b, :, lanes(768 + off)]
        )
        return carry

    lax.fori_loop(0, BLOCKS, hidden_step, 0)
    grad_low = part_s[...]
    small_narrow[4:5] += jnp.sum(grad_low * normed, axis=0, keepdims=True)
    small_narrow[5:6] += jnp.sum(grad_low, axis=0, keepdims=True)
    grad_mixer_out[0] = grad_low * mixer_norm[0:1]

    @pl.when(step == UTTS - 1)
    def _():
        def weight_step(k, carry):
            b, off = place(k)
            weight_grads[b, :, lanes(off)] = dot_nn(low_t[...], hidden_s[k]).astype(BF16)
            weight_grads[b, :, lanes(768 + off)] = dot_nn(low_t[...], hidden_s[BLOCKS + k]).astype(
                BF16
            )
            weight_grads[b, :, lanes(1536 + off)] = dot_nn(grad_t[...], gated_s[k]).astype(BF16)
            tap_grad = jnp.dot(
                tap_inverse[...],
                cross_s[k],
                precision=lax.Precision.HIGHEST,
                preferred_element_type=F32,
            )
            small_wide[0:31, lanes(k * BLOCK)] = tap_grad[0:31]
            return carry

        lax.fori_loop(0, BLOCKS, weight_step, 0)


def attend_backward(
    info,
    slopes,
    mixing,
    frames,
    grad_merged,
    grad_mixer,
    triple,
    context,
    log_total,
    norm,
    weights,
    frames_grad,
    weight_grads,
    small_narrow,
    slope_grads,
    distance,
    low_t,
    grad_t,
    context_t,
    triple_t,
    grad_context,
):
    step = pl.program_id(0)
    here = pl.ds(pl.multiple_of(step * SLOT, SLOT), SLOT)

    @pl.when(step == 0)
    def _():
        fill_distance(distance)
        small_narrow[...] = jnp.zeros_like(small_narrow)
        slope_grads[...] = jnp.zeros_like(slope_grads)

    normed, rstd = standardize(frames[0, 0])
    low = (normed * norm[0:1] + norm[1:2]).astype(BF16)
    low_t[:, here] = low.T
    grad_attend = (mixing[0] * grad_merged[0]).astype(BF16)
    grad_t[:, here] = grad_attend.T
    context_t[:, here] = context[0]
    for b in range(2):
        grad_context[b * 256 : (b + 1) * 256, :] = (
            dot_nn(grad_attend, weights[b, :, 768:1024]).astype(BF16).T
        )
    length = info[1 + step]
    is_key = lax.broadcasted_iota(jnp.int32, (SLOT, SLOT), 0) < length

    def head(h, carry):
        base = pl.multiple_of((h // 4) * 768 + (h % 4) * HEAD, HEAD)
        at = pl.multiple_of(h * HEAD, HEAD)
        q = triple[0, pl.ds(base, HEAD), :]
        k = triple[0, pl.ds(base + 256, HEAD), :]
        v = triple[0, pl.ds(base + 512, HEAD), :]
        grad_here = grad_context[pl.ds(at, HEAD), :]
        logits = dot_tn(k, q) - slopes[h] * distance[...]
        logits = jnp.where(is_key, logits, NEGATIVE)
        prob = jnp.exp(logits - log_total[0, pl.ds(h, 1), :])
        grad_prob = dot_tn(v, grad_here)
        row_dot = jnp.sum(prob * grad_prob, axis=0, keepdims=True)
        grad_logits = prob * (grad_prob - row_dot)
        slope_grads[pl.ds(h, 1), :] -= jnp.sum(grad_logits * distance[...], axis=0, keepdims=True)
        grad_scores = grad_logits.astype(BF16)
        grad_q = dot_nn(k, grad_scores) * (HEAD**-0.5)
        grad_k = dot_nt(q, grad_scores)
        grad_v = dot_nt(grad_here, prob.astype(BF16))
        triple_t[pl.ds(base, HEAD), here] = grad_q.astype(BF16)
        triple_t[pl.ds(base + 256, HEAD), here] = grad_k.astype(BF16)
        triple_t[pl.ds(base + 512, HEAD), here] = grad_v.astype(BF16)
        return carry

    lax.fori_loop(0, HEADS, head, 0)
    grad_low = dot_nt(triple_t[0:768, here].T, weights[0, :, 0:768]) + dot_nt(
        triple_t[768:1536, here].T, weights[1, :, 0:768]
    )
    small_narrow[0:1] += jnp.sum(grad_low * normed, axis=0, keepdims=True)
    small_narrow[1:2] += jnp.sum(grad_low, axis=0, keepdims=True)
    scaled = grad_low * norm[0:1] + grad_mixer[0]
    frames_grad[0] = (
        grad_merged[0]
        + rstd
        * (
            scaled
            - jnp.mean(scaled, axis=-1, keepdims=True)
            - normed * jnp.mean(scaled * normed, axis=-1, keepdims=True)
        )
    ).astype(BF16)

    @pl.when(step == UTTS - 1)
    def _():
        for b in range(2):
            weight_grads[b, :, 0:768] = dot_nt(
                low_t[...], triple_t[b * 768 : (b + 1) * 768, :]
            ).astype(BF16)
            weight_grads[b, :, 768:1024] = dot_nt(
                grad_t[...], context_t[b * 256 : (b + 1) * 256, :]
            ).astype(BF16)


def whole(shape):
    return pl.BlockSpec(shape, lambda i, *_: (0,) * len(shape), pipeline_mode=pl.Buffered(1))


def kept(shape):
    return pl.BlockSpec(shape, lambda i, *_: (0,) * len(shape))


def per_utt(shape):
    return pl.BlockSpec((1,) + shape, lambda i, *_: (i,) + (0,) * len(shape))


OWN_FRAMES = pl.BlockSpec((1, 1, SLOT, WIDTH), lambda i, info, *_: (i, info[0], 0, 0))


def scratch(*shape, dtype=F32):
    return pltpu.VMEM(shape, dtype)


def struct(*shape, dtype=F32):
    return jax.ShapeDtypeStruct(shape, dtype)


def params():
    return pltpu.CompilerParams(
        dimension_semantics=("arbitrary",), vmem_limit_bytes=VMEM_LIMIT
    )


def run_attend_forward(info, slopes, frames, norm, weights):
    return pl.pallas_call(
        attend_forward,
        grid_spec=pltpu.PrefetchScalarGridSpec(
            num_scalar_prefetch=2,
            grid=(UTTS,),
            in_specs=[OWN_FRAMES, whole((2, WIDTH)), whole((2, WIDTH, 1024))],
            out_specs=[
                per_utt((HALF, SLOT)),
                per_utt((WIDTH, SLOT)),
                per_utt((HEADS, SLOT)),
            ],
            scratch_shapes=[scratch(SLOT, SLOT)],
        ),
        out_shape=[
            struct(UTTS, HALF, SLOT, dtype=BF16),
            struct(UTTS, WIDTH, SLOT, dtype=BF16),
            struct(UTTS, HEADS, SLOT),
        ],
        compiler_params=params(),
        cost_estimate=pl.CostEstimate(
            flops=2 * ROWS * 512 * 1536, bytes_accessed=8 << 20, transcendentals=0
        ),
        name="attend_forward",
    )(info, slopes, frames, norm, weights)


def run_mixer(
    info, mixing, frames, cotangent, context, mnorm, fnorm, gnorm, taps, bias, weights, attend_w
):
    forward, inverse, tap_forward, tap_inverse = transform_tables()
    tables = (
        jnp.asarray(forward, BF16),
        jnp.asarray(inverse, BF16),
        jnp.asarray(tap_forward, F32),
        jnp.asarray(tap_inverse, F32),
    )
    block = (BLOCKS, SLOT, BLOCK)
    return pl.pallas_call(
        mixer_both,
        grid_spec=pltpu.PrefetchScalarGridSpec(
            num_scalar_prefetch=2,
            grid=(UTTS,),
            in_specs=[
                OWN_FRAMES,
                OWN_FRAMES,
                per_utt((WIDTH, SLOT)),
                whole((2, WIDTH)),
                whole((2, WIDTH)),
                whole((2, HALF)),
                whole((32, HALF)),
                whole((1, HALF)),
                whole((2, WIDTH, 2304)),
                pl.BlockSpec(
                    (2, WIDTH, 256), lambda i, *_: (0, 0, 3), pipeline_mode=pl.Buffered(1)
                ),
                whole((SPEC, SLOT)),
                whole((SLOT, SPEC)),
                whole((SPEC, 32)),
                whole((32, SPEC)),
            ],
            out_specs=[
                per_utt((SLOT, WIDTH)),
                per_utt((SLOT, WIDTH)),
                per_utt((SLOT, WIDTH)),
                whole((2, WIDTH, 2304)),
                kept((40, HALF)),
                kept((8, WIDTH)),
            ],
            scratch_shapes=[
                scratch(BLOCKS, SPEC, BLOCK),
                scratch(*block),
                scratch(*block),
                scratch(*block),
                scratch(*block),
                scratch(*block),
                scratch(BLOCKS, SPEC, BLOCK),
                scratch(BLOCKS, SPEC, BLOCK),
                scratch(*block),
                scratch(2, SLOT, 128),
                scratch(SLOT, WIDTH),
                scratch(BLOCKS, ROWS, BLOCK, dtype=BF16),
                scratch(2 * BLOCKS, ROWS, BLOCK, dtype=BF16),
                scratch(WIDTH, ROWS, dtype=BF16),
                scratch(WIDTH, ROWS, dtype=BF16),
            ],
        ),
        out_shape=[
            struct(UTTS, SLOT, WIDTH, dtype=BF16),
            struct(UTTS, SLOT, WIDTH),
            struct(UTTS, SLOT, WIDTH),
            struct(2, WIDTH, 2304, dtype=BF16),
            struct(40, HALF),
            struct(8, WIDTH),
        ],
        compiler_params=params(),
        cost_estimate=pl.CostEstimate(
            flops=6 * ROWS * 512 * 4608, bytes_accessed=20 << 20, transcendentals=0
        ),
        name="mixer_both",
    )(
        info,
        mixing,
        frames,
        cotangent,
        context,
        mnorm,
        fnorm,
        gnorm,
        taps,
        bias,
        weights,
        attend_w,
        *tables,
    )


def run_attend_backward(
    info, slopes, mixing, frames, grad_merged, grad_mixer, triple, context, log_total, norm, weights
):
    return pl.pallas_call(
        attend_backward,
        grid_spec=pltpu.PrefetchScalarGridSpec(
            num_scalar_prefetch=3,
            grid=(UTTS,),
            in_specs=[
                OWN_FRAMES,
                per_utt((SLOT, WIDTH)),
                per_utt((SLOT, WIDTH)),
                per_utt((HALF, SLOT)),
                per_utt((WIDTH, SLOT)),
                per_utt((HEADS, SLOT)),
                whole((2, WIDTH)),
                whole((2, WIDTH, 1024)),
            ],
            out_specs=[
                per_utt((SLOT, WIDTH)),
                whole((2, WIDTH, 1024)),
                kept((8, WIDTH)),
                kept((HEADS, SLOT)),
            ],
            scratch_shapes=[
                scratch(SLOT, SLOT),
                scratch(WIDTH, ROWS, dtype=BF16),
                scratch(WIDTH, ROWS, dtype=BF16),
                scratch(WIDTH, ROWS, dtype=BF16),
                scratch(HALF, ROWS, dtype=BF16),
                scratch(WIDTH, SLOT, dtype=BF16),
            ],
        ),
        out_shape=[
            struct(UTTS, SLOT, WIDTH, dtype=BF16),
            struct(2, WIDTH, 1024, dtype=BF16),
            struct(8, WIDTH),
            struct(HEADS, SLOT),
        ],
        compiler_params=params(),
        cost_estimate=pl.CostEstimate(
            flops=6 * ROWS * 512 * 1536, bytes_accessed=20 << 20, transcendentals=0
        ),
        name="attend_backward",
    )(
        info,
        slopes,
        mixing,
        frames,
        grad_merged,
        grad_mixer,
        triple,
        context,
        log_total,
        norm,
        weights,
    )


EXTENT = {"x": 4, "y": 4, "z": 4, "core": 2, "branch": 2}


def device_index(x, y, z, core):
    return (y % 2) * 64 + ((x * 4 + z) * 2 + y // 2) * 2 + core


def shift(value, axis, distance):
    pairs = []
    for x in range(4):
        for y in range(4):
            for z in range(4):
                for core in range(2):
                    at = {"x": x, "y": y, "z": z, "core": core}
                    to = dict(at)
                    if axis == "branch":
                        to["y"] = y ^ 1
                    else:
                        to[axis] = (at[axis] + distance) % EXTENT[axis]
                    pairs.append((device_index(**at), device_index(**to)))
    return lax.ppermute(value, ("branch", "dp"), pairs)


def gather_weights(local, core, place):
    columns = local.shape[1]
    half = columns // 2
    other = shift(local, "core", 1)
    pair = jnp.where(
        core == 0, jnp.concatenate([local, other]), jnp.concatenate([other, local])
    )
    block = lax.dynamic_slice_in_dim(pair, core * half, half, 1)
    full = jnp.zeros((4, 16, half), BF16)
    pieces = [block] + [shift(block, "y", s) for s in (1, 3, 2)]
    for s, piece in zip((0, 1, 3, 2), pieces):
        at = (place["y"] - s) % 4
        full = lax.dynamic_update_slice(full, piece[None], ((at % 2) * 2 + at // 2, 0, 0))
    block = full.reshape(2, 32, half)
    for axis, rows in (("z", 32), ("x", 128)):
        full = jnp.zeros((2, 4 * rows, half), BF16)
        pieces = [block] + [shift(block, axis, s) for s in (1, 3, 2)]
        for s, piece in zip((0, 1, 3, 2), pieces):
            at = (place[axis] - s) % 4
            full = lax.dynamic_update_slice(full, piece, (0, at * rows, 0))
        block = full
    other = shift(block, "core", 1)
    return jnp.where(
        core == 0,
        jnp.concatenate([block, other], axis=2),
        jnp.concatenate([other, block], axis=2),
    )


def add_low(terms):
    total = (terms[0].astype(F32) + terms[1].astype(F32)) + (
        terms[2].astype(F32) + terms[3].astype(F32)
    )
    return total


def scatter_grads(grads, core, place):
    half = grads.shape[2] // 2
    keep = lax.dynamic_slice_in_dim(grads, core * half, half, 2)
    send = lax.dynamic_slice_in_dim(grads, (1 - core) * half, half, 2)
    block = (keep.astype(F32) + shift(send, "core", 1).astype(F32)).astype(BF16)
    for axis, rows in (("x", 128), ("z", 32)):
        terms = [lax.dynamic_slice_in_dim(block, place[axis] * rows, rows, 1)]
        for s in (2, 1, 3):
            piece = lax.dynamic_slice_in_dim(block, ((place[axis] + s) % 4) * rows, rows, 1)
            terms.append(shift(piece, axis, s))
        block = add_low(terms).astype(BF16)
    block = block.reshape(4, 16, half)

    def at_y(y):
        return lax.dynamic_slice_in_dim(block, (y % 2) * 2 + y // 2, 1, 0)[0]

    terms = [at_y(place["y"])]
    for s in (2, 1, 3):
        terms.append(shift(at_y((place["y"] + s) % 4), "y", s))
    total = add_low(terms)
    keep = lax.dynamic_slice_in_dim(total, core * 8, 8, 0)
    send = lax.dynamic_slice_in_dim(total, (1 - core) * 8, 8, 0)
    other = shift(send, "core", 1)
    return jnp.where(
        core == 0,
        jnp.concatenate([keep, other], axis=1),
        jnp.concatenate([other, keep], axis=1),
    )


def sum_all(values):
    values = values + shift(values, "core", 1)
    for axis in ("x", "z", "y"):
        values = (values + shift(values, axis, 2)) + (shift(values, axis, 1) + shift(values, axis, 3))
    return values


def shards(
    frames,
    attend_norm,
    attend_in,
    attend_out,
    position_slope,
    mixer_norm,
    mixer_in,
    gating_norm,
    kernel_taps,
    kernel_bias,
    mixer_out,
    merge_logits,
    final_norm,
    lengths,
    cotangent,
):
    branch = lax.axis_index("branch")
    dp = lax.axis_index("dp")
    core = dp % 2
    place = {"x": dp // 16, "z": (dp // 4) % 4, "y": ((dp // 2) % 2) * 2 + branch}
    attend_w = gather_weights(
        jnp.concatenate([attend_in.reshape(8, 768), attend_out], axis=1), core, place
    )
    mixer_w = gather_weights(
        jnp.concatenate([mixer_in.reshape(8, 1536), mixer_out], axis=1), core, place
    )
    slopes_row = jnp.pad(position_slope, (0, 764))[None]
    local = jnp.concatenate([gating_norm, kernel_taps, kernel_bias[None], slopes_row])
    other = shift(local, "branch", 1)
    wide = jnp.where(
        branch == 0,
        jnp.concatenate([local, other], axis=1),
        jnp.concatenate([other, local], axis=1),
    )
    gnorm = wide[0:2]
    taps = jnp.pad(wide[2:33], ((0, 1), (0, 0)))
    bias = wide[33:34]
    slopes = jnp.concatenate([wide[34, 0:4], wide[34, 768:772]])
    own_lengths = lax.dynamic_slice_in_dim(lengths, branch, 1, 1)[:, 0]
    info = jnp.concatenate([branch[None].astype(jnp.int32), own_lengths])
    merge_exp = jnp.exp(merge_logits - jnp.max(merge_logits))
    mixing = merge_exp / jnp.sum(merge_exp)

    triple, context, log_total = run_attend_forward(info, slopes, frames, attend_norm, attend_w)
    layer, grad_merged, grad_mixer, mixer_grads, small_wide, small_mixer = run_mixer(
        info,
        mixing,
        frames,
        cotangent,
        context,
        mixer_norm,
        final_norm,
        gnorm,
        taps,
        bias,
        mixer_w,
        attend_w,
    )
    frame_grads, attend_grads, small_attend, slope_grads = run_attend_backward(
        info,
        slopes,
        mixing,
        frames,
        grad_merged,
        grad_mixer,
        triple,
        context,
        log_total,
        attend_norm,
        attend_w,
    )

    def both(own):
        other = shift(own, "branch", 1)
        pair = jnp.where(
            branch == 0, jnp.stack([own, other], axis=1), jnp.stack([other, own], axis=1)
        )
        return pair.astype(F32)

    layer_out = both(layer)
    frames_out = both(frame_grads)
    mixer_sums = scatter_grads(mixer_grads, core, place)
    attend_sums = scatter_grads(attend_grads, core, place)
    small = sum_all(
        jnp.concatenate(
            [
                small_wide[0:34].reshape(-1),
                small_mixer[0:6].reshape(-1),
                small_attend[0:2].reshape(-1),
                slope_grads.reshape(-1),
            ]
        )
    )
    wide_sum = small[0 : 34 * HALF].reshape(34, HALF)
    narrow = small[34 * HALF : 34 * HALF + 8 * WIDTH].reshape(8, WIDTH)
    slope_sum = jnp.sum(small[34 * HALF + 8 * WIDTH :].reshape(HEADS, SLOT), axis=1)
    wide_own = lax.dynamic_slice_in_dim(wide_sum, branch * 768, 768, 1)
    slope_own = lax.dynamic_slice_in_dim(slope_sum, branch * 4, 4, 0)
    branch_sums = jnp.sum(narrow[2:4], axis=1)
    merge_grad = mixing * (branch_sums - jnp.sum(mixing * branch_sums))
    return (
        layer_out,
        frames_out,
        narrow[6:8],
        attend_sums[:, 0:768].reshape(8, 3, 256),
        attend_sums[:, 768:1024],
        slope_own,
        narrow[4:6],
        mixer_sums[:, 0:1536].reshape(8, 2, 768),
        wide_own[32:34],
        wide_own[0:31],
        wide_own[31],
        mixer_sums[:, 1536:2304],
        merge_grad,
        narrow[0:2],
    )


def solution(mesh):
    placed = (
        P(None, "dp", None, None),
        P(),
        P("dp", None, "branch"),
        P("dp", "branch"),
        P("branch"),
        P(),
        P("dp", None, "branch"),
        P(None, "branch"),
        P(None, "branch"),
        P("branch"),
        P("dp", "branch"),
        P(),
        P(),
        P(None, "dp"),
        P(None, "dp", None, None),
    )
    return jax.shard_map(
        shards,
        mesh=mesh,
        in_specs=placed,
        out_specs=(
            P(None, "dp", None, None),
            P(None, "dp", None, None),
            P(),
            P("dp", None, "branch"),
            P("dp", "branch"),
            P("branch"),
            P(),
            P("dp", None, "branch"),
            P(None, "branch"),
            P(None, "branch"),
            P("branch"),
            P("dp", "branch"),
            P(),
            P(),
        ),
        check_vma=False,
    )
```

```python
from functools import partial

import jax
import jax.numpy as jnp
import numpy as np
from jax import lax
from jax.experimental import pallas as pl
from jax.experimental.pallas import tpu as pltpu
from jax.sharding import Mesh
from jax.sharding import PartitionSpec as P

EPSILON = 1e-05
NEGATIVE = -1e30
F32 = jnp.float32
BF16 = jnp.bfloat16
SLOT = 256
WIDTH = 512
HEADS = 8
HEAD = 64
HALF = 1536
TAPS = 31
REACH = 15
UTTS = 3
ROWS = UTTS * SLOT
PERIOD = SLOT + REACH
BINS = (PERIOD + 1) // 2
SPEC = 2 * BINS
BLOCK = 256
BLOCKS = HALF // BLOCK
PER_BRANCH = 768 // BLOCK
GELU_A = 0.7978845608028654
GELU_B = GELU_A * 0.044715
HEAD_UNROLL = 8
VMEM_LIMIT = 60 * 1024 * 1024


def transform_tables():
    bins = np.arange(BINS)[:, None]
    angle = 2 * np.pi * bins * np.arange(SLOT)[None, :] / PERIOD
    lag_angle = 2 * np.pi * bins * (np.arange(TAPS) - REACH)[None, :] / PERIOD
    weight = np.where(bins == 0, 1.0, 2.0) / PERIOD
    forward = np.concatenate([np.cos(angle), -np.sin(angle)], 0)
    inverse = np.concatenate([np.cos(angle) * weight, -np.sin(angle) * weight], 0).T
    tap_forward = np.concatenate([np.cos(lag_angle), -np.sin(lag_angle)], 0)
    tap_inverse = np.concatenate([np.cos(lag_angle) * weight, -np.sin(lag_angle) * weight], 0).T
    tap_forward = np.pad(tap_forward, ((0, 0), (0, 1)))
    tap_high = np.asarray(tap_forward.astype(BF16)).astype(np.float64)
    tap_forward = np.concatenate([tap_high, tap_high, tap_forward - tap_high], 1)
    tap_inverse = np.pad(tap_inverse, ((0, 1), (0, 0)))
    return forward, inverse, tap_forward, tap_inverse


def dot_nn(a, b):
    return lax.dot_general(a, b, (((1,), (0,)), ((), ())), preferred_element_type=F32)


def dot_nt(a, b):
    return lax.dot_general(a, b, (((1,), (1,)), ((), ())), preferred_element_type=F32)


def dot_tn(a, b):
    return lax.dot_general(a, b, (((0,), (0,)), ((), ())), preferred_element_type=F32)


def dot_tt(a, b):
    return lax.dot_general(a, b, (((0,), (1,)), ((), ())), preferred_element_type=F32)


def standardize(rows_in):
    average = jnp.mean(rows_in, axis=-1, keepdims=True)
    centered = rows_in - average
    variance = jnp.mean(centered * centered, axis=-1, keepdims=True)
    rstd = lax.rsqrt(variance + EPSILON)
    return centered * rstd, rstd


def gelu_pair(v):
    square = v * v
    half = 0.5 + 0.5 * jnp.tanh(v * (GELU_A + GELU_B * square))
    active = v * half
    slope = half + active * (1.0 - half) * (2 * GELU_A + 6 * GELU_B * square)
    return active, slope


def merge_mix(merge_logits):
    exponent = jnp.exp(merge_logits[...] - jnp.max(merge_logits[...], axis=1, keepdims=True))
    mixing = exponent / jnp.sum(exponent, axis=1, keepdims=True)
    return mixing[:, 0:1], mixing[:, 1:2]


INFO_BRANCH, INFO_CORE, INFO_X, INFO_LENGTH = 0, 1, 2, 3
SHIFTS = (0, 1, 3, 2)


def piece_copies(info, pieces, target, sems):
    core = info[INFO_CORE]
    half = pieces[0].shape[2]
    copies = []
    for i, piece in enumerate(pieces):
        at = lax.rem(info[INFO_X] + (4 - SHIFTS[i // 2]), 4)
        side = core if i % 2 == 0 else 1 - core
        rows = pl.ds(pl.multiple_of(at * 128, 128), 128)
        columns = pl.ds(pl.multiple_of(side * half, 128), half)
        for b in range(2):
            copies.append(
                pltpu.make_async_copy(
                    piece.at[b], target.at[b, rows, columns], sems.at[2 * i + b]
                )
            )
    return copies


def pack_local(info, att_in, att_out, mix_in, mix_out, out):
    for i in range(3):
        out[:, i * 256 : (i + 1) * 256] = att_in[i]
    for i in range(2):
        out[:, 768 + i * 768 : 768 + (i + 1) * 768] = mix_in[:, i, :]
    out[:, 2304:3072] = mix_out[...]
    out[:, 3072:3328] = att_out[...]


def spread_block(info, local, other, out):
    core = info[INFO_CORE]
    mine, theirs = local[...].astype(F32), other[...].astype(F32)
    rows = jnp.concatenate(
        [jnp.where(core == 0, mine, theirs), jnp.where(core == 0, theirs, mine)], axis=0
    )
    block = jnp.concatenate(
        [
            jnp.where(core == 0, rows[:, 0:384], rows[:, 384:768]),
            jnp.where(core == 0, rows[:, 768:2048], rows[:, 2048:3328]),
        ],
        axis=1,
    ).astype(BF16)
    for j in range(16):
        out[j] = block


def fill_distance(distance):
    key_at = lax.broadcasted_iota(jnp.int32, (SLOT, SLOT), 0)
    query_at = lax.broadcasted_iota(jnp.int32, (SLOT, SLOT), 1)
    offset = (key_at - query_at).astype(F32)
    distance[...] = jnp.sqrt(offset * offset + 1.0)


def attend_forward(
    info,
    frames,
    norm,
    own,
    other,
    *rest,
):
    pieces, (triple, context, log_total, weights, slopes, bias_s, sems) = rest[:8], rest[8:]
    step = pl.program_id(0)
    copies = piece_copies(info, pieces, weights, sems)

    @pl.when(step == 0)
    def _():
        for copy in copies:
            copy.start()
        branch = info[INFO_BRANCH]
        key_at = lax.broadcasted_iota(jnp.int32, (SLOT, SLOT), 0)
        query_at = lax.broadcasted_iota(jnp.int32, (SLOT, SLOT), 1)
        offset = (key_at - query_at).astype(F32)
        distance = jnp.sqrt(offset * offset + 1.0)
        for h in range(HEADS):
            lane = slice(h % 4, h % 4 + 1)
            slope = jnp.where(branch == h // 4, own[34:35, lane], other[34:35, lane])
            slopes[h : h + 1, :] = jnp.broadcast_to(slope, (1, 128))
            bias_s[h] = slope * distance
        for copy in copies:
            copy.wait()

    normed, _ = standardize(frames[0, 0])
    low = (normed * norm[0:1] + norm[1:2]).astype(BF16)
    for b in range(2):
        part = dot_tt(weights[b, :, 0:256], low) * (HEAD**-0.5)
        triple[0, b * 768 : b * 768 + 256, :] = part.astype(BF16)
        part = dot_tt(weights[b, :, 256:768], low)
        triple[0, b * 768 + 256 : (b + 1) * 768, :] = part.astype(BF16)
    is_key = lax.broadcasted_iota(jnp.int32, (SLOT, SLOT), 0) < info[INFO_LENGTH + step]

    def head(h, carry):
        base = pl.multiple_of((h // 4) * 768 + (h % 4) * HEAD, HEAD)
        q = triple[0, pl.ds(base, HEAD), :]
        k = triple[0, pl.ds(base + 256, HEAD), :]
        v = triple[0, pl.ds(base + 512, HEAD), :]
        logits = jnp.where(is_key, dot_tn(k, q) - bias_s[h], NEGATIVE)
        highest = jnp.max(logits, axis=0, keepdims=True)
        exponent = jnp.exp(logits - highest)
        total = jnp.sum(exponent, axis=0, keepdims=True)
        prob = (exponent * (1.0 / total)).astype(BF16)
        context[0, pl.ds(pl.multiple_of(h * HEAD, HEAD), HEAD), :] = dot_nn(v, prob).astype(BF16)
        log_total[0, pl.ds(h, 1), :] = highest + jnp.log(total)
        return carry

    lax.fori_loop(0, HEADS, head, 0, unroll=HEAD_UNROLL)


def mixer_both(
    info,
    frames,
    cotangent,
    context,
    mixer_norm,
    final_norm,
    merge_logits,
    own,
    other,
    forward,
    inverse,
    tap_forward,
    tap_inverse,
    *rest,
):
    pieces, rest = rest[:8], rest[8:]
    (
        layer,
        grad_frames,
        grad_context,
        keep,
        send,
        small,
        weights,
        params_s,
        small_wide,
        small_narrow,
        tap_spec,
        second_s,
        second_slope,
        first_s,
        first_slope,
        conv_s,
        spec_s,
        cross_s,
        back_s,
        gated_s,
        hidden_s,
        low_s,
        grad_s,
        attend_s,
        context_s,
        grads_s,
        sems,
    ) = rest
    step = pl.program_id(0)
    branch, core = info[INFO_BRANCH], info[INFO_CORE]
    here = pl.ds(pl.multiple_of(step * SLOT, SLOT), SLOT)
    copies = piece_copies(info, pieces, weights, sems)

    @pl.when(step == 0)
    def _():
        for copy in copies:
            copy.start()
        params_s[branch] = own[...]
        params_s[1 - branch] = other[...]
        for b in range(2):
            high, low = split_low(params_s[b, 0:32, :])
            stacked = jnp.concatenate([high, low, high], axis=0).astype(BF16)
            tap_spec[:, b * 768 : (b + 1) * 768] = dot_nn(tap_forward[...], stacked)
        cross_s[...] = jnp.zeros_like(cross_s)
        small_wide[...] = jnp.zeros_like(small_wide)
        small_narrow[...] = jnp.zeros_like(small_narrow)
        for copy in copies:
            copy.wait()

    mix_attend, mix_mixer = merge_mix(merge_logits)
    rows_in = frames[0, 0]
    normed, rstd = standardize(rows_in)
    low = (normed * mixer_norm[0:1] + mixer_norm[1:2]).astype(BF16)
    low_s[here, :] = low
    length = info[INFO_LENGTH + step]
    valid = (lax.broadcasted_iota(jnp.int32, (SLOT, 1), 0) < length).astype(F32)

    places = [
        (k // PER_BRANCH, slice((k % PER_BRANCH) * BLOCK, (k % PER_BRANCH + 1) * BLOCK),
         slice(k * BLOCK, (k + 1) * BLOCK))
        for k in range(BLOCKS)
    ]

    def weight(b, kind, off):
        return weights[b, :, kind * 768 + off.start : kind * 768 + off.stop]

    def fold(v):
        return v[:, 0:128] + v[:, 128:256]

    def lane_sum(v):
        return jnp.sum(v, axis=-1, keepdims=True)

    total = jnp.zeros((SLOT, 128), F32)
    for b, off, wide in places:
        active, slope = gelu_pair(dot_nn(low, weight(b, 1, off)))
        second_s[:, wide] = active
        second_slope[:, wide] = slope
        total += fold(active)
    average = lane_sum(total) / HALF
    total = jnp.zeros((SLOT, 128), F32)
    for b, off, wide in places:
        centered = second_s[:, wide] - average
        total += fold(centered * centered)
    gate_rstd = lax.rsqrt(lane_sum(total) / HALF + EPSILON)

    for b, off, wide in places:
        standard = (second_s[:, wide] - average) * gate_rstd
        gate_in = (standard * params_s[b, 32:33, off] + params_s[b, 33:34, off]) * valid
        spec = dot_nn(forward[...], gate_in.astype(BF16))
        spec_s[:, wide] = spec
        real, imag = spec[0:BINS], spec[BINS:SPEC]
        tap_real, tap_imag = tap_spec[0:BINS, wide], tap_spec[BINS:SPEC, wide]
        product = jnp.concatenate(
            [real * tap_real + imag * tap_imag, imag * tap_real - real * tap_imag], axis=0
        )
        conved = dot_nn(inverse[...], product.astype(BF16)) + params_s[b, 31:32, off]
        conv_s[:, wide] = conved
        active, slope = gelu_pair(dot_nn(low, weight(b, 0, off)))
        first_s[:, wide] = active
        first_slope[:, wide] = slope
        gated_s[here, wide] = (active * conved).astype(BF16)

    mixer_part = dot_nt(gated_s[here, 0:768], weights[0, :, 1536:2304]) + dot_nt(
        gated_s[here, 768:1536], weights[1, :, 1536:2304]
    )
    context_s[:, here] = context[0]
    attend_part = dot_tt(context[0, 0:256, :], weights[0, :, 2304:2560]) + dot_tt(
        context[0, 256:512, :], weights[1, :, 2304:2560]
    )
    merged = rows_in + mix_attend * attend_part + mix_mixer * mixer_part
    merged_normed, merged_rstd = standardize(merged)
    layer[0] = ((merged_normed * final_norm[0:1] + final_norm[1:2]) * valid).astype(BF16)
    grad_out = cotangent[0, 0] * valid
    scaled = grad_out * final_norm[0:1]
    grad_merged = merged_rstd * (
        scaled
        - jnp.mean(scaled, axis=-1, keepdims=True)
        - merged_normed * jnp.mean(scaled * merged_normed, axis=-1, keepdims=True)
    )
    small_narrow[0:1] += jnp.sum(grad_out * merged_normed, axis=0, keepdims=True)
    small_narrow[1:2] += jnp.sum(grad_out, axis=0, keepdims=True)
    small_narrow[2:3] += jnp.sum(grad_merged * attend_part, axis=0, keepdims=True)
    small_narrow[3:4] += jnp.sum(grad_merged * mixer_part, axis=0, keepdims=True)
    grad_mixer = (mix_mixer * grad_merged).astype(BF16)
    grad_s[here, :] = grad_mixer
    grad_attend = (mix_attend * grad_merged).astype(BF16)
    attend_s[here, :] = grad_attend
    for b in range(2):
        grad_context[0, b * 256 : (b + 1) * 256, :] = dot_tt(
            weights[b, :, 2304:2560], grad_attend
        ).astype(BF16)

    total, cross_total = jnp.zeros((SLOT, 128), F32), jnp.zeros((SLOT, 128), F32)
    for b, off, wide in places:
        grad_gated = dot_nn(grad_mixer, weight(b, 2, off))
        grad_conved = grad_gated * first_s[:, wide]
        hidden_s[here, wide] = (first_slope[:, wide] * (grad_gated * conv_s[:, wide])).astype(BF16)
        small_wide[31:32, wide] += jnp.sum(grad_conved, axis=0, keepdims=True)
        grad_spec = dot_nn(forward[...], grad_conved.astype(BF16))
        grad_real, grad_imag = grad_spec[0:BINS], grad_spec[BINS:SPEC]
        real, imag = spec_s[0:BINS, wide], spec_s[BINS:SPEC, wide]
        cross_s[0:BINS, wide] += grad_real * real + grad_imag * imag
        cross_s[BINS:SPEC, wide] += grad_real * imag - grad_imag * real
        tap_real, tap_imag = tap_spec[0:BINS, wide], tap_spec[BINS:SPEC, wide]
        product = jnp.concatenate(
            [
                grad_real * tap_real - grad_imag * tap_imag,
                grad_real * tap_imag + grad_imag * tap_real,
            ],
            axis=0,
        )
        grad_gate = dot_nn(inverse[...], product.astype(BF16)) * valid
        standard = (second_s[:, wide] - average) * gate_rstd
        small_wide[32:33, wide] += jnp.sum(grad_gate * standard, axis=0, keepdims=True)
        small_wide[33:34, wide] += jnp.sum(grad_gate, axis=0, keepdims=True)
        grad_standard = grad_gate * params_s[b, 32:33, off]
        back_s[:, wide] = grad_standard
        total += fold(grad_standard)
        cross_total += fold(grad_standard * standard)
    back_average = lane_sum(total) / HALF
    back_scale = lane_sum(cross_total) / HALF

    for b, off, wide in places:
        standard = (second_s[:, wide] - average) * gate_rstd
        grad_second = gate_rstd * (back_s[:, wide] - back_average - standard * back_scale)
        hidden_s[here, HALF + wide.start : HALF + wide.stop] = (
            second_slope[:, wide] * grad_second
        ).astype(BF16)
    grad_low = (
        dot_nt(hidden_s[here, 0:768], weights[0, :, 0:768])
        + dot_nt(hidden_s[here, 768:1536], weights[1, :, 0:768])
    ) + (
        dot_nt(hidden_s[here, 1536:2304], weights[0, :, 768:1536])
        + dot_nt(hidden_s[here, 2304:3072], weights[1, :, 768:1536])
    )
    small_narrow[4:5] += jnp.sum(grad_low * normed, axis=0, keepdims=True)
    small_narrow[5:6] += jnp.sum(grad_low, axis=0, keepdims=True)
    scaled = grad_low * mixer_norm[0:1]
    grad_frames[0] = grad_merged + rstd * (
        scaled
        - jnp.mean(scaled, axis=-1, keepdims=True)
        - normed * jnp.mean(scaled * normed, axis=-1, keepdims=True)
    )

    @pl.when(step == UTTS - 1)
    def _():
        outs = []
        for half in range(2):
            for b in range(2):
                if half == 0:
                    parts = [
                        dot_tn(low_s[...], hidden_s[:, b * 768 : (b + 1) * 768]),
                        dot_tn(low_s[...], hidden_s[:, HALF + b * 768 : HALF + b * 768 + 512]),
                    ]
                else:
                    parts = [
                        dot_tn(
                            low_s[...], hidden_s[:, HALF + b * 768 + 512 : HALF + (b + 1) * 768]
                        ),
                        dot_tn(grad_s[...], gated_s[:, b * 768 : (b + 1) * 768]),
                        dot_tt(attend_s[...], context_s[b * 256 : (b + 1) * 256, :]),
                    ]
                column = 0
                for part in parts:
                    grads_s[half, b, :, column : column + part.shape[1]] = part.astype(BF16)
                    column += part.shape[1]
                for i, target in enumerate((keep, send)):
                    copy = pltpu.make_async_copy(
                        grads_s.at[half, b], target.at[b], sems.at[half * 2 + b]
                    )
                    outs.append((core == half if i == 0 else core != half, copy))
                    pl.when(outs[-1][0])(copy.start)
        tap_grad = dot_nn(tap_inverse[...], cross_s[...].astype(BF16))
        small_wide[0:31, :] = tap_grad[0:31]
        for g in range(12):
            small[g * 40 : (g + 1) * 40, :] = small_wide[:, g * 128 : (g + 1) * 128]
        for j in range(4):
            small[480 + 8 * j : 488 + 8 * j, :] = small_narrow[:, j * 128 : (j + 1) * 128]
        for wanted, copy in outs:
            pl.when(wanted)(copy.wait)


def attend_backward(
    info,
    frames,
    grad_mixed,
    triple,
    log_total,
    grad_context,
    norm,
    slopes,
    weights,
    frames_grad,
    keep,
    send,
    distance,
    low_s,
    triple_t,
    small,
    grads_s,
    sems,
):
    step = pl.program_id(0)
    here = pl.ds(pl.multiple_of(step * SLOT, SLOT), SLOT)
    core = info[INFO_CORE]

    @pl.when(step == 0)
    def _():
        fill_distance(distance)
        small[...] = jnp.zeros_like(small)

    normed, rstd = standardize(frames[0, 0])
    low_s[here, :] = (normed * norm[0:1] + norm[1:2]).astype(BF16)
    is_key = lax.broadcasted_iota(jnp.int32, (SLOT, SLOT), 0) < info[INFO_LENGTH + step]

    def head(h, carry):
        base = pl.multiple_of((h // 4) * 768 + (h % 4) * HEAD, HEAD)
        q = triple[0, pl.ds(base, HEAD), :]
        k = triple[0, pl.ds(base + 256, HEAD), :]
        v = triple[0, pl.ds(base + 512, HEAD), :]
        grad_here = grad_context[0, pl.ds(pl.multiple_of(h * HEAD, HEAD), HEAD), :]
        logits = dot_tn(k, q) - slopes[pl.ds(h, 1), 0:1] * distance[...]
        logits = jnp.where(is_key, logits, NEGATIVE)
        prob = jnp.exp(logits - log_total[0, pl.ds(h, 1), :])
        grad_prob = dot_tn(v, grad_here)
        row_dot = jnp.sum(prob * grad_prob, axis=0, keepdims=True)
        grad_logits = prob * (grad_prob - row_dot)
        slope_row = -jnp.sum(grad_logits * distance[...], axis=0, keepdims=True)
        small[pl.ds(8 + h, 1), :] += slope_row[:, 0:128] + slope_row[:, 128:256]
        grad_scores = grad_logits.astype(BF16)
        grad_q = dot_nn(k, grad_scores) * (HEAD**-0.5)
        grad_k = dot_nt(q, grad_scores)
        grad_v = dot_nt(grad_here, prob.astype(BF16))
        triple_t[pl.ds(base, HEAD), here] = grad_q.astype(BF16)
        triple_t[pl.ds(base + 256, HEAD), here] = grad_k.astype(BF16)
        triple_t[pl.ds(base + 512, HEAD), here] = grad_v.astype(BF16)
        return carry

    lax.fori_loop(0, HEADS, head, 0, unroll=HEAD_UNROLL)
    grad_low = dot_tt(triple_t[0:768, here], weights[0]) + dot_tt(
        triple_t[768:1536, here], weights[1]
    )
    gain_row = jnp.sum(grad_low * normed, axis=0, keepdims=True)
    bias_row = jnp.sum(grad_low, axis=0, keepdims=True)
    for j in range(4):
        small[j : j + 1, :] += gain_row[:, j * 128 : (j + 1) * 128]
        small[4 + j : 5 + j, :] += bias_row[:, j * 128 : (j + 1) * 128]
    scaled = grad_low * norm[0:1]
    frames_grad[0] = (
        grad_mixed[0]
        + rstd
        * (
            scaled
            - jnp.mean(scaled, axis=-1, keepdims=True)
            - normed * jnp.mean(scaled * normed, axis=-1, keepdims=True)
        )
    ).astype(BF16)

    @pl.when(step == UTTS - 1)
    def _():
        high, low = split_low(small[...])
        pair = jnp.concatenate([high, low], axis=1).astype(BF16)
        outs = []
        for half in range(2):
            for b in range(2):
                rows = b * 768 + half * 512
                if half == 0:
                    grads_s[half, b] = dot_tt(low_s[...], triple_t[rows : rows + 512, :]).astype(
                        BF16
                    )
                else:
                    grads_s[half, b, :, 0:256] = dot_tt(
                        low_s[...], triple_t[rows : rows + 256, :]
                    ).astype(BF16)
                    for m in range(32):
                        grads_s[half, b, 16 * m : 16 * m + 16, 256:512] = pair
                for i, target in enumerate((keep, send)):
                    copy = pltpu.make_async_copy(
                        grads_s.at[half, b], target.at[b], sems.at[half * 2 + b]
                    )
                    outs.append((core == half if i == 0 else core != half, copy))
                    pl.when(outs[-1][0])(copy.start)
        for wanted, copy in outs:
            pl.when(wanted)(copy.wait)


def split_low(value):
    high = value.astype(BF16).astype(F32)
    return high, value - high


def start_all(copies):
    for copy in copies:
        copy.start()
    return copies


def chunk_copies(source, target, count, sems):
    size = target.shape[0] // count
    return start_all(
        [
            pltpu.make_async_copy(
                source.at[pl.ds(i * size, size)], target.at[pl.ds(i * size, size)], sems.at[i]
            )
            for i in range(count)
        ]
    )


CHUNKS = 8


def sum_mixer(info, keep, other, small, small_other, out, keep_s, other_s, out_s, sems):
    first = chunk_copies(keep, keep_s, CHUNKS, sems.at[0])
    second = chunk_copies(other, other_s, CHUNKS, sems.at[1])
    high, low = split_low(small[...] + small_other[...])
    for j in range(64):
        rows = slice(8 * j, 8 * j + 8)
        out_s[16 * j : 16 * j + 16, 1280:1408] = jnp.concatenate(
            [high[rows], low[rows]], axis=0
        ).astype(BF16)
    outs = []
    for i in range(CHUNKS):
        rows = slice(i * 128, (i + 1) * 128)
        first[i].wait()
        second[i].wait()
        out_s[rows, 0:1280] = (keep_s[rows].astype(F32) + other_s[rows].astype(F32)).astype(BF16)
        outs.append(pltpu.make_async_copy(out_s.at[rows], out.at[rows], sems.at[2, i]))
        outs[-1].start()
    for copy in outs:
        copy.wait()


def sum_attend(info, keep, other, mixer_total, out, keep_s, other_s, out_s, sems):
    first = chunk_copies(keep, keep_s, CHUNKS, sems.at[0])
    second = chunk_copies(other, other_s, CHUNKS, sems.at[1])
    high, low = split_low(mixer_total[0:8, :] + mixer_total[8:16, :])
    block = jnp.concatenate([high, low], axis=0).astype(BF16)
    outs = []
    for i in range(CHUNKS):
        rows = slice(i * 128, (i + 1) * 128)
        first[i].wait()
        second[i].wait()
        total = keep_s[rows].astype(F32) + other_s[rows].astype(F32)
        out_s[rows, 0:512] = total.astype(BF16)

        @pl.when(info[INFO_CORE] == 1)
        def _():
            high, low = split_low(total[:, 256:384] + total[:, 384:512])
            out_s[rows, 256:384] = high.astype(BF16)
            out_s[rows, 384:512] = low.astype(BF16)

        for j in range(8):
            out_s[i * 128 + 16 * j : i * 128 + 16 * j + 16, 512:640] = block
        outs.append(pltpu.make_async_copy(out_s.at[rows], out.at[rows], sems.at[2, i]))
        outs[-1].start()
    for copy in outs:
        copy.wait()


def sum_chips(info, terms, out, *rest):
    small = rest[0] if len(rest) == 3 else None
    terms_s, sems = rest[-2:]
    copies = chunk_copies(terms, terms_s, CHUNKS, sems)
    columns = out.shape[1]
    for c in range(CHUNKS):
        copies[c].wait()
        parts = [terms_s[8 * c + i, :, 0:columns].astype(F32) for i in range(8)]
        total = ((parts[0] + parts[1]) + (parts[2] + parts[3])) + (
            (parts[4] + parts[5]) + (parts[6] + parts[7])
        )
        if c == 0:
            out[...] = total
        else:
            out[...] += total
        if small is not None:
            for i in range(8 * c, 8 * c + 8):
                pair = terms_s[i, :, columns : columns + 128].astype(F32)
                small[8 * i : 8 * i + 8, :] = pair[0:8] + pair[8:16]


def finish(
    info,
    merge_logits,
    mixer_mine,
    mixer_theirs,
    mine,
    theirs,
    small,
    att_in,
    att_out,
    mix_in,
    mix_out,
    anorm,
    mnorm,
    fnorm,
    gnorm,
    taps,
    bias,
    slope,
    merge,
):
    core, branch = info[INFO_CORE], info[INFO_BRANCH]

    def rows(v):
        return jnp.where(core == 0, v[0:8], v[8:16])

    def halves(a, b):
        return jnp.where(core == 0, a, b), jnp.where(core == 0, b, a)

    low, high = halves(rows(mixer_mine), rows(mixer_theirs))
    first, second = halves(mine[...], theirs[...])
    att_in[0] = rows(first)[:, 0:256]
    att_in[1] = rows(first)[:, 256:512]
    att_in[2] = rows(second)[:, 0:256]
    mix_in[:, 0, :] = low[:, 0:768]
    mix_in[:, 1, :] = jnp.concatenate([low[:, 768:1280], high[:, 0:256]], axis=1)
    mix_out[...] = high[:, 256:1024]
    att_out[...] = high[:, 1024:1280]
    little = second[:, 256:384] + second[:, 384:512]
    for p in range(2):
        for j in range(4):
            anorm[p : p + 1, j * 128 : (j + 1) * 128] = little[p * 4 + j : p * 4 + j + 1]
    for r in range(4):
        slope[r] = jnp.where(
            branch == 0, jnp.sum(little[8 + r : 9 + r]), jnp.sum(little[12 + r : 13 + r])
        )
    for g in range(6):
        group = small[pl.ds(pl.multiple_of((branch * 6 + g) * 40, 8), 40), :]
        columns = slice(g * 128, (g + 1) * 128)
        taps[:, columns] = group[0:31]
        bias[:, columns] = group[31:32]
        gnorm[:, columns] = group[32:34]
    attend_sum, mixer_sum = 0.0, 0.0
    for j in range(4):
        columns = slice(j * 128, (j + 1) * 128)
        group = small[480 + 8 * j : 488 + 8 * j, :]
        fnorm[:, columns] = group[0:2]
        mnorm[:, columns] = group[4:6]
        attend_sum += jnp.sum(group[2:3], axis=1, keepdims=True)
        mixer_sum += jnp.sum(group[3:4], axis=1, keepdims=True)
    mix_attend, mix_mixer = merge_mix(merge_logits)
    average = mix_attend * attend_sum + mix_mixer * mixer_sum
    merge[0] = jnp.sum(mix_attend * (attend_sum - average))
    merge[1] = jnp.sum(mix_mixer * (mixer_sum - average))


def place_pair(info, own, other, out, own_s, other_s, out_s, sems):
    branch = info[INFO_BRANCH]
    loads = [
        start_all(
            [
                pltpu.make_async_copy(source.at[u], target.at[u], sems.at[p, u])
                for u in range(UTTS)
            ]
        )
        for p, (source, target) in enumerate(((own, own_s), (other, other_s)))
    ]
    stores = []
    for u in range(UTTS):
        for p, source in enumerate((own_s, other_s)):
            loads[p][u].wait()
            out_s[p, u] = source[u].astype(F32)
            at = branch if p == 0 else 1 - branch
            stores.append(
                pltpu.make_async_copy(out_s.at[p, u], out.at[u, at], sems.at[2 + p, u])
            )
            stores[-1].start()
    for copy in stores:
        copy.wait()


def whole(shape):
    return pl.BlockSpec(shape, lambda i, *_: (0,) * len(shape), pipeline_mode=pl.Buffered(1))


def per_utt(shape):
    return pl.BlockSpec((1,) + shape, lambda i, *_: (i,) + (0,) * len(shape))


ANY = pl.BlockSpec(memory_space=pl.ANY)
OWN_FRAMES = pl.BlockSpec((1, 1, SLOT, WIDTH), lambda i, info, *_: (i, info[0], 0, 0))


def scratch(*shape, dtype=F32):
    return pltpu.VMEM(shape, dtype)


def struct(*shape, dtype=F32):
    return jax.ShapeDtypeStruct(shape, dtype)


def call(kernel, name, info, operands, in_specs, outs, out_specs, scratches=(), grid=1, us=2, **extra):
    return pl.pallas_call(
        kernel,
        grid_spec=pltpu.PrefetchScalarGridSpec(
            num_scalar_prefetch=1,
            grid=(grid,),
            in_specs=in_specs,
            out_specs=out_specs,
            scratch_shapes=scratches,
        ),
        out_shape=outs,
        compiler_params=pltpu.CompilerParams(
            dimension_semantics=("arbitrary",), vmem_limit_bytes=VMEM_LIMIT
        ),
        cost_estimate=pl.CostEstimate(
            flops=us * 100000000, bytes_accessed=1 << 16, transcendentals=0
        ),
        name=name,
        **extra,
    )(info, *operands)


def run_pack(info, *operands):
    return call(
        pack_local,
        "pack_local",
        info,
        operands,
        [whole(a.shape) for a in operands],
        struct(8, 3328, dtype=BF16),
        whole((8, 3328)),
    )


def run_spread(info, local, other):
    return call(
        spread_block,
        "spread_block",
        info,
        (local, other),
        [whole((8, 3328))] * 2,
        struct(16, 16, 1664, dtype=BF16),
        whole((16, 16, 1664)),
    )


def run_attend_forward(info, frames, norm, own, other, pieces):
    return call(
        attend_forward,
        "attend_forward",
        info,
        (frames, norm, own, other, *pieces),
        [OWN_FRAMES, whole((2, WIDTH)), whole((35, 768)), whole((35, 768))] + [ANY] * 8,
        [
            struct(UTTS, HALF, SLOT, dtype=BF16),
            struct(UTTS, WIDTH, SLOT, dtype=BF16),
            struct(UTTS, HEADS, SLOT),
            struct(2, WIDTH, 768, dtype=BF16),
            struct(HEADS, 128),
        ],
        [
            per_utt((HALF, SLOT)),
            per_utt((WIDTH, SLOT)),
            per_utt((HEADS, SLOT)),
            whole((2, WIDTH, 768)),
            whole((HEADS, 128)),
        ],
        [scratch(HEADS, SLOT, SLOT), pltpu.SemaphoreType.DMA((16,))],
        grid=UTTS,
    )


def run_mixer(info, frames, cotangent, context, mnorm, fnorm, merge_logits, own, other, pieces):
    forward, inverse, tap_forward, tap_inverse = transform_tables()
    tables = (
        jnp.asarray(forward, BF16),
        jnp.asarray(inverse, BF16),
        jnp.asarray(tap_forward, BF16),
        jnp.asarray(tap_inverse, BF16),
    )
    return call(
        mixer_both,
        "mixer_both",
        info,
        (frames, cotangent, context, mnorm, fnorm, merge_logits, own, other, *tables, *pieces),
        [
            OWN_FRAMES,
            OWN_FRAMES,
            per_utt((WIDTH, SLOT)),
            whole((2, WIDTH)),
            whole((2, WIDTH)),
            whole((1, 2)),
            whole((35, 768)),
            whole((35, 768)),
            whole((SPEC, SLOT)),
            whole((SLOT, SPEC)),
            whole((SPEC, 96)),
            whole((32, SPEC)),
        ]
        + [ANY] * 8,
        [
            struct(UTTS, SLOT, WIDTH, dtype=BF16),
            struct(UTTS, SLOT, WIDTH),
            struct(UTTS, WIDTH, SLOT, dtype=BF16),
            struct(2, WIDTH, 1280, dtype=BF16),
            struct(2, WIDTH, 1280, dtype=BF16),
            struct(512, 128),
        ],
        [
            per_utt((SLOT, WIDTH)),
            per_utt((SLOT, WIDTH)),
            per_utt((WIDTH, SLOT)),
            ANY,
            ANY,
            whole((512, 128)),
        ],
        [
            scratch(2, WIDTH, 2560, dtype=BF16),
            scratch(2, 35, 768),
            scratch(40, HALF),
            scratch(8, WIDTH),
            scratch(SPEC, HALF),
            scratch(SLOT, HALF),
            scratch(SLOT, HALF),
            scratch(SLOT, HALF),
            scratch(SLOT, HALF),
            scratch(SLOT, HALF),
            scratch(SPEC, HALF),
            scratch(SPEC, HALF),
            scratch(SLOT, HALF),
            scratch(ROWS, HALF, dtype=BF16),
            scratch(ROWS, 2 * HALF, dtype=BF16),
            scratch(ROWS, WIDTH, dtype=BF16),
            scratch(ROWS, WIDTH, dtype=BF16),
            scratch(ROWS, WIDTH, dtype=BF16),
            scratch(WIDTH, ROWS, dtype=BF16),
            scratch(2, 2, WIDTH, 1280, dtype=BF16),
            pltpu.SemaphoreType.DMA((16,)),
        ],
        grid=UTTS,
    )


def run_attend_backward(
    info, frames, grad_mixed, triple, log_total, grad_context, norm, slopes, weights
):
    return call(
        attend_backward,
        "attend_backward",
        info,
        (frames, grad_mixed, triple, log_total, grad_context, norm, slopes, weights),
        [
            OWN_FRAMES,
            per_utt((SLOT, WIDTH)),
            per_utt((HALF, SLOT)),
            per_utt((HEADS, SLOT)),
            per_utt((WIDTH, SLOT)),
            whole((2, WIDTH)),
            whole((HEADS, 128)),
            whole((2, WIDTH, 768)),
        ],
        [
            struct(UTTS, SLOT, WIDTH, dtype=BF16),
            struct(2, WIDTH, 512, dtype=BF16),
            struct(2, WIDTH, 512, dtype=BF16),
        ],
        [per_utt((SLOT, WIDTH)), ANY, ANY],
        [
            scratch(SLOT, SLOT),
            scratch(ROWS, WIDTH, dtype=BF16),
            scratch(HALF, ROWS, dtype=BF16),
            scratch(16, 128),
            scratch(2, 2, WIDTH, 512, dtype=BF16),
            pltpu.SemaphoreType.DMA((4,)),
        ],
        grid=UTTS,
    )


def run_sum_mixer(info, keep, other, small, small_other):
    return call(
        sum_mixer,
        "sum_mixer",
        info,
        (keep.reshape(1024, 1280), other.reshape(1024, 1280), small, small_other),
        [ANY, ANY, whole((512, 128)), whole((512, 128))],
        struct(1024, 1408, dtype=BF16),
        ANY,
        [
            scratch(1024, 1280, dtype=BF16),
            scratch(1024, 1280, dtype=BF16),
            scratch(1024, 1408, dtype=BF16),
            pltpu.SemaphoreType.DMA((3, CHUNKS)),
        ],
    )


def run_sum_attend(info, keep, other, mixer_total):
    return call(
        sum_attend,
        "sum_attend",
        info,
        (keep.reshape(1024, 512), other.reshape(1024, 512), mixer_total),
        [ANY, ANY, pl.BlockSpec((16, 128), lambda i, *_: (0, 10))],
        struct(1024, 640, dtype=BF16),
        ANY,
        [
            scratch(1024, 512, dtype=BF16),
            scratch(1024, 512, dtype=BF16),
            scratch(1024, 640, dtype=BF16),
            pltpu.SemaphoreType.DMA((3, CHUNKS)),
        ],
    )


def run_sum_chips(info, terms, small):
    columns = terms.shape[2]
    outs = [struct(16, columns)] if not small else [struct(16, columns - 128), struct(512, 128)]
    return call(
        sum_chips,
        "sum_chips",
        info,
        (terms,),
        [ANY],
        outs,
        [whole(o.shape) for o in outs],
        [scratch(*terms.shape, dtype=BF16), pltpu.SemaphoreType.DMA((CHUNKS,))],
    )


def run_finish(info, *operands):
    shapes = [
        (3, 8, 256),
        (8, 256),
        (8, 2, 768),
        (8, 768),
        (2, WIDTH),
        (2, WIDTH),
        (2, WIDTH),
        (2, 768),
        (31, 768),
        (1, 768),
    ]
    scalars = pl.BlockSpec(memory_space=pltpu.SMEM)
    return call(
        finish,
        "finish",
        info,
        operands,
        [whole(a.shape) for a in operands],
        [struct(*s) for s in shapes] + [struct(4), struct(2)],
        [whole(s) for s in shapes] + [scalars, scalars],
    )


def run_place_pair(info, own, other):
    return call(
        place_pair,
        "place_pair",
        info,
        (own, other),
        [ANY, ANY],
        struct(UTTS, 2, SLOT, WIDTH),
        ANY,
        [
            scratch(UTTS, SLOT, WIDTH, dtype=BF16),
            scratch(UTTS, SLOT, WIDTH, dtype=BF16),
            scratch(2, UTTS, SLOT, WIDTH),
            pltpu.SemaphoreType.DMA((4, UTTS)),
        ],
    )


def swap(value, axis):
    return lax.ppermute(value, axis, [(0, 1), (1, 0)])


def along_x(block):
    return [block] + [
        lax.ppermute(block, "x", [(i, (i + s) % 4) for i in range(4)]) for s in SHIFTS[1:]
    ]


def with_partner(pieces):
    both = []
    for piece in pieces:
        both += [piece, swap(piece, "core")]
    return both


CHIPS = ("branch", "x", "z", "yh")


def exchange(blocks):
    return lax.all_to_all(blocks, CHIPS, 0, 0, tiled=True)


def shards(
    frames,
    attend_norm,
    attend_in,
    attend_out,
    position_slope,
    mixer_norm,
    mixer_in,
    gating_norm,
    kernel_taps,
    kernel_bias,
    mixer_out,
    merge_logits,
    final_norm,
    lengths,
    cotangent,
):
    branch = lax.axis_index("branch")
    core = lax.axis_index("core")
    own_lengths = lax.dynamic_slice_in_dim(lengths, branch, 1, 1)[:, 0]
    info = jnp.concatenate([jnp.stack([branch, core, lax.axis_index("x")]), own_lengths])
    merge_logits = merge_logits[None]
    local = run_pack(info, attend_in.transpose(1, 0, 2), attend_out, mixer_in, mixer_out)
    own = jnp.concatenate(
        [kernel_taps, kernel_bias[None], gating_norm, jnp.pad(position_slope, (0, 764))[None]]
    )
    other = swap(own, "branch")
    block = run_spread(info, local, swap(local, "core"))
    block, other = lax.optimization_barrier((block, other))
    plane = lax.all_to_all(block, ("branch", "z", "yh"), 0, 0, tiled=True).reshape(2, 128, 1664)
    attend_pieces = along_x(plane[:, :, 0:384])
    *attend_pieces, mixer_block = lax.optimization_barrier(
        (*attend_pieces, plane[:, :, 384:1664])
    )
    mixer_pieces = along_x(mixer_block)

    triple, context, log_total, attend_w, slopes = run_attend_forward(
        info, frames, attend_norm, own, other, with_partner(attend_pieces)
    )
    *mixer_pieces, context = lax.optimization_barrier((*mixer_pieces, context))
    layer, grad_mixed, grad_context, mixer_keep, mixer_send, small = run_mixer(
        info,
        frames,
        cotangent,
        context,
        mixer_norm,
        final_norm,
        merge_logits,
        own,
        other,
        with_partner(mixer_pieces),
    )
    mixer_other = swap(mixer_send, "core")
    small_other = swap(small, "core")
    layer_other = swap(layer, "branch")
    mixer_other, small_other, grad_context = lax.optimization_barrier(
        (mixer_other, small_other, grad_context)
    )
    mixer_terms = run_sum_mixer(info, mixer_keep, mixer_other, small, small_other)
    mixer_terms, grad_context, layer_other = lax.optimization_barrier(
        (mixer_terms, grad_context, layer_other)
    )
    mixer_terms = exchange(mixer_terms.reshape(64, 16, 1408))
    grads, attend_keep, attend_send = run_attend_backward(
        info,
        frames,
        grad_mixed,
        triple,
        log_total,
        grad_context,
        attend_norm,
        slopes,
        attend_w,
    )
    grads_other = swap(grads, "branch")
    mixer_total = run_sum_chips(info, mixer_terms, False)[0]
    attend_terms = run_sum_attend(info, attend_keep, swap(attend_send, "core"), mixer_total)
    attend_total, small = run_sum_chips(info, exchange(attend_terms.reshape(64, 16, 640)), True)
    (
        att_in,
        att_out,
        mix_in,
        mix_out,
        anorm,
        mnorm,
        fnorm,
        gnorm,
        taps,
        bias,
        slope,
        merge,
    ) = run_finish(
        info,
        merge_logits,
        mixer_total,
        swap(mixer_total, "core"),
        attend_total,
        swap(attend_total, "core"),
        small,
    )
    return (
        run_place_pair(info, layer, layer_other),
        run_place_pair(info, grads, grads_other),
        anorm,
        att_in.transpose(1, 0, 2),
        att_out,
        slope,
        mnorm,
        mix_in,
        gnorm,
        taps,
        bias[0],
        mix_out,
        merge,
        fnorm,
    )


def solution(mesh):
    fine = Mesh(mesh.devices.reshape(2, 4, 4, 2, 2), ("branch", "x", "z", "yh", "core"))
    dp = ("x", "z", "yh", "core")
    placed = (
        P(None, dp, None, None),
        P(),
        P(dp, None, "branch"),
        P(dp, "branch"),
        P("branch"),
        P(),
        P(dp, None, "branch"),
        P(None, "branch"),
        P(None, "branch"),
        P("branch"),
        P(dp, "branch"),
        P(),
        P(),
        P(None, dp),
        P(None, dp, None, None),
    )
    return jax.shard_map(
        shards,
        mesh=fine,
        in_specs=placed,
        out_specs=(
            P(None, dp, None, None),
            P(None, dp, None, None),
            P(),
            P(dp, None, "branch"),
            P(dp, "branch"),
            P("branch"),
            P(),
            P(dp, None, "branch"),
            P(None, "branch"),
            P(None, "branch"),
            P("branch"),
            P(dp, "branch"),
            P(),
            P(),
        ),
        check_vma=False,
    )
```

```python
from functools import partial

import jax
import jax.numpy as jnp
import numpy as np
from jax import lax
from jax.experimental import pallas as pl
from jax.experimental.pallas import tpu as pltpu
from jax.sharding import Mesh
from jax.sharding import PartitionSpec as P

EPSILON = 1e-05
NEGATIVE = -1e30
F32 = jnp.float32
BF16 = jnp.bfloat16
SLOT = 256
WIDTH = 512
HEADS = 8
HEAD = 64
HALF = 1536
TAPS = 31
REACH = 15
UTTS = 3
ROWS = UTTS * SLOT
PERIOD = SLOT + REACH
BINS = (PERIOD + 1) // 2
SPEC = 2 * BINS
BLOCK = 256
BLOCKS = HALF // BLOCK
PER_BRANCH = 768 // BLOCK
GELU_A = 0.7978845608028654
GELU_B = GELU_A * 0.044715
HEAD_UNROLL = 8
VMEM_LIMIT = 64 * 1024 * 1024 - 65536


def three_terms(table):
    high = np.asarray(table.astype(BF16)).astype(np.float64)
    return np.concatenate([high, high, table - high], 1)


def transform_tables():
    bins = np.arange(BINS)[:, None]
    angle = 2 * np.pi * bins * np.arange(SLOT)[None, :] / PERIOD
    lag_angle = 2 * np.pi * bins * (np.arange(TAPS) - REACH)[None, :] / PERIOD
    weight = np.where(bins == 0, 1.0, 2.0) / PERIOD
    forward = np.concatenate([np.cos(angle), -np.sin(angle)], 0)
    inverse = np.concatenate([np.cos(angle) * weight, -np.sin(angle) * weight], 0).T
    tap_forward = np.concatenate([np.cos(lag_angle), -np.sin(lag_angle)], 0)
    tap_inverse = np.concatenate([np.cos(lag_angle) * weight, -np.sin(lag_angle) * weight], 0).T
    tap_forward = three_terms(np.pad(tap_forward, ((0, 0), (0, 1))))
    tap_inverse = np.pad(tap_inverse, ((0, 1), (0, 0)))
    return three_terms(forward), inverse, three_terms(inverse), tap_forward, tap_inverse


def dot_nn(a, b):
    return lax.dot_general(a, b, (((1,), (0,)), ((), ())), preferred_element_type=F32)


def dot_nt(a, b):
    return lax.dot_general(a, b, (((1,), (1,)), ((), ())), preferred_element_type=F32)


def dot_tn(a, b):
    return lax.dot_general(a, b, (((0,), (0,)), ((), ())), preferred_element_type=F32)


def dot_tt(a, b):
    return lax.dot_general(a, b, (((0,), (1,)), ((), ())), preferred_element_type=F32)


def standardize(rows_in):
    average = jnp.mean(rows_in, axis=-1, keepdims=True)
    centered = rows_in - average
    variance = jnp.mean(centered * centered, axis=-1, keepdims=True)
    rstd = lax.rsqrt(variance + EPSILON)
    return centered * rstd, rstd


def gelu_pair(v):
    square = v * v
    half = 0.5 + 0.5 * jnp.tanh(v * (GELU_A + GELU_B * square))
    active = v * half
    slope = half + active * (1.0 - half) * (2 * GELU_A + 6 * GELU_B * square)
    return active, slope


def merge_mix(merge_logits):
    exponent = jnp.exp(merge_logits[...] - jnp.max(merge_logits[...], axis=1, keepdims=True))
    mixing = exponent / jnp.sum(exponent, axis=1, keepdims=True)
    return mixing[:, 0:1], mixing[:, 1:2]


INFO_BRANCH, INFO_CORE, INFO_X, INFO_Y, INFO_Z, INFO_LENGTH = 0, 1, 2, 3, 4, 5
SHIFTS = (0, 1, 3, 2)


def piece_copies(info, pieces, target, sems, along="x"):
    core = info[INFO_CORE]
    columns_in = pieces[0].shape[3]
    copies = []
    for i, piece in enumerate(pieces):
        at = lax.rem(info[INFO_X if along == "x" else INFO_Z] + (4 - SHIFTS[i // 2]), 4)
        side = core if i % 2 == 0 else 1 - core
        columns = pl.ds(pl.multiple_of(side * columns_in, 128), columns_in)
        for b in range(2):
            if along == "x":
                goal = target.at[b, at, :, :, columns]
            else:
                goal = target.at[b, :, at, :, columns]
            copies.append(pltpu.make_async_copy(piece.at[b], goal, sems.at[2 * i + b]))
    return copies


def weight(weights, b, first, last):
    return weights[b, :, :, :, first:last].reshape(WIDTH, last - first)


def pack_local(info, slopes, att_in, att_out, mix_in, mix_out, taps, bias, gnorm, out, own):
    for i in range(3):
        out[:, i * 256 : (i + 1) * 256] = att_in[i]
    for i in range(2):
        out[:, 768 + i * 768 : 768 + (i + 1) * 768] = mix_in[:, i, :]
    out[:, 2304:3072] = mix_out[...]
    out[:, 3072:3328] = att_out[...]
    own[0:31, :] = taps[...]
    own[31, :] = bias[...]
    own[32:34, :] = gnorm[...]
    lane = lax.broadcasted_iota(jnp.int32, (1, 768), 1)
    row = jnp.zeros((1, 768), F32)
    for r in range(4):
        row = jnp.where(lane == r, slopes[r], row)
    own[34:35, :] = row


def pair_rows(info, local, other, out):
    core = info[INFO_CORE]
    mine, theirs = local[...].astype(F32), other[...].astype(F32)
    rows = jnp.concatenate(
        [jnp.where(core == 0, mine, theirs), jnp.where(core == 0, theirs, mine)], axis=0
    )
    out[:, 0:384] = jnp.where(core == 0, rows[:, 0:384], rows[:, 384:768]).astype(BF16)
    out[:, 384:1664] = jnp.where(core == 0, rows[:, 768:2048], rows[:, 2048:3328]).astype(BF16)


def join_y(info, *rest):
    pieces, (first, second) = rest[:4], rest[4:]
    for piece, s in zip(pieces, SHIFTS):
        y = lax.rem(info[INFO_Y] + (4 - s), 4)
        at = lax.rem(y, 2) * 2 + y // 2
        first[at] = piece[:, 0:384]
        second[at] = piece[:, 384:1664]


def join_planes(info, *rest):
    over_z, over_x, (attend, mixer) = rest[:4], rest[4:8], rest[8:]
    for i, s in enumerate(SHIFTS):
        z = lax.rem(info[INFO_Z] + (4 - s), 4)
        x = lax.rem(info[INFO_X] + (4 - s), 4)
        for b in range(2):
            here = slice(b * 2, b * 2 + 2)
            attend[b, pl.ds(z * 2, 2)] = over_z[i][here]
            mixer[b, pl.ds(x * 2, 2)] = over_x[i][here]


def fill_distance(distance):
    key_at = lax.broadcasted_iota(jnp.int32, (SLOT, SLOT), 0)
    query_at = lax.broadcasted_iota(jnp.int32, (SLOT, SLOT), 1)
    offset = (key_at - query_at).astype(F32)
    distance[...] = jnp.sqrt(offset * offset + 1.0)


def attend_forward(
    info,
    frames,
    norm,
    own,
    other,
    *rest,
):
    pieces, (triple, context, log_total, weights, slopes, bias_s, sems) = rest[:8], rest[8:]
    step = pl.program_id(0)
    copies = piece_copies(info, pieces, weights, sems)

    @pl.when(step == 0)
    def _():
        for copy in copies:
            copy.start()
        branch = info[INFO_BRANCH]
        key_at = lax.broadcasted_iota(jnp.int32, (SLOT, SLOT), 0)
        query_at = lax.broadcasted_iota(jnp.int32, (SLOT, SLOT), 1)
        offset = (key_at - query_at).astype(F32)
        distance = jnp.sqrt(offset * offset + 1.0)
        for h in range(HEADS):
            lane = slice(h % 4, h % 4 + 1)
            slope = jnp.where(branch == h // 4, own[34:35, lane], other[34:35, lane])
            slopes[h : h + 1, :] = jnp.broadcast_to(slope, (1, 128))
            bias_s[h] = slope * distance
        for copy in copies:
            copy.wait()

    normed, _ = standardize(frames[0, 0])
    low = (normed * norm[0:1] + norm[1:2]).astype(BF16)
    for b in range(2):
        part = dot_tt(weight(weights, b, 0, 256), low) * (HEAD**-0.5)
        triple[0, b * 768 : b * 768 + 256, :] = part.astype(BF16)
        part = dot_tt(weight(weights, b, 256, 768), low)
        triple[0, b * 768 + 256 : (b + 1) * 768, :] = part.astype(BF16)
    is_key = lax.broadcasted_iota(jnp.int32, (SLOT, SLOT), 0) < info[INFO_LENGTH + step]

    def head(h, carry):
        base = pl.multiple_of((h // 4) * 768 + (h % 4) * HEAD, HEAD)
        q = triple[0, pl.ds(base, HEAD), :]
        k = triple[0, pl.ds(base + 256, HEAD), :]
        v = triple[0, pl.ds(base + 512, HEAD), :]
        logits = jnp.where(is_key, dot_tn(k, q) - bias_s[h], NEGATIVE)
        highest = jnp.max(logits, axis=0, keepdims=True)
        exponent = jnp.exp(logits - highest)
        total = jnp.sum(exponent, axis=0, keepdims=True)
        prob = (exponent * (1.0 / total)).astype(BF16)
        context[0, pl.ds(pl.multiple_of(h * HEAD, HEAD), HEAD), :] = dot_nn(v, prob).astype(BF16)
        log_total[0, pl.ds(h, 1), :] = highest + jnp.log(total)
        return carry

    lax.fori_loop(0, HEADS, head, 0, unroll=HEAD_UNROLL)


def mixer_both(
    info,
    frames,
    cotangent,
    context,
    mixer_norm,
    final_norm,
    merge_logits,
    own,
    other,
    forward,
    inverse,
    inverse_three,
    tap_forward,
    tap_inverse,
    *rest,
):
    pieces, rest = rest[:8], rest[8:]
    (
        layer,
        grad_frames,
        grad_context,
        keep,
        send,
        small,
        weights,
        params_s,
        small_wide,
        small_narrow,
        tap_spec,
        second_s,
        second_slope,
        first_s,
        first_slope,
        conv_s,
        spec_s,
        cross_s,
        back_s,
        gated_s,
        hidden_s,
        low_s,
        grad_s,
        attend_s,
        context_s,
        grads_s,
        sems,
    ) = rest
    step = pl.program_id(0)
    branch, core = info[INFO_BRANCH], info[INFO_CORE]
    here = pl.ds(pl.multiple_of(step * SLOT, SLOT), SLOT)
    copies = piece_copies(info, pieces, weights, sems, "z")

    @pl.when(step == 0)
    def _():
        for copy in copies:
            copy.start()
        params_s[branch] = own[...]
        params_s[1 - branch] = other[...]
        for b in range(2):
            tap_spec[:, b * 768 : (b + 1) * 768] = dot_nn(
                tap_forward[...], stack_terms(params_s[b, 0:32, :])
            )
        cross_s[...] = jnp.zeros_like(cross_s)
        small_wide[...] = jnp.zeros_like(small_wide)
        small_narrow[...] = jnp.zeros_like(small_narrow)
        for copy in copies:
            copy.wait()

    mix_attend, mix_mixer = merge_mix(merge_logits)
    rows_in = frames[0, 0]
    normed, rstd = standardize(rows_in)
    low = (normed * mixer_norm[0:1] + mixer_norm[1:2]).astype(BF16)
    low_s[here, :] = low
    length = info[INFO_LENGTH + step]
    valid = (lax.broadcasted_iota(jnp.int32, (SLOT, 1), 0) < length).astype(F32)

    places = [
        (k // PER_BRANCH, slice((k % PER_BRANCH) * BLOCK, (k % PER_BRANCH + 1) * BLOCK),
         slice(k * BLOCK, (k + 1) * BLOCK))
        for k in range(BLOCKS)
    ]

    def part(b, kind, off):
        return weight(weights, b, kind * 768 + off.start, kind * 768 + off.stop)

    def fold(v):
        return v[:, 0:128] + v[:, 128:256]

    def lane_sum(v):
        return jnp.sum(v, axis=-1, keepdims=True)

    total = jnp.zeros((SLOT, 128), F32)
    for b, off, wide in places:
        active, slope = gelu_pair(dot_nn(low, part(b, 1, off)))
        second_s[:, wide] = active
        second_slope[:, wide] = slope
        total += fold(active)
    average = lane_sum(total) / HALF
    total = jnp.zeros((SLOT, 128), F32)
    for b, off, wide in places:
        centered = second_s[:, wide] - average
        total += fold(centered * centered)
    gate_rstd = lax.rsqrt(lane_sum(total) / HALF + EPSILON)

    for b, off, wide in places:
        standard = (second_s[:, wide] - average) * gate_rstd
        gate_in = (standard * params_s[b, 32:33, off] + params_s[b, 33:34, off]) * valid
        spec = dot_nn(forward[...], stack_terms(gate_in))
        spec_s[:, wide] = spec
        real, imag = spec[0:BINS], spec[BINS:SPEC]
        tap_real, tap_imag = tap_spec[0:BINS, wide], tap_spec[BINS:SPEC, wide]
        product = jnp.concatenate(
            [real * tap_real + imag * tap_imag, imag * tap_real - real * tap_imag], axis=0
        )
        conved = dot_nn(inverse_three[...], stack_terms(product)) + params_s[b, 31:32, off]
        conv_s[:, wide] = conved
        active, slope = gelu_pair(dot_nn(low, part(b, 0, off)))
        first_s[:, wide] = active
        first_slope[:, wide] = slope
        gated_s[here, wide] = (active * conved).astype(BF16)

    mixer_part = dot_nt(gated_s[here, 0:768], weight(weights, 0, 1536, 2304)) + dot_nt(
        gated_s[here, 768:1536], weight(weights, 1, 1536, 2304)
    )
    context_s[:, here] = context[0]
    attend_part = dot_tt(context[0, 0:256, :], weight(weights, 0, 2304, 2560)) + dot_tt(
        context[0, 256:512, :], weight(weights, 1, 2304, 2560)
    )
    merged = rows_in + mix_attend * attend_part + mix_mixer * mixer_part
    merged_normed, merged_rstd = standardize(merged)
    layer[0] = ((merged_normed * final_norm[0:1] + final_norm[1:2]) * valid).astype(BF16)
    grad_out = cotangent[0, 0] * valid
    scaled = grad_out * final_norm[0:1]
    grad_merged = merged_rstd * (
        scaled
        - jnp.mean(scaled, axis=-1, keepdims=True)
        - merged_normed * jnp.mean(scaled * merged_normed, axis=-1, keepdims=True)
    )
    small_narrow[0:1] += jnp.sum(grad_out * merged_normed, axis=0, keepdims=True)
    small_narrow[1:2] += jnp.sum(grad_out, axis=0, keepdims=True)
    small_narrow[2:3] += jnp.sum(grad_merged * attend_part, axis=0, keepdims=True)
    small_narrow[3:4] += jnp.sum(grad_merged * mixer_part, axis=0, keepdims=True)
    grad_mixer = (mix_mixer * grad_merged).astype(BF16)
    grad_s[here, :] = grad_mixer
    grad_attend = (mix_attend * grad_merged).astype(BF16)
    attend_s[here, :] = grad_attend
    for b in range(2):
        grad_context[0, b * 256 : (b + 1) * 256, :] = dot_tt(
            weight(weights, b, 2304, 2560), grad_attend
        ).astype(BF16)

    total, cross_total = jnp.zeros((SLOT, 128), F32), jnp.zeros((SLOT, 128), F32)
    for b, off, wide in places:
        grad_gated = dot_nn(grad_mixer, part(b, 2, off))
        grad_conved = grad_gated * first_s[:, wide]
        hidden_s[here, wide] = (first_slope[:, wide] * (grad_gated * conv_s[:, wide])).astype(BF16)
        small_wide[31:32, wide] += jnp.sum(grad_conved, axis=0, keepdims=True)
        grad_spec = dot_nn(forward[:, 0:SLOT], grad_conved.astype(BF16))
        grad_real, grad_imag = grad_spec[0:BINS], grad_spec[BINS:SPEC]
        real, imag = spec_s[0:BINS, wide], spec_s[BINS:SPEC, wide]
        cross_s[0:BINS, wide] += grad_real * real + grad_imag * imag
        cross_s[BINS:SPEC, wide] += grad_real * imag - grad_imag * real
        tap_real, tap_imag = tap_spec[0:BINS, wide], tap_spec[BINS:SPEC, wide]
        product = jnp.concatenate(
            [
                grad_real * tap_real - grad_imag * tap_imag,
                grad_real * tap_imag + grad_imag * tap_real,
            ],
            axis=0,
        )
        grad_gate = dot_nn(inverse[...], product.astype(BF16)) * valid
        standard = (second_s[:, wide] - average) * gate_rstd
        small_wide[32:33, wide] += jnp.sum(grad_gate * standard, axis=0, keepdims=True)
        small_wide[33:34, wide] += jnp.sum(grad_gate, axis=0, keepdims=True)
        grad_standard = grad_gate * params_s[b, 32:33, off]
        back_s[:, wide] = grad_standard
        total += fold(grad_standard)
        cross_total += fold(grad_standard * standard)
    back_average = lane_sum(total) / HALF
    back_scale = lane_sum(cross_total) / HALF

    for b, off, wide in places:
        standard = (second_s[:, wide] - average) * gate_rstd
        grad_second = gate_rstd * (back_s[:, wide] - back_average - standard * back_scale)
        hidden_s[here, HALF + wide.start : HALF + wide.stop] = (
            second_slope[:, wide] * grad_second
        ).astype(BF16)
    grad_low = (
        dot_nt(hidden_s[here, 0:768], weight(weights, 0, 0, 768))
        + dot_nt(hidden_s[here, 768:1536], weight(weights, 1, 0, 768))
    ) + (
        dot_nt(hidden_s[here, 1536:2304], weight(weights, 0, 768, 1536))
        + dot_nt(hidden_s[here, 2304:3072], weight(weights, 1, 768, 1536))
    )
    small_narrow[4:5] += jnp.sum(grad_low * normed, axis=0, keepdims=True)
    small_narrow[5:6] += jnp.sum(grad_low, axis=0, keepdims=True)
    scaled = grad_low * mixer_norm[0:1]
    grad_frames[0] = grad_merged + rstd * (
        scaled
        - jnp.mean(scaled, axis=-1, keepdims=True)
        - normed * jnp.mean(scaled * normed, axis=-1, keepdims=True)
    )

    @pl.when(step == UTTS - 1)
    def _():
        outs = []
        for b in range(2):
            first, second = b * 768, HALF + b * 768
            pairs = [
                (dot_tn(low_s[...], hidden_s[:, first : first + 256]),
                 dot_tn(low_s[...], hidden_s[:, second + 512 : second + 768])),
                (dot_tn(low_s[...], hidden_s[:, first + 256 : first + 512]),
                 dot_tn(grad_s[...], gated_s[:, first : first + 256])),
                (dot_tn(low_s[...], hidden_s[:, first + 512 : first + 768]),
                 dot_tn(grad_s[...], gated_s[:, first + 256 : first + 512])),
                (dot_tn(low_s[...], hidden_s[:, second : second + 256]),
                 dot_tn(grad_s[...], gated_s[:, first + 512 : first + 768])),
                (dot_tn(low_s[...], hidden_s[:, second + 256 : second + 512]),
                 dot_tt(attend_s[...], context_s[b * 256 : (b + 1) * 256, :])),
            ]
            for i, (upper, lower) in enumerate(pairs):
                upper, lower = upper.reshape(32, 2, 8, 256), lower.reshape(32, 2, 8, 256)
                for p in range(2):
                    grads_s[p, b * 32 : (b + 1) * 32, :, i * 256 : (i + 1) * 256] = (
                        jnp.concatenate([upper[:, p], lower[:, p]], axis=1).astype(BF16)
                    )
            chips = pl.ds(b * 32, 32)
            outs += start_all(
                [
                    pltpu.make_async_copy(
                        grads_s.at[core, chips], keep.at[chips], sems.at[2 * b]
                    ),
                    pltpu.make_async_copy(
                        grads_s.at[1 - core, chips], send.at[chips], sems.at[2 * b + 1]
                    ),
                ]
            )
        tap_grad = dot_nn(tap_inverse[...], cross_s[...].astype(BF16))
        small_wide[0:31, :] = tap_grad[0:31]
        for g in range(12):
            small[g * 40 : (g + 1) * 40, :] = small_wide[:, g * 128 : (g + 1) * 128]
        for j in range(4):
            small[480 + 8 * j : 488 + 8 * j, :] = small_narrow[:, j * 128 : (j + 1) * 128]
        for copy in outs:
            copy.wait()


def attend_backward(
    info,
    frames,
    grad_mixed,
    triple,
    log_total,
    grad_context,
    norm,
    slopes,
    weights,
    frames_grad,
    keep,
    send,
    distance,
    low_s,
    triple_t,
    small,
    terms,
    sems,
):
    step = pl.program_id(0)
    here = pl.ds(pl.multiple_of(step * SLOT, SLOT), SLOT)

    @pl.when(step == 0)
    def _():
        fill_distance(distance)
        small[...] = jnp.zeros_like(small)

    normed, rstd = standardize(frames[0, 0])
    low_s[here, :] = (normed * norm[0:1] + norm[1:2]).astype(BF16)
    is_key = lax.broadcasted_iota(jnp.int32, (SLOT, SLOT), 0) < info[INFO_LENGTH + step]

    def head(h, carry):
        base = pl.multiple_of((h // 4) * 768 + (h % 4) * HEAD, HEAD)
        q = triple[0, pl.ds(base, HEAD), :]
        k = triple[0, pl.ds(base + 256, HEAD), :]
        v = triple[0, pl.ds(base + 512, HEAD), :]
        grad_here = grad_context[0, pl.ds(pl.multiple_of(h * HEAD, HEAD), HEAD), :]
        logits = dot_tn(k, q) - slopes[pl.ds(h, 1), 0:1] * distance[...]
        logits = jnp.where(is_key, logits, NEGATIVE)
        prob = jnp.exp(logits - log_total[0, pl.ds(h, 1), :])
        grad_prob = dot_tn(v, grad_here)
        row_dot = jnp.sum(prob * grad_prob, axis=0, keepdims=True)
        grad_logits = prob * (grad_prob - row_dot)
        slope_row = -jnp.sum(grad_logits * distance[...], axis=0, keepdims=True)
        small[pl.ds(8 + h, 1), :] += slope_row[:, 0:128] + slope_row[:, 128:256]
        grad_scores = grad_logits.astype(BF16)
        grad_q = dot_nn(k, grad_scores) * (HEAD**-0.5)
        grad_k = dot_nt(q, grad_scores)
        grad_v = dot_nt(grad_here, prob.astype(BF16))
        triple_t[pl.ds(base, HEAD), here] = grad_q.astype(BF16)
        triple_t[pl.ds(base + 256, HEAD), here] = grad_k.astype(BF16)
        triple_t[pl.ds(base + 512, HEAD), here] = grad_v.astype(BF16)
        return carry

    lax.fori_loop(0, HEADS, head, 0, unroll=HEAD_UNROLL)
    grad_low = dot_tt(triple_t[0:768, here], weight(weights, 0, 0, 768)) + dot_tt(
        triple_t[768:1536, here], weight(weights, 1, 0, 768)
    )
    gain_row = jnp.sum(grad_low * normed, axis=0, keepdims=True)
    bias_row = jnp.sum(grad_low, axis=0, keepdims=True)
    for j in range(4):
        small[j : j + 1, :] += gain_row[:, j * 128 : (j + 1) * 128]
        small[4 + j : 5 + j, :] += bias_row[:, j * 128 : (j + 1) * 128]
    scaled = grad_low * norm[0:1]
    frames_grad[0] = (
        grad_mixed[0]
        + rstd
        * (
            scaled
            - jnp.mean(scaled, axis=-1, keepdims=True)
            - normed * jnp.mean(scaled * normed, axis=-1, keepdims=True)
        )
    ).astype(BF16)

    @pl.when(step == UTTS - 1)
    def _():
        high, low = split_low(jnp.sum(small[8:16, :], axis=1, keepdims=True))
        block = jnp.concatenate([small[0:8, :], slope_rows(high, low)], axis=0).astype(BF16)
        for b in range(2):
            grads = dot_tt(low_s[...], triple_t[b * 768 : (b + 1) * 768, :]).reshape(32, 2, 8, 768)
            for p in range(2):
                terms[p, b * 32 : (b + 1) * 32, :, 0:384] = jnp.concatenate(
                    [grads[:, p, :, 0:384], grads[:, p, :, 384:768]], axis=1
                ).astype(BF16)
                for m in range(32):
                    terms[p, b * 32 + m, :, 384:512] = block
        core = info[INFO_CORE]
        outs = start_all(
            [
                pltpu.make_async_copy(terms.at[core], keep, sems.at[0]),
                pltpu.make_async_copy(terms.at[1 - core], send, sems.at[1]),
            ]
        )
        for copy in outs:
            copy.wait()


def stack_terms(value):
    high, low = split_low(value)
    return jnp.concatenate([high, low, high], axis=0).astype(BF16)


def slope_rows(high, low):
    lane = lax.broadcasted_iota(jnp.int32, (8, 128), 1)
    return jnp.where(lane == 0, high, jnp.where(lane == 1, low, 0.0))


def split_low(value):
    high = value.astype(BF16).astype(F32)
    return high, value - high


def start_all(copies):
    for copy in copies:
        copy.start()
    return copies


def chunk_copies(source, target, count, sems):
    size = target.shape[0] // count
    return start_all(
        [
            pltpu.make_async_copy(
                source.at[pl.ds(i * size, size)], target.at[pl.ds(i * size, size)], sems.at[i]
            )
            for i in range(count)
        ]
    )


CHUNKS = 8


def sum_pairs(info, keep, other, pieces, keep_s, other_s, out_s, sems):
    loads = []
    for i, s in enumerate(SHIFTS):
        x = lax.rem(info[INFO_X] + s, 4)
        for b in range(2):
            chips = pl.ds(b * 32 + x * 8, 8)
            here = pl.ds(b * 8, 8)
            loads.append(
                start_all(
                    [
                        pltpu.make_async_copy(
                            source.at[chips], target.at[i, here], sems.at[p, 2 * i + b]
                        )
                        for p, (source, target) in enumerate(((keep, keep_s), (other, other_s)))
                    ]
                )
            )
    stores = []
    columns = keep.shape[2]
    for i in (1, 2, 3, 0):
        for b in range(2):
            for copy in loads[2 * i + b]:
                copy.wait()
            here = slice(b * 8, b * 8 + 8)
            out_s[i, here, :, 0:columns] = (
                keep_s[i, here].astype(F32) + other_s[i, here].astype(F32)
            ).astype(BF16)
        yield i
        stores.append(pltpu.make_async_copy(out_s.at[i], pieces[i], sems.at[2, i]))
        stores[-1].start()
    for copy in stores:
        copy.wait()


def spread_small(small, small_other, out):
    high, low = split_low(small[...] + small_other[...])
    for j in range(16):
        for x in range(4):
            chip = (j // 8 * 4 + x) * 8 + j % 8
            rows = slice(8 * chip, 8 * chip + 8)
            out[j, 16 * x : 16 * x + 16, :] = jnp.concatenate(
                [high[rows], low[rows]], axis=0
            ).astype(BF16)


def sum_mixer(info, keep, other, small, small_other, *rest):
    pieces, (small_out, keep_s, other_s, out_s, sems) = rest[:4], rest[4:]
    sums = sum_pairs(info, keep, other, pieces, keep_s, other_s, out_s, sems)
    next(sums)
    spread_small(small, small_other, small_out)
    for _ in sums:
        pass


def sum_attend(info, keep, other, small_terms, *rest):
    pieces, (keep_s, other_s, out_s, sems) = rest[:4], rest[4:]
    total = (small_terms[0].astype(F32) + small_terms[1].astype(F32)) + (
        small_terms[2].astype(F32) + small_terms[3].astype(F32)
    )
    for i in range(4, 16):
        total += small_terms[i].astype(F32)
    chunks = []
    for x in range(4):
        high, low = split_low(total[16 * x : 16 * x + 8] + total[16 * x + 8 : 16 * x + 16])
        chunks.append(jnp.concatenate([high, low], axis=0))
    chunks = jnp.concatenate(chunks, axis=1).astype(BF16)
    for i in sum_pairs(info, keep, other, pieces, keep_s, other_s, out_s, sems):
        total = keep_s[i, 0, :, 384:512].astype(F32) + other_s[i, 0, :, 384:512].astype(F32)
        high, low = split_low(total[8:16, 0:1] + total[8:16, 1:2])
        block = jnp.concatenate([total[0:8], slope_rows(high, low)], axis=0).astype(BF16)
        for j in range(16):
            out_s[i, j, :, 384:512] = block
        out_s[i, 16] = chunks


def sum_four(info, *rest):
    terms, (out, terms_s, sems) = rest[:4], rest[4:]
    loads = [
        start_all(
            [
                pltpu.make_async_copy(
                    terms[i].at[pl.ds(c * 4, 4)], terms_s.at[i, pl.ds(c * 4, 4)], sems.at[i, c]
                )
                for i in range(4)
            ]
        )
        for c in range(4)
    ]
    for c in range(4):
        for copy in loads[c]:
            copy.wait()
        here = slice(c * 4, c * 4 + 4)
        total = (terms_s[0, here].astype(F32) + terms_s[1, here].astype(F32)) + (
            terms_s[2, here].astype(F32) + terms_s[3, here].astype(F32)
        )
        out[here] = total.astype(BF16)


def join_terms(info, mixer, *rest):
    terms, out = rest[0:4], rest[4]
    for j in range(16):
        out[j, :, 0:1280] = mixer[j]
        total = (terms[0][j].astype(F32) + terms[1][j].astype(F32)) + (
            terms[2][j].astype(F32) + terms[3][j].astype(F32)
        )
        out[j, :, 1280:1664] = total[:, 0:384].astype(BF16)
        if j == 0:
            little = total[:, 384:512]
            high, low = split_low(little[8:16, 0:1] + little[8:16, 1:2])
            block = jnp.concatenate([little[0:8], slope_rows(high, low)], axis=0).astype(BF16)
        out[j, :, 1664:1792] = block
    total = (terms[0][16].astype(F32) + terms[1][16].astype(F32)) + (
        terms[2][16].astype(F32) + terms[3][16].astype(F32)
    )
    high, low = split_low(total[0:8] + total[8:16])
    chunks = jnp.concatenate([high, low], axis=0).astype(BF16)
    for j in range(16):
        out[j, :, 1792:2304] = chunks


def finish(
    info,
    merge_logits,
    terms,
    att_in,
    att_out,
    mix_in,
    mix_out,
    anorm,
    mnorm,
    fnorm,
    gnorm,
    taps,
    bias,
    slope,
    merge,
    terms_s,
    small,
    sems,
):
    branch = info[INFO_BRANCH]
    copies = chunk_copies(terms, terms_s, CHUNKS, sems)
    total = jnp.zeros((16, 1792), F32)
    for c in range(CHUNKS):
        copies[c].wait()
        for i in range(c * 2, c * 2 + 2):
            total += terms_s[i, :, 0:1792].astype(F32)
            for x in range(4):
                pair = terms_s[i, :, 1792 + x * 128 : 1920 + x * 128].astype(F32)
                chip = (i // 8 * 4 + x) * 8 + i % 8
                small[8 * chip : 8 * chip + 8, :] = pair[0:8] + pair[8:16]
    upper, lower = total[0:8], total[8:16]
    mix_in[:, 0, :] = upper[:, 0:768]
    mix_in[:, 1, :] = jnp.concatenate([upper[:, 768:1280], lower[:, 0:256]], axis=1)
    mix_out[...] = lower[:, 256:1024]
    att_out[...] = lower[:, 1024:1280]
    total = total[:, 1280:1792]
    for g in range(6):
        group = small[pl.ds(pl.multiple_of((branch * 6 + g) * 40, 8), 40), :]
        columns = slice(g * 128, (g + 1) * 128)
        taps[:, columns] = group[0:31]
        bias[columns] = group[31]
        gnorm[:, columns] = group[32:34]
    attend_sum, mixer_sum = 0.0, 0.0
    for j in range(4):
        columns = slice(j * 128, (j + 1) * 128)
        group = small[480 + 8 * j : 488 + 8 * j, :]
        fnorm[:, columns] = group[0:2]
        mnorm[:, columns] = group[4:6]
        attend_sum += jnp.sum(group[2:3], axis=1, keepdims=True)
        mixer_sum += jnp.sum(group[3:4], axis=1, keepdims=True)
    mix_attend, mix_mixer = merge_mix(merge_logits)
    average = mix_attend * attend_sum + mix_mixer * mixer_sum
    merge[0] = jnp.sum(mix_attend * (attend_sum - average))
    merge[1] = jnp.sum(mix_mixer * (mixer_sum - average))
    att_in[0] = total[0:8, 0:256]
    att_in[1] = jnp.concatenate([total[0:8, 256:384], total[8:16, 0:128]], axis=1)
    att_in[2] = total[8:16, 128:384]
    for p in range(2):
        for j in range(4):
            r = p * 4 + j
            anorm[p : p + 1, j * 128 : (j + 1) * 128] = total[r : r + 1, 384:512]
    slopes = total[8:16, 384:385] + total[8:16, 385:386]
    for r in range(4):
        slope[r] = jnp.where(
            branch == 0, jnp.sum(slopes[r : r + 1]), jnp.sum(slopes[4 + r : 5 + r])
        )


def place_pair(info, own, other, out, own_s, other_s, out_s, sems):
    branch = info[INFO_BRANCH]
    loads = [
        start_all(
            [
                pltpu.make_async_copy(source.at[u], target.at[u], sems.at[p, u])
                for u in range(UTTS)
            ]
        )
        for p, (source, target) in enumerate(((own, own_s), (other, other_s)))
    ]
    stores = []
    for u in range(UTTS):
        for p, source in enumerate((own_s, other_s)):
            loads[p][u].wait()
            out_s[p, u] = source[u].astype(F32)
            at = branch if p == 0 else 1 - branch
            stores.append(
                pltpu.make_async_copy(out_s.at[p, u], out.at[u, at], sems.at[2 + p, u])
            )
            stores[-1].start()
    for copy in stores:
        copy.wait()


def whole(shape):
    return pl.BlockSpec(shape, lambda i, *_: (0,) * len(shape), pipeline_mode=pl.Buffered(1))


def per_utt(shape):
    return pl.BlockSpec((1,) + shape, lambda i, *_: (i,) + (0,) * len(shape))


ANY = pl.BlockSpec(memory_space=pl.ANY)
OWN_FRAMES = pl.BlockSpec((1, 1, SLOT, WIDTH), lambda i, info, *_: (i, info[0], 0, 0))


def scratch(*shape, dtype=F32):
    return pltpu.VMEM(shape, dtype)


def struct(*shape, dtype=F32):
    return jax.ShapeDtypeStruct(shape, dtype)


def call(kernel, name, info, operands, in_specs, outs, out_specs, scratches=(), grid=1, us=2, **extra):
    return pl.pallas_call(
        kernel,
        grid_spec=pltpu.PrefetchScalarGridSpec(
            num_scalar_prefetch=1,
            grid=(grid,),
            in_specs=in_specs,
            out_specs=out_specs,
            scratch_shapes=scratches,
        ),
        out_shape=outs,
        compiler_params=pltpu.CompilerParams(
            dimension_semantics=("arbitrary",), vmem_limit_bytes=VMEM_LIMIT
        ),
        cost_estimate=pl.CostEstimate(
            flops=us * 100000000, bytes_accessed=1 << 16, transcendentals=0
        ),
        name=name,
        **extra,
    )(info, *operands)


def run_pack(info, slopes, *operands):
    return call(
        pack_local,
        "pack_local",
        info,
        (slopes, *operands),
        [pl.BlockSpec(memory_space=pltpu.SMEM)] + [whole(a.shape) for a in operands],
        [struct(8, 3328, dtype=BF16), struct(35, 768)],
        [whole((8, 3328)), whole((35, 768))],
    )


def run_pair(info, local, other):
    return call(
        pair_rows,
        "pair_rows",
        info,
        (local, other),
        [whole((8, 3328))] * 2,
        struct(16, 1664, dtype=BF16),
        whole((16, 1664)),
    )


def run_join_y(info, pieces):
    shapes = [(4, 16, 384), (4, 16, 1280)]
    return call(
        join_y,
        "join_y",
        info,
        pieces,
        [whole((16, 1664))] * 4,
        [struct(*s, dtype=BF16) for s in shapes],
        [whole(s) for s in shapes],
    )


def run_join_planes(info, over_z, over_x):
    shapes = [(2, 8, 16, 384), (2, 8, 16, 1280)]
    return call(
        join_planes,
        "join_planes",
        info,
        (*over_z, *over_x),
        [whole((4, 16, 384))] * 4 + [whole((4, 16, 1280))] * 4,
        [struct(*s, dtype=BF16) for s in shapes],
        [whole(s) for s in shapes],
    )


def run_attend_forward(info, frames, norm, own, other, pieces):
    return call(
        attend_forward,
        "attend_forward",
        info,
        (frames, norm, own, other, *pieces),
        [OWN_FRAMES, whole((2, WIDTH)), whole((35, 768)), whole((35, 768))] + [ANY] * 8,
        [
            struct(UTTS, HALF, SLOT, dtype=BF16),
            struct(UTTS, WIDTH, SLOT, dtype=BF16),
            struct(UTTS, HEADS, SLOT),
            struct(2, 4, 4, 32, 768, dtype=BF16),
            struct(HEADS, 128),
        ],
        [
            per_utt((HALF, SLOT)),
            per_utt((WIDTH, SLOT)),
            per_utt((HEADS, SLOT)),
            whole((2, 4, 4, 32, 768)),
            whole((HEADS, 128)),
        ],
        [scratch(HEADS, SLOT, SLOT), pltpu.SemaphoreType.DMA((16,))],
        grid=UTTS,
    )


def run_mixer(info, frames, cotangent, context, mnorm, fnorm, merge_logits, own, other, pieces):
    forward, inverse, inverse_three, tap_forward, tap_inverse = transform_tables()
    tables = (
        jnp.asarray(forward, BF16),
        jnp.asarray(inverse, BF16),
        jnp.asarray(inverse_three, BF16),
        jnp.asarray(tap_forward, BF16),
        jnp.asarray(tap_inverse, BF16),
    )
    return call(
        mixer_both,
        "mixer_both",
        info,
        (frames, cotangent, context, mnorm, fnorm, merge_logits, own, other, *tables, *pieces),
        [
            OWN_FRAMES,
            OWN_FRAMES,
            per_utt((WIDTH, SLOT)),
            whole((2, WIDTH)),
            whole((2, WIDTH)),
            whole((1, 2)),
            whole((35, 768)),
            whole((35, 768)),
            whole((SPEC, 3 * SLOT)),
            whole((SLOT, SPEC)),
            whole((SLOT, 3 * SPEC)),
            whole((SPEC, 96)),
            whole((32, SPEC)),
        ]
        + [ANY] * 8,
        [
            struct(UTTS, SLOT, WIDTH, dtype=BF16),
            struct(UTTS, SLOT, WIDTH),
            struct(UTTS, WIDTH, SLOT, dtype=BF16),
            struct(64, 16, 1280, dtype=BF16),
            struct(64, 16, 1280, dtype=BF16),
            struct(512, 128),
        ],
        [
            per_utt((SLOT, WIDTH)),
            per_utt((SLOT, WIDTH)),
            per_utt((WIDTH, SLOT)),
            ANY,
            ANY,
            whole((512, 128)),
        ],
        [
            scratch(2, 4, 4, 32, 2560, dtype=BF16),
            scratch(2, 35, 768),
            scratch(40, HALF),
            scratch(8, WIDTH),
            scratch(SPEC, HALF),
            scratch(SLOT, HALF),
            scratch(SLOT, HALF),
            scratch(SLOT, HALF),
            scratch(SLOT, HALF),
            scratch(SLOT, HALF),
            scratch(SPEC, HALF),
            scratch(SPEC, HALF),
            scratch(SLOT, HALF),
            scratch(ROWS, HALF, dtype=BF16),
            scratch(ROWS, 2 * HALF, dtype=BF16),
            scratch(ROWS, WIDTH, dtype=BF16),
            scratch(ROWS, WIDTH, dtype=BF16),
            scratch(ROWS, WIDTH, dtype=BF16),
            scratch(WIDTH, ROWS, dtype=BF16),
            scratch(2, 64, 16, 1280, dtype=BF16),
            pltpu.SemaphoreType.DMA((16,)),
        ],
        grid=UTTS,
    )


def run_attend_backward(
    info, frames, grad_mixed, triple, log_total, grad_context, norm, slopes, weights
):
    return call(
        attend_backward,
        "attend_backward",
        info,
        (frames, grad_mixed, triple, log_total, grad_context, norm, slopes, weights),
        [
            OWN_FRAMES,
            per_utt((SLOT, WIDTH)),
            per_utt((HALF, SLOT)),
            per_utt((HEADS, SLOT)),
            per_utt((WIDTH, SLOT)),
            whole((2, WIDTH)),
            whole((HEADS, 128)),
            whole((2, 4, 4, 32, 768)),
        ],
        [
            struct(UTTS, SLOT, WIDTH, dtype=BF16),
            struct(64, 16, 512, dtype=BF16),
            struct(64, 16, 512, dtype=BF16),
        ],
        [per_utt((SLOT, WIDTH)), ANY, ANY],
        [
            scratch(SLOT, SLOT),
            scratch(ROWS, WIDTH, dtype=BF16),
            scratch(HALF, ROWS, dtype=BF16),
            scratch(16, 128),
            scratch(2, 64, 16, 512, dtype=BF16),
            pltpu.SemaphoreType.DMA((2,)),
        ],
        grid=UTTS,
    )


def run_sum_mixer(info, keep, other, small, small_other):
    piece = (16, 16, 1280)
    return call(
        sum_mixer,
        "sum_mixer",
        info,
        (keep, other, small, small_other),
        [ANY, ANY, whole((512, 128)), whole((512, 128))],
        [struct(*piece, dtype=BF16)] * 4 + [struct(16, 64, 128, dtype=BF16)],
        [ANY] * 4 + [whole((16, 64, 128))],
        [scratch(4, *piece, dtype=BF16)] * 3 + [pltpu.SemaphoreType.DMA((3, 8))],
    )


def run_sum_attend(info, keep, other, small_terms):
    piece, wider = (16, 16, 512), (17, 16, 512)
    return call(
        sum_attend,
        "sum_attend",
        info,
        (keep, other, small_terms),
        [ANY, ANY, whole((16, 64, 128))],
        [struct(*wider, dtype=BF16)] * 4,
        [ANY] * 4,
        [scratch(4, *piece, dtype=BF16)] * 2
        + [scratch(4, *wider, dtype=BF16), pltpu.SemaphoreType.DMA((3, 8))],
    )


def run_sum_four(info, terms):
    piece = terms[0].shape
    return call(
        sum_four,
        "sum_four",
        info,
        terms,
        [ANY] * 4,
        struct(*piece, dtype=BF16),
        whole(piece),
        [scratch(4, *piece, dtype=BF16), pltpu.SemaphoreType.DMA((4, 4))],
    )


def run_join(info, mixer, terms):
    return call(
        join_terms,
        "join_terms",
        info,
        (mixer, *terms),
        [whole(mixer.shape)] + [whole(terms[0].shape)] * 4,
        struct(16, 16, 2304, dtype=BF16),
        whole((16, 16, 2304)),
    )


def run_finish(info, *operands):
    shapes = [
        (3, 8, 256),
        (8, 256),
        (8, 2, 768),
        (8, 768),
        (2, WIDTH),
        (2, WIDTH),
        (2, WIDTH),
        (2, 768),
        (31, 768),
        (768,),
    ]
    scalars = pl.BlockSpec(memory_space=pltpu.SMEM)
    return call(
        finish,
        "finish",
        info,
        operands,
        [whole(a.shape) for a in operands[:-1]] + [ANY],
        [struct(*s) for s in shapes] + [struct(4), struct(2)],
        [whole(s) for s in shapes] + [scalars, scalars],
        [
            scratch(*operands[-1].shape, dtype=BF16),
            scratch(512, 128),
            pltpu.SemaphoreType.DMA((CHUNKS,)),
        ],
    )


def run_place_pair(info, own, other):
    return call(
        place_pair,
        "place_pair",
        info,
        (own, other),
        [ANY, ANY],
        struct(UTTS, 2, SLOT, WIDTH),
        ANY,
        [
            scratch(UTTS, SLOT, WIDTH, dtype=BF16),
            scratch(UTTS, SLOT, WIDTH, dtype=BF16),
            scratch(2, UTTS, SLOT, WIDTH),
            pltpu.SemaphoreType.DMA((4, UTTS)),
        ],
    )


def swap(value, axis):
    return lax.ppermute(value, axis, [(0, 1), (1, 0)])


def move_x(block, distance):
    return lax.ppermute(block, "x", [(i, (i + distance) % 4) for i in range(4)])


def move_y(block, distance):
    def joint(y):
        return (y % 2) * 2 + y // 2

    return lax.ppermute(
        block, ("branch", "yh"), [(joint(y), joint((y + distance) % 4)) for y in range(4)]
    )


def move(block, axis, distance):
    return lax.ppermute(block, axis, [(i, (i + distance) % 4) for i in range(4)])


def along(block, axis):
    return [block] + [move(block, axis, s) for s in SHIFTS[1:]]


def with_partner(pieces):
    both = []
    for piece in pieces:
        both += [piece, swap(piece, "core")]
    return both


def exchange_x(pieces):
    return [pieces[0]] + [move(p, "x", s) for p, s in zip(pieces[1:], SHIFTS[1:])]


CHIPS = ("branch", "x", "z", "yh")
PLANE = ("branch", "z", "yh")


def exchange(blocks, axes):
    return lax.all_to_all(blocks, axes, 0, 0, tiled=True)


def shards(
    frames,
    attend_norm,
    attend_in,
    attend_out,
    position_slope,
    mixer_norm,
    mixer_in,
    gating_norm,
    kernel_taps,
    kernel_bias,
    mixer_out,
    merge_logits,
    final_norm,
    lengths,
    cotangent,
):
    branch = lax.axis_index("branch")
    core = lax.axis_index("core")
    own_lengths = lax.dynamic_slice_in_dim(lengths, branch, 1, 1)[:, 0]
    x, yh, z = (lax.axis_index(axis) for axis in ("x", "yh", "z"))
    info = jnp.concatenate([jnp.stack([branch, core, x, 2 * yh + branch, z]), own_lengths])
    merge_logits = merge_logits[None]
    local, own = run_pack(
        info,
        position_slope,
        attend_in.transpose(1, 0, 2),
        attend_out,
        mixer_in,
        mixer_out,
        kernel_taps,
        kernel_bias,
        gating_norm,
    )
    other = swap(own, "branch")
    block = run_pair(info, local, swap(local, "core"))
    first, second = run_join_y(info, [block] + [move_y(block, s) for s in SHIFTS[1:]])
    first, second, other = lax.optimization_barrier((first, second, other))
    attend_block, mixer_block = run_join_planes(info, along(first, "z"), along(second, "x"))
    attend_pieces = along(attend_block.reshape(2, 4, 32, 384), "x")
    mixer_pieces = along(mixer_block.reshape(2, 4, 32, 1280), "z")

    triple, context, log_total, attend_w, slopes = run_attend_forward(
        info, frames, attend_norm, own, other, with_partner(attend_pieces)
    )
    *mixer_pieces, context = lax.optimization_barrier((*mixer_pieces, context))
    layer, grad_mixed, grad_context, mixer_keep, mixer_send, small = run_mixer(
        info,
        frames,
        cotangent,
        context,
        mixer_norm,
        final_norm,
        merge_logits,
        own,
        other,
        with_partner(mixer_pieces),
    )
    small_other = swap(small, "core")
    mixer_other = swap(mixer_send, "core")
    layer_other = swap(layer, "branch")
    *mixer_sent, small_sent = run_sum_mixer(info, mixer_keep, mixer_other, small, small_other)
    mixer_terms = exchange_x(mixer_sent)
    small_sent, _, grad_context = lax.optimization_barrier(
        (small_sent, mixer_sent[0], grad_context)
    )
    grads, attend_keep, attend_send = run_attend_backward(
        info,
        frames,
        grad_mixed,
        triple,
        log_total,
        grad_context,
        attend_norm,
        slopes,
        attend_w,
    )
    small_sent, grads = lax.optimization_barrier((small_sent, grads))
    small_terms = exchange(small_sent, PLANE)
    grads, attend_keep, attend_send, layer_other, small_terms, *mixer_terms = (
        lax.optimization_barrier(
            (grads, attend_keep, attend_send, layer_other, small_terms, *mixer_terms)
        )
    )
    grads_other = swap(grads, "branch")
    attend_terms = exchange_x(
        run_sum_attend(info, attend_keep, swap(attend_send, "core"), small_terms)
    )
    mixer_total = run_sum_four(info, mixer_terms)
    layer_out = run_place_pair(info, layer, layer_other)
    *attend_terms, mixer_total, grads_other, layer_out = lax.optimization_barrier(
        (*attend_terms, mixer_total, grads_other, layer_out)
    )
    terms = exchange(run_join(info, mixer_total, attend_terms), PLANE)
    frames_out = run_place_pair(info, grads, grads_other)
    (
        att_in,
        att_out,
        mix_in,
        mix_out,
        anorm,
        mnorm,
        fnorm,
        gnorm,
        taps,
        bias,
        slope,
        merge,
    ) = run_finish(
        info,
        merge_logits,
        terms,
    )
    return (
        layer_out,
        frames_out,
        anorm,
        att_in.transpose(1, 0, 2),
        att_out,
        slope,
        mnorm,
        mix_in,
        gnorm,
        taps,
        bias,
        mix_out,
        merge,
        fnorm,
    )


def solution(mesh):
    fine = Mesh(mesh.devices.reshape(2, 4, 4, 2, 2), ("branch", "x", "z", "yh", "core"))
    dp = ("x", "z", "yh", "core")
    placed = (
        P(None, dp, None, None),
        P(),
        P(dp, None, "branch"),
        P(dp, "branch"),
        P("branch"),
        P(),
        P(dp, None, "branch"),
        P(None, "branch"),
        P(None, "branch"),
        P("branch"),
        P(dp, "branch"),
        P(),
        P(),
        P(None, dp),
        P(None, dp, None, None),
    )
    return jax.shard_map(
        shards,
        mesh=fine,
        in_specs=placed,
        out_specs=(
            P(None, dp, None, None),
            P(None, dp, None, None),
            P(),
            P(dp, None, "branch"),
            P(dp, "branch"),
            P("branch"),
            P(),
            P(dp, None, "branch"),
            P(None, "branch"),
            P(None, "branch"),
            P("branch"),
            P(dp, "branch"),
            P(),
            P(),
        ),
        check_vma=False,
    )
```

```python
from functools import partial

import jax
import jax.numpy as jnp
import numpy as np
from jax import lax
from jax.experimental import pallas as pl
from jax.experimental.pallas import tpu as pltpu
from jax.sharding import Mesh
from jax.sharding import PartitionSpec as P

EPSILON = 1e-05
NEGATIVE = -1e30
F32 = jnp.float32
BF16 = jnp.bfloat16
SLOT = 256
WIDTH = 512
HEADS = 8
HEAD = 64
HALF = 1536
TAPS = 31
REACH = 15
UTTS = 3
ROWS = UTTS * SLOT
PERIOD = SLOT + REACH
BINS = (PERIOD + 1) // 2
SPEC = 2 * BINS
BLOCK = 768
BLOCKS = HALF // BLOCK
PER_BRANCH = 768 // BLOCK
GELU_A = 0.7978845608028654
GELU_B = GELU_A * 0.044715
HEAD_UNROLL = 8
VMEM_LIMIT = 64 * 1024 * 1024 - 65536


def three_terms(table):
    high = np.asarray(table.astype(BF16)).astype(np.float64)
    return np.concatenate([high, high, table - high], 1)


def transform_tables():
    bins = np.arange(BINS)[:, None]
    angle = 2 * np.pi * bins * np.arange(SLOT)[None, :] / PERIOD
    lag_angle = 2 * np.pi * bins * (np.arange(TAPS) - REACH)[None, :] / PERIOD
    weight = np.where(bins == 0, 1.0, 2.0) / PERIOD
    forward = np.concatenate([np.cos(angle), -np.sin(angle)], 0)
    inverse = np.concatenate([np.cos(angle) * weight, -np.sin(angle) * weight], 0).T
    tap_forward = np.concatenate([np.cos(lag_angle), -np.sin(lag_angle)], 0)
    tap_inverse = np.concatenate([np.cos(lag_angle) * weight, -np.sin(lag_angle) * weight], 0).T
    tap_forward = three_terms(np.pad(tap_forward, ((0, 0), (0, 1))))
    tap_inverse = np.pad(tap_inverse, ((0, 1), (0, 0)))
    return three_terms(forward), inverse, three_terms(inverse), tap_forward, tap_inverse


def dot_nn(a, b):
    return lax.dot_general(a, b, (((1,), (0,)), ((), ())), preferred_element_type=F32)


def dot_nt(a, b):
    return lax.dot_general(a, b, (((1,), (1,)), ((), ())), preferred_element_type=F32)


def dot_tn(a, b):
    return lax.dot_general(a, b, (((0,), (0,)), ((), ())), preferred_element_type=F32)


def dot_tt(a, b):
    return lax.dot_general(a, b, (((0,), (1,)), ((), ())), preferred_element_type=F32)


def standardize(rows_in):
    average = jnp.mean(rows_in, axis=-1, keepdims=True)
    centered = rows_in - average
    variance = jnp.mean(centered * centered, axis=-1, keepdims=True)
    rstd = lax.rsqrt(variance + EPSILON)
    return centered * rstd, rstd


def gelu_pair(v):
    square = v * v
    half = 0.5 + 0.5 * jnp.tanh(v * (GELU_A + GELU_B * square))
    active = v * half
    slope = half + active * (1.0 - half) * (2 * GELU_A + 6 * GELU_B * square)
    return active, slope


def merge_mix(merge_logits):
    exponent = jnp.exp(merge_logits[...] - jnp.max(merge_logits[...], axis=1, keepdims=True))
    mixing = exponent / jnp.sum(exponent, axis=1, keepdims=True)
    return mixing[:, 0:1], mixing[:, 1:2]


INFO_BRANCH, INFO_CORE, INFO_X, INFO_Y, INFO_Z, INFO_LENGTH = 0, 1, 2, 3, 4, 5
SHIFTS = (0, 1, 3, 2)


def piece_copies(info, pieces, target, sems, along="x"):
    core = info[INFO_CORE]
    columns_in = pieces[0].shape[3]
    copies = []
    for i, piece in enumerate(pieces):
        at = lax.rem(info[INFO_X if along == "x" else INFO_Z] + (4 - SHIFTS[i // 2]), 4)
        side = core if i % 2 == 0 else 1 - core
        columns = pl.ds(pl.multiple_of(side * columns_in, 128), columns_in)
        for b in range(2):
            if along == "x":
                goal = target.at[b, at, :, :, columns]
            else:
                goal = target.at[b, :, at, :, columns]
            copies.append(pltpu.make_async_copy(piece.at[b], goal, sems.at[2 * i + b]))
    return copies


def weight(weights, b, first, last):
    return weights[b, :, :, :, first:last].reshape(WIDTH, last - first)


def pack_local(info, slopes, att_in, att_out, mix_in, mix_out, taps, bias, gnorm, out, own):
    for i in range(3):
        out[:, i * 256 : (i + 1) * 256] = att_in[i]
    for i in range(2):
        out[:, 768 + i * 768 : 768 + (i + 1) * 768] = mix_in[:, i, :]
    out[:, 2304:3072] = mix_out[...]
    out[:, 3072:3328] = att_out[...]
    own[0:31, :] = taps[...]
    own[31, :] = bias[...]
    own[32:34, :] = gnorm[...]
    lane = lax.broadcasted_iota(jnp.int32, (1, 768), 1)
    row = jnp.zeros((1, 768), F32)
    for r in range(4):
        row = jnp.where(lane == r, slopes[r], row)
    own[34:35, :] = row


def pair_rows(info, local, other, out):
    core = info[INFO_CORE]
    mine, theirs = local[...].astype(F32), other[...].astype(F32)
    rows = jnp.concatenate(
        [jnp.where(core == 0, mine, theirs), jnp.where(core == 0, theirs, mine)], axis=0
    )
    out[:, 0:384] = jnp.where(core == 0, rows[:, 0:384], rows[:, 384:768]).astype(BF16)
    out[:, 384:1664] = jnp.where(core == 0, rows[:, 768:2048], rows[:, 2048:3328]).astype(BF16)


def join_y(info, *rest):
    pieces, (first, second) = rest[:4], rest[4:]
    for piece, s in zip(pieces, SHIFTS):
        y = lax.rem(info[INFO_Y] + (4 - s), 4)
        at = lax.rem(y, 2) * 2 + y // 2
        first[at] = piece[:, 0:384]
        second[at] = piece[:, 384:1664]


def join_planes(info, *rest):
    over_z, over_x, (attend, mixer) = rest[:4], rest[4:8], rest[8:]
    for i, s in enumerate(SHIFTS):
        z = lax.rem(info[INFO_Z] + (4 - s), 4)
        x = lax.rem(info[INFO_X] + (4 - s), 4)
        for b in range(2):
            here = slice(b * 2, b * 2 + 2)
            attend[b, pl.ds(z * 2, 2)] = over_z[i][here]
            mixer[b, pl.ds(x * 2, 2)] = over_x[i][here]


def fill_distance(distance):
    key_at = lax.broadcasted_iota(jnp.int32, (SLOT, SLOT), 0)
    query_at = lax.broadcasted_iota(jnp.int32, (SLOT, SLOT), 1)
    offset = (key_at - query_at).astype(F32)
    distance[...] = jnp.sqrt(offset * offset + 1.0)


def attend_forward(
    info,
    frames,
    norm,
    own,
    other,
    *rest,
):
    pieces, (triple, context, log_total, weights, slopes, bias_s, sems) = rest[:8], rest[8:]
    step = pl.program_id(0)
    copies = piece_copies(info, pieces, weights, sems)

    @pl.when(step == 0)
    def _():
        for copy in copies:
            copy.start()
        branch = info[INFO_BRANCH]
        key_at = lax.broadcasted_iota(jnp.int32, (SLOT, SLOT), 0)
        query_at = lax.broadcasted_iota(jnp.int32, (SLOT, SLOT), 1)
        offset = (key_at - query_at).astype(F32)
        distance = jnp.sqrt(offset * offset + 1.0)
        for h in range(HEADS):
            lane = slice(h % 4, h % 4 + 1)
            slope = jnp.where(branch == h // 4, own[34:35, lane], other[34:35, lane])
            slopes[h : h + 1, :] = jnp.broadcast_to(slope, (1, 128))
            bias_s[h] = slope * distance
        for copy in copies:
            copy.wait()

    normed, _ = standardize(frames[0, 0])
    low = (normed * norm[0:1] + norm[1:2]).astype(BF16)
    for b in range(2):
        part = dot_tt(weight(weights, b, 0, 256), low) * (HEAD**-0.5)
        triple[0, b * 768 : b * 768 + 256, :] = part.astype(BF16)
        part = dot_tt(weight(weights, b, 256, 768), low)
        triple[0, b * 768 + 256 : (b + 1) * 768, :] = part.astype(BF16)
    is_key = lax.broadcasted_iota(jnp.int32, (SLOT, SLOT), 0) < info[INFO_LENGTH + step]

    def head(h, carry):
        base = pl.multiple_of((h // 4) * 768 + (h % 4) * HEAD, HEAD)
        q = triple[0, pl.ds(base, HEAD), :]
        k = triple[0, pl.ds(base + 256, HEAD), :]
        v = triple[0, pl.ds(base + 512, HEAD), :]
        logits = jnp.where(is_key, dot_tn(k, q) - bias_s[h], NEGATIVE)
        highest = jnp.max(logits, axis=0, keepdims=True)
        exponent = jnp.exp(logits - highest)
        total = jnp.sum(exponent, axis=0, keepdims=True)
        prob = (exponent * (1.0 / total)).astype(BF16)
        context[0, pl.ds(pl.multiple_of(h * HEAD, HEAD), HEAD), :] = dot_nn(v, prob).astype(BF16)
        log_total[0, pl.ds(h, 1), :] = highest + jnp.log(total)
        return carry

    lax.fori_loop(0, HEADS, head, 0, unroll=HEAD_UNROLL)


def mixer_both(
    info,
    frames,
    cotangent,
    context,
    mixer_norm,
    final_norm,
    merge_logits,
    own,
    other,
    forward,
    inverse,
    inverse_three,
    tap_forward,
    tap_inverse,
    *rest,
):
    pieces, rest = rest[:8], rest[8:]
    (
        layer,
        grad_frames,
        grad_context,
        keep,
        send,
        small,
        weights,
        params_s,
        small_wide,
        small_narrow,
        tap_spec,
        second_s,
        second_slope,
        first_s,
        first_slope,
        conv_s,
        spec_s,
        cross_s,
        back_s,
        gated_s,
        hidden_s,
        low_s,
        grad_s,
        attend_s,
        context_s,
        grads_s,
        sems,
    ) = rest
    step = pl.program_id(0)
    branch, core = info[INFO_BRANCH], info[INFO_CORE]
    here = pl.ds(pl.multiple_of(step * SLOT, SLOT), SLOT)
    copies = piece_copies(info, pieces, weights, sems, "z")

    @pl.when(step == 0)
    def _():
        for copy in copies:
            copy.start()
        params_s[branch] = own[...]
        params_s[1 - branch] = other[...]
        for b in range(2):
            tap_spec[:, b * 768 : (b + 1) * 768] = dot_nn(
                tap_forward[...], stack_terms(params_s[b, 0:32, :])
            )
        cross_s[...] = jnp.zeros_like(cross_s)
        small_wide[...] = jnp.zeros_like(small_wide)
        small_narrow[...] = jnp.zeros_like(small_narrow)

    mix_attend, mix_mixer = merge_mix(merge_logits)
    rows_in = frames[0, 0]
    normed, rstd = standardize(rows_in)
    low = (normed * mixer_norm[0:1] + mixer_norm[1:2]).astype(BF16)
    low_s[here, :] = low

    @pl.when(step == 0)
    def _():
        for copy in copies:
            copy.wait()

    length = info[INFO_LENGTH + step]
    valid = (lax.broadcasted_iota(jnp.int32, (SLOT, 1), 0) < length).astype(F32)

    places = [
        (k // PER_BRANCH, slice((k % PER_BRANCH) * BLOCK, (k % PER_BRANCH + 1) * BLOCK),
         slice(k * BLOCK, (k + 1) * BLOCK))
        for k in range(BLOCKS)
    ]

    def part(b, kind, off):
        return weight(weights, b, kind * 768 + off.start, kind * 768 + off.stop)

    def fold(v):
        total = v[:, 0:128]
        for at in range(128, BLOCK, 128):
            total = total + v[:, at : at + 128]
        return total

    def lane_sum(v):
        return jnp.sum(v, axis=-1, keepdims=True)

    total = jnp.zeros((SLOT, 128), F32)
    for b, off, wide in places:
        active, slope = gelu_pair(dot_nn(low, part(b, 1, off)))
        second_s[:, wide] = active
        second_slope[:, wide] = slope
        total += fold(active)
    average = lane_sum(total) / HALF
    total = jnp.zeros((SLOT, 128), F32)
    for b, off, wide in places:
        centered = second_s[:, wide] - average
        total += fold(centered * centered)
    gate_rstd = lax.rsqrt(lane_sum(total) / HALF + EPSILON)

    for b, off, wide in places:
        standard = (second_s[:, wide] - average) * gate_rstd
        gate_in = (standard * params_s[b, 32:33, off] + params_s[b, 33:34, off]) * valid
        spec = dot_nn(forward[...], stack_terms(gate_in))
        spec_s[:, wide] = spec
        real, imag = spec[0:BINS], spec[BINS:SPEC]
        tap_real, tap_imag = tap_spec[0:BINS, wide], tap_spec[BINS:SPEC, wide]
        product = jnp.concatenate(
            [real * tap_real + imag * tap_imag, imag * tap_real - real * tap_imag], axis=0
        )
        conved = dot_nn(inverse_three[...], stack_terms(product)) + params_s[b, 31:32, off]
        conv_s[:, wide] = conved
        active, slope = gelu_pair(dot_nn(low, part(b, 0, off)))
        first_s[:, wide] = active
        first_slope[:, wide] = slope
        gated_s[here, wide] = (active * conved).astype(BF16)

    mixer_part = dot_nt(gated_s[here, 0:768], weight(weights, 0, 1536, 2304)) + dot_nt(
        gated_s[here, 768:1536], weight(weights, 1, 1536, 2304)
    )
    context_s[:, here] = context[0]
    attend_part = dot_tt(context[0, 0:256, :], weight(weights, 0, 2304, 2560)) + dot_tt(
        context[0, 256:512, :], weight(weights, 1, 2304, 2560)
    )
    merged = rows_in + mix_attend * attend_part + mix_mixer * mixer_part
    merged_normed, merged_rstd = standardize(merged)
    layer[0] = ((merged_normed * final_norm[0:1] + final_norm[1:2]) * valid).astype(BF16)
    grad_out = cotangent[0, 0] * valid
    scaled = grad_out * final_norm[0:1]
    grad_merged = merged_rstd * (
        scaled
        - jnp.mean(scaled, axis=-1, keepdims=True)
        - merged_normed * jnp.mean(scaled * merged_normed, axis=-1, keepdims=True)
    )
    small_narrow[0:1] += jnp.sum(grad_out * merged_normed, axis=0, keepdims=True)
    small_narrow[1:2] += jnp.sum(grad_out, axis=0, keepdims=True)
    small_narrow[2:3] += jnp.sum(grad_merged * attend_part, axis=0, keepdims=True)
    small_narrow[3:4] += jnp.sum(grad_merged * mixer_part, axis=0, keepdims=True)
    grad_mixer = (mix_mixer * grad_merged).astype(BF16)
    grad_s[here, :] = grad_mixer
    grad_attend = (mix_attend * grad_merged).astype(BF16)
    attend_s[here, :] = grad_attend
    for b in range(2):
        grad_context[0, b * 256 : (b + 1) * 256, :] = dot_tt(
            weight(weights, b, 2304, 2560), grad_attend
        ).astype(BF16)

    total, cross_total = jnp.zeros((SLOT, 128), F32), jnp.zeros((SLOT, 128), F32)
    for b, off, wide in places:
        grad_gated = dot_nn(grad_mixer, part(b, 2, off))
        grad_conved = grad_gated * first_s[:, wide]
        hidden_s[here, wide] = (first_slope[:, wide] * (grad_gated * conv_s[:, wide])).astype(BF16)
        small_wide[31:32, wide] += jnp.sum(grad_conved, axis=0, keepdims=True)
        grad_spec = dot_nn(forward[:, 0:SLOT], grad_conved.astype(BF16))
        grad_real, grad_imag = grad_spec[0:BINS], grad_spec[BINS:SPEC]
        real, imag = spec_s[0:BINS, wide], spec_s[BINS:SPEC, wide]
        cross_s[0:BINS, wide] += grad_real * real + grad_imag * imag
        cross_s[BINS:SPEC, wide] += grad_real * imag - grad_imag * real
        tap_real, tap_imag = tap_spec[0:BINS, wide], tap_spec[BINS:SPEC, wide]
        product = jnp.concatenate(
            [
                grad_real * tap_real - grad_imag * tap_imag,
                grad_real * tap_imag + grad_imag * tap_real,
            ],
            axis=0,
        )
        grad_gate = dot_nn(inverse[...], product.astype(BF16)) * valid
        standard = (second_s[:, wide] - average) * gate_rstd
        small_wide[32:33, wide] += jnp.sum(grad_gate * standard, axis=0, keepdims=True)
        small_wide[33:34, wide] += jnp.sum(grad_gate, axis=0, keepdims=True)
        grad_standard = grad_gate * params_s[b, 32:33, off]
        back_s[:, wide] = grad_standard
        total += fold(grad_standard)
        cross_total += fold(grad_standard * standard)
    back_average = lane_sum(total) / HALF
    back_scale = lane_sum(cross_total) / HALF

    for b, off, wide in places:
        standard = (second_s[:, wide] - average) * gate_rstd
        grad_second = gate_rstd * (back_s[:, wide] - back_average - standard * back_scale)
        hidden_s[here, HALF + wide.start : HALF + wide.stop] = (
            second_slope[:, wide] * grad_second
        ).astype(BF16)
    grad_low = (
        dot_nt(hidden_s[here, 0:768], weight(weights, 0, 0, 768))
        + dot_nt(hidden_s[here, 768:1536], weight(weights, 1, 0, 768))
    ) + (
        dot_nt(hidden_s[here, 1536:2304], weight(weights, 0, 768, 1536))
        + dot_nt(hidden_s[here, 2304:3072], weight(weights, 1, 768, 1536))
    )
    small_narrow[4:5] += jnp.sum(grad_low * normed, axis=0, keepdims=True)
    small_narrow[5:6] += jnp.sum(grad_low, axis=0, keepdims=True)
    scaled = grad_low * mixer_norm[0:1]
    grad_frames[0] = grad_merged + rstd * (
        scaled
        - jnp.mean(scaled, axis=-1, keepdims=True)
        - normed * jnp.mean(scaled * normed, axis=-1, keepdims=True)
    )

    @pl.when(step == UTTS - 1)
    def _():
        outs = []
        for b in range(2):
            first, second = b * 768, HALF + b * 768
            pairs = [
                (dot_tn(low_s[...], hidden_s[:, first : first + 256]),
                 dot_tn(low_s[...], hidden_s[:, second + 512 : second + 768])),
                (dot_tn(low_s[...], hidden_s[:, first + 256 : first + 512]),
                 dot_tn(grad_s[...], gated_s[:, first : first + 256])),
                (dot_tn(low_s[...], hidden_s[:, first + 512 : first + 768]),
                 dot_tn(grad_s[...], gated_s[:, first + 256 : first + 512])),
                (dot_tn(low_s[...], hidden_s[:, second : second + 256]),
                 dot_tn(grad_s[...], gated_s[:, first + 512 : first + 768])),
                (dot_tn(low_s[...], hidden_s[:, second + 256 : second + 512]),
                 dot_tt(attend_s[...], context_s[b * 256 : (b + 1) * 256, :])),
            ]
            for i, (upper, lower) in enumerate(pairs):
                upper, lower = upper.reshape(32, 2, 8, 256), lower.reshape(32, 2, 8, 256)
                for p in range(2):
                    grads_s[p, b * 32 : (b + 1) * 32, :, i * 256 : (i + 1) * 256] = (
                        jnp.concatenate([upper[:, p], lower[:, p]], axis=1).astype(BF16)
                    )
            chips = pl.ds(b * 32, 32)
            outs += start_all(
                [
                    pltpu.make_async_copy(
                        grads_s.at[core, chips], keep.at[chips], sems.at[2 * b]
                    ),
                    pltpu.make_async_copy(
                        grads_s.at[1 - core, chips], send.at[chips], sems.at[2 * b + 1]
                    ),
                ]
            )
        tap_grad = dot_nn(tap_inverse[...], cross_s[...].astype(BF16))
        small_wide[0:31, :] = tap_grad[0:31]
        for g in range(12):
            small[g * 40 : (g + 1) * 40, :] = small_wide[:, g * 128 : (g + 1) * 128]
        for j in range(4):
            small[480 + 8 * j : 488 + 8 * j, :] = small_narrow[:, j * 128 : (j + 1) * 128]
        for copy in outs:
            copy.wait()


def attend_backward(
    info,
    frames,
    grad_mixed,
    triple,
    log_total,
    grad_context,
    norm,
    slopes,
    weights,
    frames_grad,
    keep,
    send,
    distance,
    low_s,
    triple_t,
    small,
    terms,
    sems,
):
    step = pl.program_id(0)
    here = pl.ds(pl.multiple_of(step * SLOT, SLOT), SLOT)

    @pl.when(step == 0)
    def _():
        fill_distance(distance)
        small[...] = jnp.zeros_like(small)

    normed, rstd = standardize(frames[0, 0])
    low_s[here, :] = (normed * norm[0:1] + norm[1:2]).astype(BF16)
    is_key = lax.broadcasted_iota(jnp.int32, (SLOT, SLOT), 0) < info[INFO_LENGTH + step]

    def head(h, carry):
        base = pl.multiple_of((h // 4) * 768 + (h % 4) * HEAD, HEAD)
        q = triple[0, pl.ds(base, HEAD), :]
        k = triple[0, pl.ds(base + 256, HEAD), :]
        v = triple[0, pl.ds(base + 512, HEAD), :]
        grad_here = grad_context[0, pl.ds(pl.multiple_of(h * HEAD, HEAD), HEAD), :]
        logits = dot_tn(k, q) - slopes[pl.ds(h, 1), 0:1] * distance[...]
        logits = jnp.where(is_key, logits, NEGATIVE)
        prob = jnp.exp(logits - log_total[0, pl.ds(h, 1), :])
        grad_prob = dot_tn(v, grad_here)
        row_dot = jnp.sum(prob * grad_prob, axis=0, keepdims=True)
        grad_logits = prob * (grad_prob - row_dot)
        slope_row = -jnp.sum(grad_logits * distance[...], axis=0, keepdims=True)
        small[pl.ds(8 + h, 1), :] += slope_row[:, 0:128] + slope_row[:, 128:256]
        grad_scores = grad_logits.astype(BF16)
        grad_q = dot_nn(k, grad_scores) * (HEAD**-0.5)
        grad_k = dot_nt(q, grad_scores)
        grad_v = dot_nt(grad_here, prob.astype(BF16))
        triple_t[pl.ds(base, HEAD), here] = grad_q.astype(BF16)
        triple_t[pl.ds(base + 256, HEAD), here] = grad_k.astype(BF16)
        triple_t[pl.ds(base + 512, HEAD), here] = grad_v.astype(BF16)
        return carry

    lax.fori_loop(0, HEADS, head, 0, unroll=HEAD_UNROLL)
    grad_low = dot_tt(triple_t[0:768, here], weight(weights, 0, 0, 768)) + dot_tt(
        triple_t[768:1536, here], weight(weights, 1, 0, 768)
    )
    gain_row = jnp.sum(grad_low * normed, axis=0, keepdims=True)
    bias_row = jnp.sum(grad_low, axis=0, keepdims=True)
    for j in range(4):
        small[j : j + 1, :] += gain_row[:, j * 128 : (j + 1) * 128]
        small[4 + j : 5 + j, :] += bias_row[:, j * 128 : (j + 1) * 128]
    scaled = grad_low * norm[0:1]
    frames_grad[0] = (
        grad_mixed[0]
        + rstd
        * (
            scaled
            - jnp.mean(scaled, axis=-1, keepdims=True)
            - normed * jnp.mean(scaled * normed, axis=-1, keepdims=True)
        )
    ).astype(BF16)

    @pl.when(step == UTTS - 1)
    def _():
        high, low = split_low(jnp.sum(small[8:16, :], axis=1, keepdims=True))
        block = jnp.concatenate([small[0:8, :], slope_rows(high, low)], axis=0).astype(BF16)
        for b in range(2):
            grads = dot_tt(low_s[...], triple_t[b * 768 : (b + 1) * 768, :]).reshape(32, 2, 8, 768)
            for p in range(2):
                terms[p, b * 32 : (b + 1) * 32, :, 0:384] = jnp.concatenate(
                    [grads[:, p, :, 0:384], grads[:, p, :, 384:768]], axis=1
                ).astype(BF16)
                for m in range(32):
                    terms[p, b * 32 + m, :, 384:512] = block
        core = info[INFO_CORE]
        outs = start_all(
            [
                pltpu.make_async_copy(terms.at[core], keep, sems.at[0]),
                pltpu.make_async_copy(terms.at[1 - core], send, sems.at[1]),
            ]
        )
        for copy in outs:
            copy.wait()


def stack_terms(value):
    high, low = split_low(value)
    return jnp.concatenate([high, low, high], axis=0).astype(BF16)


def slope_rows(high, low):
    lane = lax.broadcasted_iota(jnp.int32, (8, 128), 1)
    return jnp.where(lane == 0, high, jnp.where(lane == 1, low, 0.0))


def split_low(value):
    high = value.astype(BF16).astype(F32)
    return high, value - high


def start_all(copies):
    for copy in copies:
        copy.start()
    return copies


def chunk_copies(source, target, count, sems):
    size = target.shape[0] // count
    return start_all(
        [
            pltpu.make_async_copy(
                source.at[pl.ds(i * size, size)], target.at[pl.ds(i * size, size)], sems.at[i]
            )
            for i in range(count)
        ]
    )


CHUNKS = 8


def sum_pairs(info, keep, other, pieces, keep_s, other_s, out_s, sems):
    loads = []
    for i, s in enumerate(SHIFTS):
        x = lax.rem(info[INFO_X] + s, 4)
        for b in range(2):
            chips = pl.ds(b * 32 + x * 8, 8)
            here = pl.ds(b * 8, 8)
            loads.append(
                start_all(
                    [
                        pltpu.make_async_copy(
                            source.at[chips], target.at[i, here], sems.at[p, 2 * i + b]
                        )
                        for p, (source, target) in enumerate(((keep, keep_s), (other, other_s)))
                    ]
                )
            )
    stores = []
    columns = keep.shape[2]
    for i in (1, 2, 3, 0):
        for b in range(2):
            for copy in loads[2 * i + b]:
                copy.wait()
            here = slice(b * 8, b * 8 + 8)
            out_s[i, here, :, 0:columns] = (
                keep_s[i, here].astype(F32) + other_s[i, here].astype(F32)
            ).astype(BF16)
        yield i
        stores.append(pltpu.make_async_copy(out_s.at[i], pieces[i], sems.at[2, i]))
        stores[-1].start()
    for copy in stores:
        copy.wait()


def spread_small(small, small_other, out):
    high, low = split_low(small[...] + small_other[...])
    for j in range(16):
        for x in range(4):
            chip = (j // 8 * 4 + x) * 8 + j % 8
            rows = slice(8 * chip, 8 * chip + 8)
            out[j, 16 * x : 16 * x + 16, :] = jnp.concatenate(
                [high[rows], low[rows]], axis=0
            ).astype(BF16)


def sum_mixer(info, keep, other, small, small_other, *rest):
    pieces, (small_out, keep_s, other_s, out_s, sems) = rest[:4], rest[4:]
    sums = sum_pairs(info, keep, other, pieces, keep_s, other_s, out_s, sems)
    next(sums)
    spread_small(small, small_other, small_out)
    for _ in sums:
        pass


def sum_attend(info, keep, other, small_terms, *rest):
    pieces, (keep_s, other_s, out_s, sems) = rest[:4], rest[4:]
    total = (small_terms[0].astype(F32) + small_terms[1].astype(F32)) + (
        small_terms[2].astype(F32) + small_terms[3].astype(F32)
    )
    for i in range(4, 16):
        total += small_terms[i].astype(F32)
    chunks = []
    for x in range(4):
        high, low = split_low(total[16 * x : 16 * x + 8] + total[16 * x + 8 : 16 * x + 16])
        chunks.append(jnp.concatenate([high, low], axis=0))
    chunks = jnp.concatenate(chunks, axis=1).astype(BF16)
    for i in sum_pairs(info, keep, other, pieces, keep_s, other_s, out_s, sems):
        total = keep_s[i, 0, :, 384:512].astype(F32) + other_s[i, 0, :, 384:512].astype(F32)
        high, low = split_low(total[8:16, 0:1] + total[8:16, 1:2])
        block = jnp.concatenate([total[0:8], slope_rows(high, low)], axis=0).astype(BF16)
        for j in range(16):
            out_s[i, j, :, 384:512] = block
        out_s[i, 16] = chunks


def sum_four(info, *rest):
    terms, (out, terms_s, sems) = rest[:4], rest[4:]
    loads = [
        start_all(
            [
                pltpu.make_async_copy(
                    terms[i].at[pl.ds(c * 4, 4)], terms_s.at[i, pl.ds(c * 4, 4)], sems.at[i, c]
                )
                for i in range(4)
            ]
        )
        for c in range(4)
    ]
    for c in range(4):
        for copy in loads[c]:
            copy.wait()
        here = slice(c * 4, c * 4 + 4)
        total = (terms_s[0, here].astype(F32) + terms_s[1, here].astype(F32)) + (
            terms_s[2, here].astype(F32) + terms_s[3, here].astype(F32)
        )
        out[here] = total.astype(BF16)


def join_terms(info, mixer, *rest):
    terms, out = rest[0:4], rest[4]
    for j in range(16):
        out[j, :, 0:1280] = mixer[j]
        total = (terms[0][j].astype(F32) + terms[1][j].astype(F32)) + (
            terms[2][j].astype(F32) + terms[3][j].astype(F32)
        )
        out[j, :, 1280:1664] = total[:, 0:384].astype(BF16)
        if j == 0:
            little = total[:, 384:512]
            high, low = split_low(little[8:16, 0:1] + little[8:16, 1:2])
            block = jnp.concatenate([little[0:8], slope_rows(high, low)], axis=0).astype(BF16)
        out[j, :, 1664:1792] = block
    total = (terms[0][16].astype(F32) + terms[1][16].astype(F32)) + (
        terms[2][16].astype(F32) + terms[3][16].astype(F32)
    )
    high, low = split_low(total[0:8] + total[8:16])
    chunks = jnp.concatenate([high, low], axis=0).astype(BF16)
    for j in range(16):
        out[j, :, 1792:2304] = chunks


def finish(
    info,
    merge_logits,
    terms,
    att_in,
    att_out,
    mix_in,
    mix_out,
    anorm,
    mnorm,
    fnorm,
    gnorm,
    taps,
    bias,
    slope,
    merge,
    terms_s,
    small,
    sems,
):
    branch = info[INFO_BRANCH]
    copies = chunk_copies(terms, terms_s, CHUNKS, sems)
    total = jnp.zeros((16, 1792), F32)
    for c in range(CHUNKS):
        copies[c].wait()
        for i in range(c * 2, c * 2 + 2):
            total += terms_s[i, :, 0:1792].astype(F32)
            for x in range(4):
                pair = terms_s[i, :, 1792 + x * 128 : 1920 + x * 128].astype(F32)
                chip = (i // 8 * 4 + x) * 8 + i % 8
                small[8 * chip : 8 * chip + 8, :] = pair[0:8] + pair[8:16]
    upper, lower = total[0:8], total[8:16]
    mix_in[:, 0, :] = upper[:, 0:768]
    mix_in[:, 1, :] = jnp.concatenate([upper[:, 768:1280], lower[:, 0:256]], axis=1)
    mix_out[...] = lower[:, 256:1024]
    att_out[...] = lower[:, 1024:1280]
    total = total[:, 1280:1792]
    for g in range(6):
        group = small[pl.ds(pl.multiple_of((branch * 6 + g) * 40, 8), 40), :]
        columns = slice(g * 128, (g + 1) * 128)
        taps[:, columns] = group[0:31]
        bias[columns] = group[31]
        gnorm[:, columns] = group[32:34]
    attend_sum, mixer_sum = 0.0, 0.0
    for j in range(4):
        columns = slice(j * 128, (j + 1) * 128)
        group = small[480 + 8 * j : 488 + 8 * j, :]
        fnorm[:, columns] = group[0:2]
        mnorm[:, columns] = group[4:6]
        attend_sum += jnp.sum(group[2:3], axis=1, keepdims=True)
        mixer_sum += jnp.sum(group[3:4], axis=1, keepdims=True)
    mix_attend, mix_mixer = merge_mix(merge_logits)
    average = mix_attend * attend_sum + mix_mixer * mixer_sum
    merge[0] = jnp.sum(mix_attend * (attend_sum - average))
    merge[1] = jnp.sum(mix_mixer * (mixer_sum - average))
    att_in[0] = total[0:8, 0:256]
    att_in[1] = jnp.concatenate([total[0:8, 256:384], total[8:16, 0:128]], axis=1)
    att_in[2] = total[8:16, 128:384]
    for p in range(2):
        for j in range(4):
            r = p * 4 + j
            anorm[p : p + 1, j * 128 : (j + 1) * 128] = total[r : r + 1, 384:512]
    slopes = total[8:16, 384:385] + total[8:16, 385:386]
    for r in range(4):
        slope[r] = jnp.where(
            branch == 0, jnp.sum(slopes[r : r + 1]), jnp.sum(slopes[4 + r : 5 + r])
        )


def place_pair(info, own, other, out, own_s, other_s, out_s, sems):
    branch = info[INFO_BRANCH]
    loads = [
        start_all(
            [
                pltpu.make_async_copy(source.at[u], target.at[u], sems.at[p, u])
                for u in range(UTTS)
            ]
        )
        for p, (source, target) in enumerate(((own, own_s), (other, other_s)))
    ]
    stores = []
    for u in range(UTTS):
        for p, source in enumerate((own_s, other_s)):
            loads[p][u].wait()
            out_s[p, u] = source[u].astype(F32)
            at = branch if p == 0 else 1 - branch
            stores.append(
                pltpu.make_async_copy(out_s.at[p, u], out.at[u, at], sems.at[2 + p, u])
            )
            stores[-1].start()
    for copy in stores:
        copy.wait()


def whole(shape):
    return pl.BlockSpec(shape, lambda i, *_: (0,) * len(shape), pipeline_mode=pl.Buffered(1))


def per_utt(shape):
    return pl.BlockSpec((1,) + shape, lambda i, *_: (i,) + (0,) * len(shape))


ANY = pl.BlockSpec(memory_space=pl.ANY)
OWN_FRAMES = pl.BlockSpec((1, 1, SLOT, WIDTH), lambda i, info, *_: (i, info[0], 0, 0))


def scratch(*shape, dtype=F32):
    return pltpu.VMEM(shape, dtype)


def struct(*shape, dtype=F32):
    return jax.ShapeDtypeStruct(shape, dtype)


def call(kernel, name, info, operands, in_specs, outs, out_specs, scratches=(), grid=1, us=2, **extra):
    return pl.pallas_call(
        kernel,
        grid_spec=pltpu.PrefetchScalarGridSpec(
            num_scalar_prefetch=1,
            grid=(grid,),
            in_specs=in_specs,
            out_specs=out_specs,
            scratch_shapes=scratches,
        ),
        out_shape=outs,
        compiler_params=pltpu.CompilerParams(
            dimension_semantics=("arbitrary",), vmem_limit_bytes=VMEM_LIMIT
        ),
        cost_estimate=pl.CostEstimate(
            flops=us * 100000000, bytes_accessed=1 << 16, transcendentals=0
        ),
        name=name,
        **extra,
    )(info, *operands)


def run_pack(slopes, *operands):
    return call(
        pack_local,
        "pack_local",
        np.zeros((8,), np.int32),
        (slopes, *operands),
        [pl.BlockSpec(memory_space=pltpu.SMEM)] + [whole(a.shape) for a in operands],
        [struct(8, 3328, dtype=BF16), struct(35, 768)],
        [whole((8, 3328)), whole((35, 768))],
    )


def run_pair(info, local, other):
    return call(
        pair_rows,
        "pair_rows",
        info,
        (local, other),
        [whole((8, 3328))] * 2,
        struct(16, 1664, dtype=BF16),
        whole((16, 1664)),
    )


def run_join_y(info, pieces):
    shapes = [(4, 16, 384), (4, 16, 1280)]
    return call(
        join_y,
        "join_y",
        info,
        pieces,
        [whole((16, 1664))] * 4,
        [struct(*s, dtype=BF16) for s in shapes],
        [whole(s) for s in shapes],
    )


def run_join_planes(info, over_z, over_x):
    shapes = [(2, 8, 16, 384), (2, 8, 16, 1280)]
    return call(
        join_planes,
        "join_planes",
        info,
        (*over_z, *over_x),
        [whole((4, 16, 384))] * 4 + [whole((4, 16, 1280))] * 4,
        [struct(*s, dtype=BF16) for s in shapes],
        [whole(s) for s in shapes],
    )


def run_attend_forward(info, frames, norm, own, other, pieces):
    return call(
        attend_forward,
        "attend_forward",
        info,
        (frames, norm, own, other, *pieces),
        [OWN_FRAMES, whole((2, WIDTH)), whole((35, 768)), whole((35, 768))] + [ANY] * 8,
        [
            struct(UTTS, HALF, SLOT, dtype=BF16),
            struct(UTTS, WIDTH, SLOT, dtype=BF16),
            struct(UTTS, HEADS, SLOT),
            struct(2, 4, 4, 32, 768, dtype=BF16),
            struct(HEADS, 128),
        ],
        [
            per_utt((HALF, SLOT)),
            per_utt((WIDTH, SLOT)),
            per_utt((HEADS, SLOT)),
            whole((2, 4, 4, 32, 768)),
            whole((HEADS, 128)),
        ],
        [scratch(HEADS, SLOT, SLOT), pltpu.SemaphoreType.DMA((16,))],
        grid=UTTS,
    )


def run_mixer(info, frames, cotangent, context, mnorm, fnorm, merge_logits, own, other, pieces):
    forward, inverse, inverse_three, tap_forward, tap_inverse = transform_tables()
    tables = (
        jnp.asarray(forward, BF16),
        jnp.asarray(inverse, BF16),
        jnp.asarray(inverse_three, BF16),
        jnp.asarray(tap_forward, BF16),
        jnp.asarray(tap_inverse, BF16),
    )
    return call(
        mixer_both,
        "mixer_both",
        info,
        (frames, cotangent, context, mnorm, fnorm, merge_logits, own, other, *tables, *pieces),
        [
            OWN_FRAMES,
            OWN_FRAMES,
            per_utt((WIDTH, SLOT)),
            whole((2, WIDTH)),
            whole((2, WIDTH)),
            whole((1, 2)),
            whole((35, 768)),
            whole((35, 768)),
            whole((SPEC, 3 * SLOT)),
            whole((SLOT, SPEC)),
            whole((SLOT, 3 * SPEC)),
            whole((SPEC, 96)),
            whole((32, SPEC)),
        ]
        + [ANY] * 8,
        [
            struct(UTTS, SLOT, WIDTH, dtype=BF16),
            struct(UTTS, SLOT, WIDTH),
            struct(UTTS, WIDTH, SLOT, dtype=BF16),
            struct(64, 16, 1280, dtype=BF16),
            struct(64, 16, 1280, dtype=BF16),
            struct(512, 128),
        ],
        [
            per_utt((SLOT, WIDTH)),
            per_utt((SLOT, WIDTH)),
            per_utt((WIDTH, SLOT)),
            ANY,
            ANY,
            whole((512, 128)),
        ],
        [
            scratch(2, 4, 4, 32, 2560, dtype=BF16),
            scratch(2, 35, 768),
            scratch(40, HALF),
            scratch(8, WIDTH),
            scratch(SPEC, HALF),
            scratch(SLOT, HALF),
            scratch(SLOT, HALF),
            scratch(SLOT, HALF),
            scratch(SLOT, HALF),
            scratch(SLOT, HALF),
            scratch(SPEC, HALF),
            scratch(SPEC, HALF),
            scratch(SLOT, HALF),
            scratch(ROWS, HALF, dtype=BF16),
            scratch(ROWS, 2 * HALF, dtype=BF16),
            scratch(ROWS, WIDTH, dtype=BF16),
            scratch(ROWS, WIDTH, dtype=BF16),
            scratch(ROWS, WIDTH, dtype=BF16),
            scratch(WIDTH, ROWS, dtype=BF16),
            scratch(2, 64, 16, 1280, dtype=BF16),
            pltpu.SemaphoreType.DMA((16,)),
        ],
        grid=UTTS,
    )


def run_attend_backward(
    info, frames, grad_mixed, triple, log_total, grad_context, norm, slopes, weights
):
    return call(
        attend_backward,
        "attend_backward",
        info,
        (frames, grad_mixed, triple, log_total, grad_context, norm, slopes, weights),
        [
            OWN_FRAMES,
            per_utt((SLOT, WIDTH)),
            per_utt((HALF, SLOT)),
            per_utt((HEADS, SLOT)),
            per_utt((WIDTH, SLOT)),
            whole((2, WIDTH)),
            whole((HEADS, 128)),
            whole((2, 4, 4, 32, 768)),
        ],
        [
            struct(UTTS, SLOT, WIDTH, dtype=BF16),
            struct(64, 16, 512, dtype=BF16),
            struct(64, 16, 512, dtype=BF16),
        ],
        [per_utt((SLOT, WIDTH)), ANY, ANY],
        [
            scratch(SLOT, SLOT),
            scratch(ROWS, WIDTH, dtype=BF16),
            scratch(HALF, ROWS, dtype=BF16),
            scratch(16, 128),
            scratch(2, 64, 16, 512, dtype=BF16),
            pltpu.SemaphoreType.DMA((2,)),
        ],
        grid=UTTS,
    )


def run_sum_mixer(info, keep, other, small, small_other):
    piece = (16, 16, 1280)
    return call(
        sum_mixer,
        "sum_mixer",
        info,
        (keep, other, small, small_other),
        [ANY, ANY, whole((512, 128)), whole((512, 128))],
        [struct(*piece, dtype=BF16)] * 4 + [struct(16, 64, 128, dtype=BF16)],
        [ANY] * 4 + [whole((16, 64, 128))],
        [scratch(4, *piece, dtype=BF16)] * 3 + [pltpu.SemaphoreType.DMA((3, 8))],
    )


def run_sum_attend(info, keep, other, small_terms):
    piece, wider = (16, 16, 512), (17, 16, 512)
    return call(
        sum_attend,
        "sum_attend",
        info,
        (keep, other, small_terms),
        [ANY, ANY, whole((16, 64, 128))],
        [struct(*wider, dtype=BF16)] * 4,
        [ANY] * 4,
        [scratch(4, *piece, dtype=BF16)] * 2
        + [scratch(4, *wider, dtype=BF16), pltpu.SemaphoreType.DMA((3, 8))],
    )


def run_sum_four(info, terms):
    piece = terms[0].shape
    return call(
        sum_four,
        "sum_four",
        info,
        terms,
        [ANY] * 4,
        struct(*piece, dtype=BF16),
        whole(piece),
        [scratch(4, *piece, dtype=BF16), pltpu.SemaphoreType.DMA((4, 4))],
    )


def run_join(info, mixer, terms):
    return call(
        join_terms,
        "join_terms",
        info,
        (mixer, *terms),
        [whole(mixer.shape)] + [whole(terms[0].shape)] * 4,
        struct(16, 16, 2304, dtype=BF16),
        whole((16, 16, 2304)),
    )


def run_finish(info, *operands):
    shapes = [
        (3, 8, 256),
        (8, 256),
        (8, 2, 768),
        (8, 768),
        (2, WIDTH),
        (2, WIDTH),
        (2, WIDTH),
        (2, 768),
        (31, 768),
        (768,),
    ]
    scalars = pl.BlockSpec(memory_space=pltpu.SMEM)
    return call(
        finish,
        "finish",
        info,
        operands,
        [whole(a.shape) for a in operands[:-1]] + [ANY],
        [struct(*s) for s in shapes] + [struct(4), struct(2)],
        [whole(s) for s in shapes] + [scalars, scalars],
        [
            scratch(*operands[-1].shape, dtype=BF16),
            scratch(512, 128),
            pltpu.SemaphoreType.DMA((CHUNKS,)),
        ],
    )


def run_place_pair(info, own, other):
    return call(
        place_pair,
        "place_pair",
        info,
        (own, other),
        [ANY, ANY],
        struct(UTTS, 2, SLOT, WIDTH),
        ANY,
        [
            scratch(UTTS, SLOT, WIDTH, dtype=BF16),
            scratch(UTTS, SLOT, WIDTH, dtype=BF16),
            scratch(2, UTTS, SLOT, WIDTH),
            pltpu.SemaphoreType.DMA((4, UTTS)),
        ],
    )


def swap(value, axis):
    return lax.ppermute(value, axis, [(0, 1), (1, 0)])


def move_x(block, distance):
    return lax.ppermute(block, "x", [(i, (i + distance) % 4) for i in range(4)])


def move_y(block, distance):
    def joint(y):
        return (y % 2) * 2 + y // 2

    return lax.ppermute(
        block, ("branch", "yh"), [(joint(y), joint((y + distance) % 4)) for y in range(4)]
    )


def move(block, axis, distance):
    return lax.ppermute(block, axis, [(i, (i + distance) % 4) for i in range(4)])


def along(block, axis):
    return [block] + [move(block, axis, s) for s in SHIFTS[1:]]


def with_partner(pieces):
    both = []
    for piece in pieces:
        both += [piece, swap(piece, "core")]
    return both


def exchange_x(pieces):
    return [pieces[0]] + [move(p, "x", s) for p, s in zip(pieces[1:], SHIFTS[1:])]


CHIPS = ("branch", "x", "z", "yh")
PLANE = ("branch", "z", "yh")


def exchange(blocks, axes):
    return lax.all_to_all(blocks, axes, 0, 0, tiled=True)


def shards(
    frames,
    attend_norm,
    attend_in,
    attend_out,
    position_slope,
    mixer_norm,
    mixer_in,
    gating_norm,
    kernel_taps,
    kernel_bias,
    mixer_out,
    merge_logits,
    final_norm,
    lengths,
    cotangent,
):
    branch = lax.axis_index("branch")
    core = lax.axis_index("core")
    own_lengths = lax.dynamic_slice_in_dim(lengths, branch, 1, 1)[:, 0]
    x, yh, z = (lax.axis_index(axis) for axis in ("x", "yh", "z"))
    info = jnp.concatenate([jnp.stack([branch, core, x, 2 * yh + branch, z]), own_lengths])
    merge_logits = merge_logits[None]
    local, own = run_pack(
        position_slope,
        attend_in.transpose(1, 0, 2),
        attend_out,
        mixer_in,
        mixer_out,
        kernel_taps,
        kernel_bias,
        gating_norm,
    )
    other = swap(own, "branch")
    block = run_pair(info, local, swap(local, "core"))
    first, second = run_join_y(info, [block] + [move_y(block, s) for s in SHIFTS[1:]])
    first, second, other = lax.optimization_barrier((first, second, other))
    attend_block, mixer_block = run_join_planes(info, along(first, "z"), along(second, "x"))
    attend_pieces = along(attend_block.reshape(2, 4, 32, 384), "x")
    mixer_pieces = along(mixer_block.reshape(2, 4, 32, 1280), "z")

    triple, context, log_total, attend_w, slopes = run_attend_forward(
        info, frames, attend_norm, own, other, with_partner(attend_pieces)
    )
    *mixer_pieces, context = lax.optimization_barrier((*mixer_pieces, context))
    layer, grad_mixed, grad_context, mixer_keep, mixer_send, small = run_mixer(
        info,
        frames,
        cotangent,
        context,
        mixer_norm,
        final_norm,
        merge_logits,
        own,
        other,
        with_partner(mixer_pieces),
    )
    small_other = swap(small, "core")
    mixer_other = swap(mixer_send, "core")
    layer_other = swap(layer, "branch")
    *mixer_sent, small_sent = run_sum_mixer(info, mixer_keep, mixer_other, small, small_other)
    mixer_terms = exchange_x(mixer_sent)
    small_sent, _, grad_context = lax.optimization_barrier(
        (small_sent, mixer_sent[0], grad_context)
    )
    grads, attend_keep, attend_send = run_attend_backward(
        info,
        frames,
        grad_mixed,
        triple,
        log_total,
        grad_context,
        attend_norm,
        slopes,
        attend_w,
    )
    small_sent, grads = lax.optimization_barrier((small_sent, grads))
    small_terms = exchange(small_sent, PLANE)
    grads, attend_keep, attend_send, layer_other, small_terms, *mixer_terms = (
        lax.optimization_barrier(
            (grads, attend_keep, attend_send, layer_other, small_terms, *mixer_terms)
        )
    )
    grads_other = swap(grads, "branch")
    attend_terms = exchange_x(
        run_sum_attend(info, attend_keep, swap(attend_send, "core"), small_terms)
    )
    mixer_total = run_sum_four(info, mixer_terms)
    layer_out = run_place_pair(info, layer, layer_other)
    *attend_terms, mixer_total, grads_other, layer_out = lax.optimization_barrier(
        (*attend_terms, mixer_total, grads_other, layer_out)
    )
    terms = exchange(run_join(info, mixer_total, attend_terms), PLANE)
    frames_out = run_place_pair(info, grads, grads_other)
    (
        att_in,
        att_out,
        mix_in,
        mix_out,
        anorm,
        mnorm,
        fnorm,
        gnorm,
        taps,
        bias,
        slope,
        merge,
    ) = run_finish(
        info,
        merge_logits,
        terms,
    )
    return (
        layer_out,
        frames_out,
        anorm,
        att_in.transpose(1, 0, 2),
        att_out,
        slope,
        mnorm,
        mix_in,
        gnorm,
        taps,
        bias,
        mix_out,
        merge,
        fnorm,
    )


def solution(mesh):
    fine = Mesh(mesh.devices.reshape(2, 4, 4, 2, 2), ("branch", "x", "z", "yh", "core"))
    dp = ("x", "z", "yh", "core")
    placed = (
        P(None, dp, None, None),
        P(),
        P(dp, None, "branch"),
        P(dp, "branch"),
        P("branch"),
        P(),
        P(dp, None, "branch"),
        P(None, "branch"),
        P(None, "branch"),
        P("branch"),
        P(dp, "branch"),
        P(),
        P(),
        P(None, dp),
        P(None, dp, None, None),
    )
    return jax.shard_map(
        shards,
        mesh=fine,
        in_specs=placed,
        out_specs=(
            P(None, dp, None, None),
            P(None, dp, None, None),
            P(),
            P(dp, None, "branch"),
            P(dp, "branch"),
            P("branch"),
            P(),
            P(dp, None, "branch"),
            P(None, "branch"),
            P(None, "branch"),
            P("branch"),
            P(dp, "branch"),
            P(),
            P(),
        ),
        check_vma=False,
    )
```

```python
from functools import partial

import jax
import jax.numpy as jnp
import numpy as np
from jax import lax
from jax.experimental import pallas as pl
from jax.experimental.pallas import tpu as pltpu
from jax.sharding import Mesh
from jax.sharding import PartitionSpec as P

EPSILON = 1e-05
NEGATIVE = -1e30
F32 = jnp.float32
BF16 = jnp.bfloat16
SLOT = 256
WIDTH = 512
HEADS = 8
HEAD = 64
HALF = 1536
TAPS = 31
REACH = 15
UTTS = 3
ROWS = UTTS * SLOT
PERIOD = SLOT + REACH
BINS = (PERIOD + 1) // 2
SPEC = 2 * BINS
BLOCK = 768
BLOCKS = HALF // BLOCK
PER_BRANCH = 768 // BLOCK
GELU_A = 0.7978845608028654
GELU_B = GELU_A * 0.044715
HEAD_UNROLL = 8
VMEM_LIMIT = 64 * 1024 * 1024 - 65536


def three_terms(table):
    high = np.asarray(table.astype(BF16)).astype(np.float64)
    return np.concatenate([high, high, table - high], 1)


def transform_tables():
    bins = np.arange(BINS)[:, None]
    angle = 2 * np.pi * bins * np.arange(SLOT)[None, :] / PERIOD
    lag_angle = 2 * np.pi * bins * (np.arange(TAPS) - REACH)[None, :] / PERIOD
    weight = np.where(bins == 0, 1.0, 2.0) / PERIOD
    forward = np.concatenate([np.cos(angle), -np.sin(angle)], 0)
    inverse = np.concatenate([np.cos(angle) * weight, -np.sin(angle) * weight], 0).T
    tap_forward = np.concatenate([np.cos(lag_angle), -np.sin(lag_angle)], 0)
    tap_inverse = np.concatenate([np.cos(lag_angle) * weight, -np.sin(lag_angle) * weight], 0).T
    tap_forward = three_terms(np.pad(tap_forward, ((0, 0), (0, 1))))
    tap_inverse = np.pad(tap_inverse, ((0, 1), (0, 0)))
    return three_terms(forward), inverse, three_terms(inverse), tap_forward, tap_inverse


def dot_nn(a, b):
    return lax.dot_general(a, b, (((1,), (0,)), ((), ())), preferred_element_type=F32)


def dot_nt(a, b):
    return lax.dot_general(a, b, (((1,), (1,)), ((), ())), preferred_element_type=F32)


def dot_tn(a, b):
    return lax.dot_general(a, b, (((0,), (0,)), ((), ())), preferred_element_type=F32)


def dot_tt(a, b):
    return lax.dot_general(a, b, (((0,), (1,)), ((), ())), preferred_element_type=F32)


def standardize(rows_in):
    average = jnp.mean(rows_in, axis=-1, keepdims=True)
    centered = rows_in - average
    variance = jnp.mean(centered * centered, axis=-1, keepdims=True)
    rstd = lax.rsqrt(variance + EPSILON)
    return centered * rstd, rstd


def gelu_pair(v):
    square = v * v
    half = 0.5 + 0.5 * jnp.tanh(v * (GELU_A + GELU_B * square))
    active = v * half
    slope = half + active * (1.0 - half) * (2 * GELU_A + 6 * GELU_B * square)
    return active, slope


def merge_mix(merge_logits):
    exponent = jnp.exp(merge_logits[...] - jnp.max(merge_logits[...], axis=1, keepdims=True))
    mixing = exponent / jnp.sum(exponent, axis=1, keepdims=True)
    return mixing[:, 0:1], mixing[:, 1:2]


INFO_BRANCH, INFO_CORE, INFO_X, INFO_Y, INFO_Z, INFO_LENGTH = 0, 1, 2, 3, 4, 5
SHIFTS = (0, 1, 3, 2)


def piece_copies(info, pieces, target, sems, along="x"):
    core = info[INFO_CORE]
    columns_in = pieces[0].shape[3]
    copies = []
    for i, piece in enumerate(pieces):
        at = lax.rem(info[INFO_X if along == "x" else INFO_Z] + (4 - SHIFTS[i // 2]), 4)
        side = core if i % 2 == 0 else 1 - core
        columns = pl.ds(pl.multiple_of(side * columns_in, 128), columns_in)
        for b in range(2):
            if along == "x":
                goal = target.at[b, at, :, :, columns]
            else:
                goal = target.at[b, :, at, :, columns]
            copies.append(pltpu.make_async_copy(piece.at[b], goal, sems.at[2 * i + b]))
    return copies


def weight(weights, b, first, last):
    return weights[b, :, :, :, first:last].reshape(WIDTH, last - first)


def pack_local(info, slopes, att_in, att_out, mix_in, mix_out, taps, bias, gnorm, out, own):
    for i in range(3):
        out[:, i * 256 : (i + 1) * 256] = att_in[i]
    for i in range(2):
        out[:, 768 + i * 768 : 768 + (i + 1) * 768] = mix_in[:, i, :]
    out[:, 2304:3072] = mix_out[...]
    out[:, 3072:3328] = att_out[...]
    own[0:31, :] = taps[...]
    own[31, :] = bias[...]
    own[32:34, :] = gnorm[...]
    lane = lax.broadcasted_iota(jnp.int32, (1, 768), 1)
    row = jnp.zeros((1, 768), F32)
    for r in range(4):
        row = jnp.where(lane == r, slopes[r], row)
    own[34:35, :] = row


def pair_rows(info, local, other, out):
    core = info[INFO_CORE]
    mine, theirs = local[...].astype(F32), other[...].astype(F32)
    rows = jnp.concatenate(
        [jnp.where(core == 0, mine, theirs), jnp.where(core == 0, theirs, mine)], axis=0
    )
    out[:, 0:384] = jnp.where(core == 0, rows[:, 0:384], rows[:, 384:768]).astype(BF16)
    out[:, 384:1664] = jnp.where(core == 0, rows[:, 768:2048], rows[:, 2048:3328]).astype(BF16)


def join_y(info, *rest):
    pieces, (first, second) = rest[:4], rest[4:]
    for piece, s in zip(pieces, SHIFTS):
        y = lax.rem(info[INFO_Y] + (4 - s), 4)
        at = lax.rem(y, 2) * 2 + y // 2
        first[at] = piece[:, 0:384]
        second[at] = piece[:, 384:1664]


def join_planes(info, *rest):
    over_z, over_x, (attend, mixer) = rest[:4], rest[4:8], rest[8:]
    for i, s in enumerate(SHIFTS):
        z = lax.rem(info[INFO_Z] + (4 - s), 4)
        x = lax.rem(info[INFO_X] + (4 - s), 4)
        for b in range(2):
            here = slice(b * 2, b * 2 + 2)
            attend[b, pl.ds(z * 2, 2)] = over_z[i][here]
            mixer[b, pl.ds(x * 2, 2)] = over_x[i][here]


def fill_distance(distance):
    key_at = lax.broadcasted_iota(jnp.int32, (SLOT, SLOT), 0)
    query_at = lax.broadcasted_iota(jnp.int32, (SLOT, SLOT), 1)
    offset = (key_at - query_at).astype(F32)
    distance[...] = jnp.sqrt(offset * offset + 1.0)


def attend_forward(
    info,
    frames,
    norm,
    own,
    other,
    *rest,
):
    pieces, (triple, context, log_total, weights, slopes, bias_s, sems) = rest[:8], rest[8:]
    step = pl.program_id(0)
    copies = piece_copies(info, pieces, weights, sems)

    @pl.when(step == 0)
    def _():
        for copy in copies:
            copy.start()
        branch = info[INFO_BRANCH]
        key_at = lax.broadcasted_iota(jnp.int32, (SLOT, SLOT), 0)
        query_at = lax.broadcasted_iota(jnp.int32, (SLOT, SLOT), 1)
        offset = (key_at - query_at).astype(F32)
        distance = jnp.sqrt(offset * offset + 1.0)
        for h in range(HEADS):
            lane = slice(h % 4, h % 4 + 1)
            slope = jnp.where(branch == h // 4, own[34:35, lane], other[34:35, lane])
            slopes[h : h + 1, :] = jnp.broadcast_to(slope, (1, 128))
            bias_s[h] = slope * distance
        for copy in copies:
            copy.wait()

    normed, _ = standardize(frames[0, 0])
    low = (normed * norm[0:1] + norm[1:2]).astype(BF16)
    for b in range(2):
        part = dot_tt(weight(weights, b, 0, 256), low) * (HEAD**-0.5)
        triple[0, b * 768 : b * 768 + 256, :] = part.astype(BF16)
        part = dot_tt(weight(weights, b, 256, 768), low)
        triple[0, b * 768 + 256 : (b + 1) * 768, :] = part.astype(BF16)
    is_key = lax.broadcasted_iota(jnp.int32, (SLOT, SLOT), 0) < info[INFO_LENGTH + step]

    def head(h, carry):
        base = pl.multiple_of((h // 4) * 768 + (h % 4) * HEAD, HEAD)
        q = triple[0, pl.ds(base, HEAD), :]
        k = triple[0, pl.ds(base + 256, HEAD), :]
        v = triple[0, pl.ds(base + 512, HEAD), :]
        logits = jnp.where(is_key, dot_tn(k, q) - bias_s[h], NEGATIVE)
        highest = jnp.max(logits, axis=0, keepdims=True)
        exponent = jnp.exp(logits - highest)
        total = jnp.sum(exponent, axis=0, keepdims=True)
        prob = (exponent * (1.0 / total)).astype(BF16)
        context[0, pl.ds(pl.multiple_of(h * HEAD, HEAD), HEAD), :] = dot_nn(v, prob).astype(BF16)
        log_total[0, pl.ds(h, 1), :] = highest + jnp.log(total)
        return carry

    lax.fori_loop(0, HEADS, head, 0, unroll=HEAD_UNROLL)


def mixer_both(
    info,
    frames,
    cotangent,
    context,
    mixer_norm,
    final_norm,
    merge_logits,
    own,
    other,
    forward,
    inverse,
    inverse_three,
    tap_forward,
    tap_inverse,
    *rest,
):
    pieces, rest = rest[:8], rest[8:]
    (
        layer,
        grad_frames,
        grad_context,
        keep,
        send,
        small,
        weights,
        params_s,
        small_wide,
        small_narrow,
        tap_spec,
        second_s,
        second_slope,
        first_s,
        first_slope,
        conv_s,
        spec_s,
        cross_s,
        back_s,
        gated_s,
        hidden_s,
        low_s,
        grad_s,
        attend_s,
        context_s,
        grads_s,
        sems,
    ) = rest
    step = pl.program_id(0)
    branch, core = info[INFO_BRANCH], info[INFO_CORE]
    here = pl.ds(pl.multiple_of(step * SLOT, SLOT), SLOT)
    copies = piece_copies(info, pieces, weights, sems, "z")

    @pl.when(step == 0)
    def _():
        for copy in copies:
            copy.start()
        params_s[branch] = own[...]
        params_s[1 - branch] = other[...]
        for b in range(2):
            tap_spec[:, b * 768 : (b + 1) * 768] = dot_nn(
                tap_forward[...], stack_terms(params_s[b, 0:32, :])
            )
        cross_s[...] = jnp.zeros_like(cross_s)
        small_wide[...] = jnp.zeros_like(small_wide)
        small_narrow[...] = jnp.zeros_like(small_narrow)

    mix_attend, mix_mixer = merge_mix(merge_logits)
    rows_in = frames[0, 0]
    normed, rstd = standardize(rows_in)
    low = (normed * mixer_norm[0:1] + mixer_norm[1:2]).astype(BF16)
    low_s[here, :] = low

    @pl.when(step == 0)
    def _():
        for copy in copies:
            copy.wait()

    length = info[INFO_LENGTH + step]
    valid = (lax.broadcasted_iota(jnp.int32, (SLOT, 1), 0) < length).astype(F32)

    places = [
        (k // PER_BRANCH, slice((k % PER_BRANCH) * BLOCK, (k % PER_BRANCH + 1) * BLOCK),
         slice(k * BLOCK, (k + 1) * BLOCK))
        for k in range(BLOCKS)
    ]

    def part(b, kind, off):
        return weight(weights, b, kind * 768 + off.start, kind * 768 + off.stop)

    def fold(v):
        total = v[:, 0:128]
        for at in range(128, BLOCK, 128):
            total = total + v[:, at : at + 128]
        return total

    def lane_sum(v):
        return jnp.sum(v, axis=-1, keepdims=True)

    total = jnp.zeros((SLOT, 128), F32)
    for b, off, wide in places:
        active, slope = gelu_pair(dot_nn(low, part(b, 1, off)))
        second_s[:, wide] = active
        second_slope[:, wide] = slope
        total += fold(active)
    average = lane_sum(total) / HALF
    total = jnp.zeros((SLOT, 128), F32)
    for b, off, wide in places:
        centered = second_s[:, wide] - average
        total += fold(centered * centered)
    gate_rstd = lax.rsqrt(lane_sum(total) / HALF + EPSILON)

    for b, off, wide in places:
        standard = (second_s[:, wide] - average) * gate_rstd
        gate_in = (standard * params_s[b, 32:33, off] + params_s[b, 33:34, off]) * valid
        spec = dot_nn(forward[...], stack_terms(gate_in))
        spec_s[:, wide] = spec
        real, imag = spec[0:BINS], spec[BINS:SPEC]
        tap_real, tap_imag = tap_spec[0:BINS, wide], tap_spec[BINS:SPEC, wide]
        product = jnp.concatenate(
            [real * tap_real + imag * tap_imag, imag * tap_real - real * tap_imag], axis=0
        )
        conved = dot_nn(inverse_three[...], stack_terms(product)) + params_s[b, 31:32, off]
        conv_s[:, wide] = conved
        active, slope = gelu_pair(dot_nn(low, part(b, 0, off)))
        first_s[:, wide] = active
        first_slope[:, wide] = slope
        gated_s[here, wide] = (active * conved).astype(BF16)

    mixer_part = dot_nt(gated_s[here, 0:768], weight(weights, 0, 1536, 2304)) + dot_nt(
        gated_s[here, 768:1536], weight(weights, 1, 1536, 2304)
    )
    context_s[:, here] = context[0]
    attend_part = dot_tt(context[0, 0:256, :], weight(weights, 0, 2304, 2560)) + dot_tt(
        context[0, 256:512, :], weight(weights, 1, 2304, 2560)
    )
    merged = rows_in + mix_attend * attend_part + mix_mixer * mixer_part
    merged_normed, merged_rstd = standardize(merged)
    layer[0] = ((merged_normed * final_norm[0:1] + final_norm[1:2]) * valid).astype(BF16)
    grad_out = cotangent[0, 0] * valid
    scaled = grad_out * final_norm[0:1]
    grad_merged = merged_rstd * (
        scaled
        - jnp.mean(scaled, axis=-1, keepdims=True)
        - merged_normed * jnp.mean(scaled * merged_normed, axis=-1, keepdims=True)
    )
    small_narrow[0:1] += jnp.sum(grad_out * merged_normed, axis=0, keepdims=True)
    small_narrow[1:2] += jnp.sum(grad_out, axis=0, keepdims=True)
    small_narrow[2:3] += jnp.sum(grad_merged * attend_part, axis=0, keepdims=True)
    small_narrow[3:4] += jnp.sum(grad_merged * mixer_part, axis=0, keepdims=True)
    grad_mixer = (mix_mixer * grad_merged).astype(BF16)
    grad_s[here, :] = grad_mixer
    grad_attend = (mix_attend * grad_merged).astype(BF16)
    attend_s[here, :] = grad_attend
    for b in range(2):
        grad_context[0, b * 256 : (b + 1) * 256, :] = dot_tt(
            weight(weights, b, 2304, 2560), grad_attend
        ).astype(BF16)

    total, cross_total = jnp.zeros((SLOT, 128), F32), jnp.zeros((SLOT, 128), F32)
    for b, off, wide in places:
        grad_gated = dot_nn(grad_mixer, part(b, 2, off))
        grad_conved = grad_gated * first_s[:, wide]
        hidden_s[here, wide] = (first_slope[:, wide] * (grad_gated * conv_s[:, wide])).astype(BF16)
        small_wide[31:32, wide] += jnp.sum(grad_conved, axis=0, keepdims=True)
        grad_spec = dot_nn(forward[:, 0:SLOT], grad_conved.astype(BF16))
        grad_real, grad_imag = grad_spec[0:BINS], grad_spec[BINS:SPEC]
        real, imag = spec_s[0:BINS, wide], spec_s[BINS:SPEC, wide]
        cross_s[0:BINS, wide] += grad_real * real + grad_imag * imag
        cross_s[BINS:SPEC, wide] += grad_real * imag - grad_imag * real
        tap_real, tap_imag = tap_spec[0:BINS, wide], tap_spec[BINS:SPEC, wide]
        product = jnp.concatenate(
            [
                grad_real * tap_real - grad_imag * tap_imag,
                grad_real * tap_imag + grad_imag * tap_real,
            ],
            axis=0,
        )
        grad_gate = dot_nn(inverse[...], product.astype(BF16)) * valid
        standard = (second_s[:, wide] - average) * gate_rstd
        small_wide[32:33, wide] += jnp.sum(grad_gate * standard, axis=0, keepdims=True)
        small_wide[33:34, wide] += jnp.sum(grad_gate, axis=0, keepdims=True)
        grad_standard = grad_gate * params_s[b, 32:33, off]
        back_s[:, wide] = grad_standard
        total += fold(grad_standard)
        cross_total += fold(grad_standard * standard)
    back_average = lane_sum(total) / HALF
    back_scale = lane_sum(cross_total) / HALF

    for b, off, wide in places:
        standard = (second_s[:, wide] - average) * gate_rstd
        grad_second = gate_rstd * (back_s[:, wide] - back_average - standard * back_scale)
        hidden_s[here, HALF + wide.start : HALF + wide.stop] = (
            second_slope[:, wide] * grad_second
        ).astype(BF16)
    grad_low = (
        dot_nt(hidden_s[here, 0:768], weight(weights, 0, 0, 768))
        + dot_nt(hidden_s[here, 768:1536], weight(weights, 1, 0, 768))
    ) + (
        dot_nt(hidden_s[here, 1536:2304], weight(weights, 0, 768, 1536))
        + dot_nt(hidden_s[here, 2304:3072], weight(weights, 1, 768, 1536))
    )
    small_narrow[4:5] += jnp.sum(grad_low * normed, axis=0, keepdims=True)
    small_narrow[5:6] += jnp.sum(grad_low, axis=0, keepdims=True)
    scaled = grad_low * mixer_norm[0:1]
    grad_frames[0] = grad_merged + rstd * (
        scaled
        - jnp.mean(scaled, axis=-1, keepdims=True)
        - normed * jnp.mean(scaled * normed, axis=-1, keepdims=True)
    )

    @pl.when(step == UTTS - 1)
    def _():
        outs = []
        for b in range(2):
            first, second = b * 768, HALF + b * 768
            into_first = dot_tn(low_s[...], hidden_s[:, first : first + 768])
            into_second = dot_tn(low_s[...], hidden_s[:, second : second + 768])
            out = dot_tn(grad_s[...], gated_s[:, first : first + 768])
            attend = dot_tt(attend_s[...], context_s[b * 256 : (b + 1) * 256, :])
            pairs = [
                (into_first[:, 0:256], into_second[:, 512:768]),
                (into_first[:, 256:768], out[:, 0:512]),
                (into_second[:, 0:256], out[:, 512:768]),
                (into_second[:, 256:512], attend),
            ]
            column = 0
            for upper, lower in pairs:
                width = upper.shape[1]
                upper, lower = upper.reshape(32, 2, 8, width), lower.reshape(32, 2, 8, width)
                for p in range(2):
                    grads_s[p, b * 32 : (b + 1) * 32, :, column : column + width] = (
                        jnp.concatenate([upper[:, p], lower[:, p]], axis=1).astype(BF16)
                    )
                column += width
            chips = pl.ds(b * 32, 32)
            outs += start_all(
                [
                    pltpu.make_async_copy(
                        grads_s.at[core, chips], keep.at[chips], sems.at[2 * b]
                    ),
                    pltpu.make_async_copy(
                        grads_s.at[1 - core, chips], send.at[chips], sems.at[2 * b + 1]
                    ),
                ]
            )
        tap_grad = dot_nn(tap_inverse[...], cross_s[...].astype(BF16))
        small_wide[0:31, :] = tap_grad[0:31]
        for g in range(12):
            small[g * 40 : (g + 1) * 40, :] = small_wide[:, g * 128 : (g + 1) * 128]
        for j in range(4):
            small[480 + 8 * j : 488 + 8 * j, :] = small_narrow[:, j * 128 : (j + 1) * 128]
        for copy in outs:
            copy.wait()


def attend_backward(
    info,
    frames,
    grad_mixed,
    triple,
    log_total,
    grad_context,
    norm,
    slopes,
    weights,
    frames_grad,
    keep,
    send,
    distance,
    low_s,
    triple_t,
    small,
    terms,
    sems,
):
    step = pl.program_id(0)
    here = pl.ds(pl.multiple_of(step * SLOT, SLOT), SLOT)

    @pl.when(step == 0)
    def _():
        fill_distance(distance)
        small[...] = jnp.zeros_like(small)

    normed, rstd = standardize(frames[0, 0])
    low_s[here, :] = (normed * norm[0:1] + norm[1:2]).astype(BF16)
    is_key = lax.broadcasted_iota(jnp.int32, (SLOT, SLOT), 0) < info[INFO_LENGTH + step]

    def head(h, carry):
        base = pl.multiple_of((h // 4) * 768 + (h % 4) * HEAD, HEAD)
        q = triple[0, pl.ds(base, HEAD), :]
        k = triple[0, pl.ds(base + 256, HEAD), :]
        v = triple[0, pl.ds(base + 512, HEAD), :]
        grad_here = grad_context[0, pl.ds(pl.multiple_of(h * HEAD, HEAD), HEAD), :]
        logits = dot_tn(k, q) - slopes[pl.ds(h, 1), 0:1] * distance[...]
        logits = jnp.where(is_key, logits, NEGATIVE)
        prob = jnp.exp(logits - log_total[0, pl.ds(h, 1), :])
        grad_prob = dot_tn(v, grad_here)
        row_dot = jnp.sum(prob * grad_prob, axis=0, keepdims=True)
        grad_logits = prob * (grad_prob - row_dot)
        slope_row = -jnp.sum(grad_logits * distance[...], axis=0, keepdims=True)
        small[pl.ds(8 + h, 1), :] += slope_row[:, 0:128] + slope_row[:, 128:256]
        grad_scores = grad_logits.astype(BF16)
        grad_q = dot_nn(k, grad_scores) * (HEAD**-0.5)
        grad_k = dot_nt(q, grad_scores)
        grad_v = dot_nt(grad_here, prob.astype(BF16))
        triple_t[pl.ds(base, HEAD), here] = grad_q.astype(BF16)
        triple_t[pl.ds(base + 256, HEAD), here] = grad_k.astype(BF16)
        triple_t[pl.ds(base + 512, HEAD), here] = grad_v.astype(BF16)
        return carry

    lax.fori_loop(0, HEADS, head, 0, unroll=HEAD_UNROLL)
    grad_low = dot_tt(triple_t[0:768, here], weight(weights, 0, 0, 768)) + dot_tt(
        triple_t[768:1536, here], weight(weights, 1, 0, 768)
    )
    gain_row = jnp.sum(grad_low * normed, axis=0, keepdims=True)
    bias_row = jnp.sum(grad_low, axis=0, keepdims=True)
    for j in range(4):
        small[j : j + 1, :] += gain_row[:, j * 128 : (j + 1) * 128]
        small[4 + j : 5 + j, :] += bias_row[:, j * 128 : (j + 1) * 128]
    scaled = grad_low * norm[0:1]
    frames_grad[0] = (
        grad_mixed[0]
        + rstd
        * (
            scaled
            - jnp.mean(scaled, axis=-1, keepdims=True)
            - normed * jnp.mean(scaled * normed, axis=-1, keepdims=True)
        )
    ).astype(BF16)

    @pl.when(step == UTTS - 1)
    def _():
        high, low = split_low(jnp.sum(small[8:16, :], axis=1, keepdims=True))
        block = jnp.concatenate([small[0:8, :], slope_rows(high, low)], axis=0).astype(BF16)
        for b in range(2):
            grads = dot_tt(low_s[...], triple_t[b * 768 : (b + 1) * 768, :]).reshape(32, 2, 8, 768)
            for p in range(2):
                terms[p, b * 32 : (b + 1) * 32, :, 0:384] = jnp.concatenate(
                    [grads[:, p, :, 0:384], grads[:, p, :, 384:768]], axis=1
                ).astype(BF16)
                for m in range(32):
                    terms[p, b * 32 + m, :, 384:512] = block
        core = info[INFO_CORE]
        outs = start_all(
            [
                pltpu.make_async_copy(terms.at[core], keep, sems.at[0]),
                pltpu.make_async_copy(terms.at[1 - core], send, sems.at[1]),
            ]
        )
        for copy in outs:
            copy.wait()


def stack_terms(value):
    high, low = split_low(value)
    return jnp.concatenate([high, low, high], axis=0).astype(BF16)


def slope_rows(high, low):
    lane = lax.broadcasted_iota(jnp.int32, (8, 128), 1)
    return jnp.where(lane == 0, high, jnp.where(lane == 1, low, 0.0))


def split_low(value):
    high = value.astype(BF16).astype(F32)
    return high, value - high


def start_all(copies):
    for copy in copies:
        copy.start()
    return copies


def chunk_copies(source, target, count, sems):
    size = target.shape[0] // count
    return start_all(
        [
            pltpu.make_async_copy(
                source.at[pl.ds(i * size, size)], target.at[pl.ds(i * size, size)], sems.at[i]
            )
            for i in range(count)
        ]
    )


CHUNKS = 8


def sum_pairs(info, keep, other, pieces, keep_s, other_s, out_s, sems):
    loads = []
    for i, s in enumerate(SHIFTS):
        x = lax.rem(info[INFO_X] + s, 4)
        for b in range(2):
            chips = pl.ds(b * 32 + x * 8, 8)
            here = pl.ds(b * 8, 8)
            loads.append(
                start_all(
                    [
                        pltpu.make_async_copy(
                            source.at[chips], target.at[i, here], sems.at[p, 2 * i + b]
                        )
                        for p, (source, target) in enumerate(((keep, keep_s), (other, other_s)))
                    ]
                )
            )
    stores = []
    columns = keep.shape[2]
    for i in (1, 2, 3, 0):
        for b in range(2):
            for copy in loads[2 * i + b]:
                copy.wait()
            here = slice(b * 8, b * 8 + 8)
            out_s[i, here, :, 0:columns] = (
                keep_s[i, here].astype(F32) + other_s[i, here].astype(F32)
            ).astype(BF16)
        yield i
        stores.append(pltpu.make_async_copy(out_s.at[i], pieces[i], sems.at[2, i]))
        stores[-1].start()
    for copy in stores:
        copy.wait()


def spread_small(small, small_other, out):
    high, low = split_low(small[...] + small_other[...])
    for j in range(16):
        for x in range(4):
            chip = (j // 8 * 4 + x) * 8 + j % 8
            rows = slice(8 * chip, 8 * chip + 8)
            out[j, 16 * x : 16 * x + 16, :] = jnp.concatenate(
                [high[rows], low[rows]], axis=0
            ).astype(BF16)


def sum_mixer(info, keep, other, small, small_other, *rest):
    pieces, (small_out, keep_s, other_s, out_s, sems) = rest[:4], rest[4:]
    sums = sum_pairs(info, keep, other, pieces, keep_s, other_s, out_s, sems)
    next(sums)
    spread_small(small, small_other, small_out)
    for _ in sums:
        pass


def sum_attend(info, keep, other, small_terms, *rest):
    pieces, (keep_s, other_s, out_s, sems) = rest[:4], rest[4:]
    total = (small_terms[0].astype(F32) + small_terms[1].astype(F32)) + (
        small_terms[2].astype(F32) + small_terms[3].astype(F32)
    )
    for i in range(4, 16):
        total += small_terms[i].astype(F32)
    chunks = []
    for x in range(4):
        high, low = split_low(total[16 * x : 16 * x + 8] + total[16 * x + 8 : 16 * x + 16])
        chunks.append(jnp.concatenate([high, low], axis=0))
    chunks = jnp.concatenate(chunks, axis=1).astype(BF16)
    for i in sum_pairs(info, keep, other, pieces, keep_s, other_s, out_s, sems):
        total = keep_s[i, 0, :, 384:512].astype(F32) + other_s[i, 0, :, 384:512].astype(F32)
        high, low = split_low(total[8:16, 0:1] + total[8:16, 1:2])
        block = jnp.concatenate([total[0:8], slope_rows(high, low)], axis=0).astype(BF16)
        for j in range(16):
            out_s[i, j, :, 384:512] = block
        out_s[i, 16] = chunks


def sum_four(info, *rest):
    terms, (out, terms_s, sems) = rest[:4], rest[4:]
    loads = [
        start_all(
            [
                pltpu.make_async_copy(
                    terms[i].at[pl.ds(c * 4, 4)], terms_s.at[i, pl.ds(c * 4, 4)], sems.at[i, c]
                )
                for i in range(4)
            ]
        )
        for c in range(4)
    ]
    for c in range(4):
        for copy in loads[c]:
            copy.wait()
        here = slice(c * 4, c * 4 + 4)
        total = (terms_s[0, here].astype(F32) + terms_s[1, here].astype(F32)) + (
            terms_s[2, here].astype(F32) + terms_s[3, here].astype(F32)
        )
        out[here] = total.astype(BF16)


def join_terms(info, mixer, *rest):
    terms, out = rest[0:4], rest[4]
    for j in range(16):
        out[j, :, 0:1280] = mixer[j]
        total = (terms[0][j].astype(F32) + terms[1][j].astype(F32)) + (
            terms[2][j].astype(F32) + terms[3][j].astype(F32)
        )
        out[j, :, 1280:1664] = total[:, 0:384].astype(BF16)
        if j == 0:
            little = total[:, 384:512]
            high, low = split_low(little[8:16, 0:1] + little[8:16, 1:2])
            block = jnp.concatenate([little[0:8], slope_rows(high, low)], axis=0).astype(BF16)
        out[j, :, 1664:1792] = block
    total = (terms[0][16].astype(F32) + terms[1][16].astype(F32)) + (
        terms[2][16].astype(F32) + terms[3][16].astype(F32)
    )
    high, low = split_low(total[0:8] + total[8:16])
    chunks = jnp.concatenate([high, low], axis=0).astype(BF16)
    for j in range(16):
        out[j, :, 1792:2304] = chunks


def finish(
    info,
    merge_logits,
    terms,
    att_in,
    att_out,
    mix_in,
    mix_out,
    anorm,
    mnorm,
    fnorm,
    gnorm,
    taps,
    bias,
    slope,
    merge,
    terms_s,
    small,
    sems,
):
    branch = info[INFO_BRANCH]
    copies = chunk_copies(terms, terms_s, CHUNKS, sems)
    total = jnp.zeros((16, 1792), F32)
    for c in range(CHUNKS):
        copies[c].wait()
        for i in range(c * 2, c * 2 + 2):
            total += terms_s[i, :, 0:1792].astype(F32)
            for x in range(4):
                pair = terms_s[i, :, 1792 + x * 128 : 1920 + x * 128].astype(F32)
                chip = (i // 8 * 4 + x) * 8 + i % 8
                small[8 * chip : 8 * chip + 8, :] = pair[0:8] + pair[8:16]
    upper, lower = total[0:8], total[8:16]
    mix_in[:, 0, :] = upper[:, 0:768]
    mix_in[:, 1, :] = jnp.concatenate([upper[:, 768:1280], lower[:, 0:256]], axis=1)
    mix_out[...] = lower[:, 256:1024]
    att_out[...] = lower[:, 1024:1280]
    total = total[:, 1280:1792]
    for g in range(6):
        group = small[pl.ds(pl.multiple_of((branch * 6 + g) * 40, 8), 40), :]
        columns = slice(g * 128, (g + 1) * 128)
        taps[:, columns] = group[0:31]
        bias[columns] = group[31]
        gnorm[:, columns] = group[32:34]
    attend_sum, mixer_sum = 0.0, 0.0
    for j in range(4):
        columns = slice(j * 128, (j + 1) * 128)
        group = small[480 + 8 * j : 488 + 8 * j, :]
        fnorm[:, columns] = group[0:2]
        mnorm[:, columns] = group[4:6]
        attend_sum += jnp.sum(group[2:3], axis=1, keepdims=True)
        mixer_sum += jnp.sum(group[3:4], axis=1, keepdims=True)
    mix_attend, mix_mixer = merge_mix(merge_logits)
    average = mix_attend * attend_sum + mix_mixer * mixer_sum
    merge[0] = jnp.sum(mix_attend * (attend_sum - average))
    merge[1] = jnp.sum(mix_mixer * (mixer_sum - average))
    att_in[0] = total[0:8, 0:256]
    att_in[1] = jnp.concatenate([total[0:8, 256:384], total[8:16, 0:128]], axis=1)
    att_in[2] = total[8:16, 128:384]
    for p in range(2):
        for j in range(4):
            r = p * 4 + j
            anorm[p : p + 1, j * 128 : (j + 1) * 128] = total[r : r + 1, 384:512]
    slopes = total[8:16, 384:385] + total[8:16, 385:386]
    for r in range(4):
        slope[r] = jnp.where(
            branch == 0, jnp.sum(slopes[r : r + 1]), jnp.sum(slopes[4 + r : 5 + r])
        )


def place_pair(info, own, other, out, own_s, other_s, out_s, sems):
    branch = info[INFO_BRANCH]
    loads = [
        start_all(
            [
                pltpu.make_async_copy(source.at[u], target.at[u], sems.at[p, u])
                for u in range(UTTS)
            ]
        )
        for p, (source, target) in enumerate(((own, own_s), (other, other_s)))
    ]
    stores = []
    for u in range(UTTS):
        for p, source in enumerate((own_s, other_s)):
            loads[p][u].wait()
            out_s[p, u] = source[u].astype(F32)
            at = branch if p == 0 else 1 - branch
            stores.append(
                pltpu.make_async_copy(out_s.at[p, u], out.at[u, at], sems.at[2 + p, u])
            )
            stores[-1].start()
    for copy in stores:
        copy.wait()


def whole(shape):
    return pl.BlockSpec(shape, lambda i, *_: (0,) * len(shape), pipeline_mode=pl.Buffered(1))


def per_utt(shape):
    return pl.BlockSpec((1,) + shape, lambda i, *_: (i,) + (0,) * len(shape))


ANY = pl.BlockSpec(memory_space=pl.ANY)
OWN_FRAMES = pl.BlockSpec((1, 1, SLOT, WIDTH), lambda i, info, *_: (i, info[0], 0, 0))


def scratch(*shape, dtype=F32):
    return pltpu.VMEM(shape, dtype)


def struct(*shape, dtype=F32):
    return jax.ShapeDtypeStruct(shape, dtype)


def call(kernel, name, info, operands, in_specs, outs, out_specs, scratches=(), grid=1, us=2, **extra):
    return pl.pallas_call(
        kernel,
        grid_spec=pltpu.PrefetchScalarGridSpec(
            num_scalar_prefetch=1,
            grid=(grid,),
            in_specs=in_specs,
            out_specs=out_specs,
            scratch_shapes=scratches,
        ),
        out_shape=outs,
        compiler_params=pltpu.CompilerParams(
            dimension_semantics=("arbitrary",), vmem_limit_bytes=VMEM_LIMIT
        ),
        cost_estimate=pl.CostEstimate(
            flops=us * 100000000, bytes_accessed=1 << 16, transcendentals=0
        ),
        name=name,
        **extra,
    )(info, *operands)


def run_pack(slopes, *operands):
    return call(
        pack_local,
        "pack_local",
        np.zeros((8,), np.int32),
        (slopes, *operands),
        [pl.BlockSpec(memory_space=pltpu.SMEM)] + [whole(a.shape) for a in operands],
        [struct(8, 3328, dtype=BF16), struct(35, 768)],
        [whole((8, 3328)), whole((35, 768))],
    )


def run_pair(info, local, other):
    return call(
        pair_rows,
        "pair_rows",
        info,
        (local, other),
        [whole((8, 3328))] * 2,
        struct(16, 1664, dtype=BF16),
        whole((16, 1664)),
    )


def run_join_y(info, pieces):
    shapes = [(4, 16, 384), (4, 16, 1280)]
    return call(
        join_y,
        "join_y",
        info,
        pieces,
        [whole((16, 1664))] * 4,
        [struct(*s, dtype=BF16) for s in shapes],
        [whole(s) for s in shapes],
    )


def run_join_planes(info, over_z, over_x):
    shapes = [(2, 8, 16, 384), (2, 8, 16, 1280)]
    return call(
        join_planes,
        "join_planes",
        info,
        (*over_z, *over_x),
        [whole((4, 16, 384))] * 4 + [whole((4, 16, 1280))] * 4,
        [struct(*s, dtype=BF16) for s in shapes],
        [whole(s) for s in shapes],
    )


def run_attend_forward(info, frames, norm, own, other, pieces):
    return call(
        attend_forward,
        "attend_forward",
        info,
        (frames, norm, own, other, *pieces),
        [OWN_FRAMES, whole((2, WIDTH)), whole((35, 768)), whole((35, 768))] + [ANY] * 8,
        [
            struct(UTTS, HALF, SLOT, dtype=BF16),
            struct(UTTS, WIDTH, SLOT, dtype=BF16),
            struct(UTTS, HEADS, SLOT),
            struct(2, 4, 4, 32, 768, dtype=BF16),
            struct(HEADS, 128),
        ],
        [
            per_utt((HALF, SLOT)),
            per_utt((WIDTH, SLOT)),
            per_utt((HEADS, SLOT)),
            whole((2, 4, 4, 32, 768)),
            whole((HEADS, 128)),
        ],
        [scratch(HEADS, SLOT, SLOT), pltpu.SemaphoreType.DMA((16,))],
        grid=UTTS,
    )


def run_mixer(info, frames, cotangent, context, mnorm, fnorm, merge_logits, own, other, pieces):
    forward, inverse, inverse_three, tap_forward, tap_inverse = transform_tables()
    tables = (
        jnp.asarray(forward, BF16),
        jnp.asarray(inverse, BF16),
        jnp.asarray(inverse_three, BF16),
        jnp.asarray(tap_forward, BF16),
        jnp.asarray(tap_inverse, BF16),
    )
    return call(
        mixer_both,
        "mixer_both",
        info,
        (frames, cotangent, context, mnorm, fnorm, merge_logits, own, other, *tables, *pieces),
        [
            OWN_FRAMES,
            OWN_FRAMES,
            per_utt((WIDTH, SLOT)),
            whole((2, WIDTH)),
            whole((2, WIDTH)),
            whole((1, 2)),
            whole((35, 768)),
            whole((35, 768)),
            whole((SPEC, 3 * SLOT)),
            whole((SLOT, SPEC)),
            whole((SLOT, 3 * SPEC)),
            whole((SPEC, 96)),
            whole((32, SPEC)),
        ]
        + [ANY] * 8,
        [
            struct(UTTS, SLOT, WIDTH, dtype=BF16),
            struct(UTTS, SLOT, WIDTH),
            struct(UTTS, WIDTH, SLOT, dtype=BF16),
            struct(64, 16, 1280, dtype=BF16),
            struct(64, 16, 1280, dtype=BF16),
            struct(512, 128),
        ],
        [
            per_utt((SLOT, WIDTH)),
            per_utt((SLOT, WIDTH)),
            per_utt((WIDTH, SLOT)),
            ANY,
            ANY,
            whole((512, 128)),
        ],
        [
            scratch(2, 4, 4, 32, 2560, dtype=BF16),
            scratch(2, 35, 768),
            scratch(40, HALF),
            scratch(8, WIDTH),
            scratch(SPEC, HALF),
            scratch(SLOT, HALF),
            scratch(SLOT, HALF),
            scratch(SLOT, HALF),
            scratch(SLOT, HALF),
            scratch(SLOT, HALF),
            scratch(SPEC, HALF),
            scratch(SPEC, HALF),
            scratch(SLOT, HALF),
            scratch(ROWS, HALF, dtype=BF16),
            scratch(ROWS, 2 * HALF, dtype=BF16),
            scratch(ROWS, WIDTH, dtype=BF16),
            scratch(ROWS, WIDTH, dtype=BF16),
            scratch(ROWS, WIDTH, dtype=BF16),
            scratch(WIDTH, ROWS, dtype=BF16),
            scratch(2, 64, 16, 1280, dtype=BF16),
            pltpu.SemaphoreType.DMA((16,)),
        ],
        grid=UTTS,
    )


def run_attend_backward(
    info, frames, grad_mixed, triple, log_total, grad_context, norm, slopes, weights
):
    return call(
        attend_backward,
        "attend_backward",
        info,
        (frames, grad_mixed, triple, log_total, grad_context, norm, slopes, weights),
        [
            OWN_FRAMES,
            per_utt((SLOT, WIDTH)),
            per_utt((HALF, SLOT)),
            per_utt((HEADS, SLOT)),
            per_utt((WIDTH, SLOT)),
            whole((2, WIDTH)),
            whole((HEADS, 128)),
            whole((2, 4, 4, 32, 768)),
        ],
        [
            struct(UTTS, SLOT, WIDTH, dtype=BF16),
            struct(64, 16, 512, dtype=BF16),
            struct(64, 16, 512, dtype=BF16),
        ],
        [per_utt((SLOT, WIDTH)), ANY, ANY],
        [
            scratch(SLOT, SLOT),
            scratch(ROWS, WIDTH, dtype=BF16),
            scratch(HALF, ROWS, dtype=BF16),
            scratch(16, 128),
            scratch(2, 64, 16, 512, dtype=BF16),
            pltpu.SemaphoreType.DMA((2,)),
        ],
        grid=UTTS,
    )


def run_sum_mixer(info, keep, other, small, small_other):
    piece = (16, 16, 1280)
    return call(
        sum_mixer,
        "sum_mixer",
        info,
        (keep, other, small, small_other),
        [ANY, ANY, whole((512, 128)), whole((512, 128))],
        [struct(*piece, dtype=BF16)] * 4 + [struct(16, 64, 128, dtype=BF16)],
        [ANY] * 4 + [whole((16, 64, 128))],
        [scratch(4, *piece, dtype=BF16)] * 3 + [pltpu.SemaphoreType.DMA((3, 8))],
    )


def run_sum_attend(info, keep, other, small_terms):
    piece, wider = (16, 16, 512), (17, 16, 512)
    return call(
        sum_attend,
        "sum_attend",
        info,
        (keep, other, small_terms),
        [ANY, ANY, whole((16, 64, 128))],
        [struct(*wider, dtype=BF16)] * 4,
        [ANY] * 4,
        [scratch(4, *piece, dtype=BF16)] * 2
        + [scratch(4, *wider, dtype=BF16), pltpu.SemaphoreType.DMA((3, 8))],
    )


def run_sum_four(info, terms):
    piece = terms[0].shape
    return call(
        sum_four,
        "sum_four",
        info,
        terms,
        [ANY] * 4,
        struct(*piece, dtype=BF16),
        whole(piece),
        [scratch(4, *piece, dtype=BF16), pltpu.SemaphoreType.DMA((4, 4))],
    )


def run_join(info, mixer, terms):
    return call(
        join_terms,
        "join_terms",
        info,
        (mixer, *terms),
        [whole(mixer.shape)] + [whole(terms[0].shape)] * 4,
        struct(16, 16, 2304, dtype=BF16),
        whole((16, 16, 2304)),
    )


def run_finish(info, *operands):
    shapes = [
        (3, 8, 256),
        (8, 256),
        (8, 2, 768),
        (8, 768),
        (2, WIDTH),
        (2, WIDTH),
        (2, WIDTH),
        (2, 768),
        (31, 768),
        (768,),
    ]
    scalars = pl.BlockSpec(memory_space=pltpu.SMEM)
    return call(
        finish,
        "finish",
        info,
        operands,
        [whole(a.shape) for a in operands[:-1]] + [ANY],
        [struct(*s) for s in shapes] + [struct(4), struct(2)],
        [whole(s) for s in shapes] + [scalars, scalars],
        [
            scratch(*operands[-1].shape, dtype=BF16),
            scratch(512, 128),
            pltpu.SemaphoreType.DMA((CHUNKS,)),
        ],
    )


def run_place_pair(info, own, other):
    return call(
        place_pair,
        "place_pair",
        info,
        (own, other),
        [ANY, ANY],
        struct(UTTS, 2, SLOT, WIDTH),
        ANY,
        [
            scratch(UTTS, SLOT, WIDTH, dtype=BF16),
            scratch(UTTS, SLOT, WIDTH, dtype=BF16),
            scratch(2, UTTS, SLOT, WIDTH),
            pltpu.SemaphoreType.DMA((4, UTTS)),
        ],
    )


def swap(value, axis):
    return lax.ppermute(value, axis, [(0, 1), (1, 0)])


def move_x(block, distance):
    return lax.ppermute(block, "x", [(i, (i + distance) % 4) for i in range(4)])


def move_y(block, distance):
    def joint(y):
        return (y % 2) * 2 + y // 2

    return lax.ppermute(
        block, ("branch", "yh"), [(joint(y), joint((y + distance) % 4)) for y in range(4)]
    )


def move(block, axis, distance):
    return lax.ppermute(block, axis, [(i, (i + distance) % 4) for i in range(4)])


def along(block, axis):
    return [block] + [move(block, axis, s) for s in SHIFTS[1:]]


def with_partner(pieces):
    both = []
    for piece in pieces:
        both += [piece, swap(piece, "core")]
    return both


def exchange_x(pieces):
    return [pieces[0]] + [move(p, "x", s) for p, s in zip(pieces[1:], SHIFTS[1:])]


CHIPS = ("branch", "x", "z", "yh")
PLANE = ("branch", "z", "yh")


def exchange(blocks, axes):
    return lax.all_to_all(blocks, axes, 0, 0, tiled=True)


def shards(
    frames,
    attend_norm,
    attend_in,
    attend_out,
    position_slope,
    mixer_norm,
    mixer_in,
    gating_norm,
    kernel_taps,
    kernel_bias,
    mixer_out,
    merge_logits,
    final_norm,
    lengths,
    cotangent,
):
    branch = lax.axis_index("branch")
    core = lax.axis_index("core")
    own_lengths = lax.dynamic_slice_in_dim(lengths, branch, 1, 1)[:, 0]
    x, yh, z = (lax.axis_index(axis) for axis in ("x", "yh", "z"))
    info = jnp.concatenate([jnp.stack([branch, core, x, 2 * yh + branch, z]), own_lengths])
    merge_logits = merge_logits[None]
    local, own = run_pack(
        position_slope,
        attend_in.transpose(1, 0, 2),
        attend_out,
        mixer_in,
        mixer_out,
        kernel_taps,
        kernel_bias,
        gating_norm,
    )
    other = swap(own, "branch")
    block = run_pair(info, local, swap(local, "core"))
    first, second = run_join_y(info, [block] + [move_y(block, s) for s in SHIFTS[1:]])
    first, second, other = lax.optimization_barrier((first, second, other))
    attend_block, mixer_block = run_join_planes(info, along(first, "z"), along(second, "x"))
    attend_pieces = along(attend_block.reshape(2, 4, 32, 384), "x")
    mixer_pieces = along(mixer_block.reshape(2, 4, 32, 1280), "z")

    triple, context, log_total, attend_w, slopes = run_attend_forward(
        info, frames, attend_norm, own, other, with_partner(attend_pieces)
    )
    *mixer_pieces, context = lax.optimization_barrier((*mixer_pieces, context))
    layer, grad_mixed, grad_context, mixer_keep, mixer_send, small = run_mixer(
        info,
        frames,
        cotangent,
        context,
        mixer_norm,
        final_norm,
        merge_logits,
        own,
        other,
        with_partner(mixer_pieces),
    )
    small_other = swap(small, "core")
    mixer_other = swap(mixer_send, "core")
    layer_other = swap(layer, "branch")
    *mixer_sent, small_sent = run_sum_mixer(info, mixer_keep, mixer_other, small, small_other)
    mixer_terms = exchange_x(mixer_sent)
    small_sent, _, grad_context = lax.optimization_barrier(
        (small_sent, mixer_sent[0], grad_context)
    )
    grads, attend_keep, attend_send = run_attend_backward(
        info,
        frames,
        grad_mixed,
        triple,
        log_total,
        grad_context,
        attend_norm,
        slopes,
        attend_w,
    )
    small_sent, grads = lax.optimization_barrier((small_sent, grads))
    small_terms = exchange(small_sent, PLANE)
    grads, attend_keep, attend_send, layer_other, small_terms, *mixer_terms = (
        lax.optimization_barrier(
            (grads, attend_keep, attend_send, layer_other, small_terms, *mixer_terms)
        )
    )
    grads_other = swap(grads, "branch")
    attend_terms = exchange_x(
        run_sum_attend(info, attend_keep, swap(attend_send, "core"), small_terms)
    )
    mixer_total = run_sum_four(info, mixer_terms)
    layer_out = run_place_pair(info, layer, layer_other)
    *attend_terms, mixer_total, grads_other, layer_out = lax.optimization_barrier(
        (*attend_terms, mixer_total, grads_other, layer_out)
    )
    terms = exchange(run_join(info, mixer_total, attend_terms), PLANE)
    frames_out = run_place_pair(info, grads, grads_other)
    (
        att_in,
        att_out,
        mix_in,
        mix_out,
        anorm,
        mnorm,
        fnorm,
        gnorm,
        taps,
        bias,
        slope,
        merge,
    ) = run_finish(
        info,
        merge_logits,
        terms,
    )
    return (
        layer_out,
        frames_out,
        anorm,
        att_in.transpose(1, 0, 2),
        att_out,
        slope,
        mnorm,
        mix_in,
        gnorm,
        taps,
        bias,
        mix_out,
        merge,
        fnorm,
    )


def solution(mesh):
    fine = Mesh(mesh.devices.reshape(2, 4, 4, 2, 2), ("branch", "x", "z", "yh", "core"))
    dp = ("x", "z", "yh", "core")
    placed = (
        P(None, dp, None, None),
        P(),
        P(dp, None, "branch"),
        P(dp, "branch"),
        P("branch"),
        P(),
        P(dp, None, "branch"),
        P(None, "branch"),
        P(None, "branch"),
        P("branch"),
        P(dp, "branch"),
        P(),
        P(),
        P(None, dp),
        P(None, dp, None, None),
    )
    return jax.shard_map(
        shards,
        mesh=fine,
        in_specs=placed,
        out_specs=(
            P(None, dp, None, None),
            P(None, dp, None, None),
            P(),
            P(dp, None, "branch"),
            P(dp, "branch"),
            P("branch"),
            P(),
            P(dp, None, "branch"),
            P(None, "branch"),
            P(None, "branch"),
            P("branch"),
            P(dp, "branch"),
            P(),
            P(),
        ),
        check_vma=False,
    )
```
